32 devices in a mesh: rows: 4 (over z), seq: 8 (over y, x, core).
Axes of the slice: x: 2, y: 2, z: 4, core: 2. Of those that a mesh axis runs over, the one named last changes fastest.
Arguments:
- hidden_in: bfloat16 [8, 512, 2048], P('rows', 'seq'), may hold values from -6 to 6
- attn_gain: bfloat16 [2048], P(('rows', 'seq')), may hold values from 0.5 to 1.5
- query_weight: bfloat16 [2048, 2048], P(('rows', 'seq')), may hold values from -0.125 to 0.125
- key_weight: bfloat16 [2048, 2048], P(('rows', 'seq')), may hold values from -0.125 to 0.125
- value_weight: bfloat16 [2048, 2048], P(('rows', 'seq')), may hold values from -0.125 to 0.125
- rate_weight: bfloat16 [2048, 32], P(('rows', 'seq')), may hold values from -0.125 to 0.125
- gate_weight: bfloat16 [2048, 2048], P(('rows', 'seq')), may hold values from -0.125 to 0.125
- init_weight: bfloat16 [2048, 64], P(('rows', 'seq')), may hold values from -0.75 to 0.75
- init_bias: bfloat16 [2048], P(('rows', 'seq')), may hold values from -2 to 2
- inner_gain: bfloat16 [2048], P(('rows', 'seq')), may hold values from 0.5 to 1.5
- inner_shift: bfloat16 [2048], P(('rows', 'seq')), may hold values from -2 to 2
- post_gain: bfloat16 [2048], P(('rows', 'seq')), may hold values from 0.5 to 1.5
- post_shift: bfloat16 [2048], P(('rows', 'seq')), may hold values from -2 to 2
- out_weight: bfloat16 [2048, 2048], P(('rows', 'seq')), may hold values from -0.25 to 0.25
- ffn_gain: bfloat16 [2048], P(('rows', 'seq')), may hold values from 0.5 to 1.5
- ffn_gate_weight: bfloat16 [2048, 5504], P(('rows', 'seq')), may hold values from -0.125 to 0.125
- ffn_up_weight: bfloat16 [2048, 5504], P(('rows', 'seq')), may hold values from -0.125 to 0.125
- ffn_down_weight: bfloat16 [5504, 2048], P(('rows', 'seq')), may hold values from -0.15625 to 0.15625
- doc_starts: int32 [8, 6], P('rows'), may hold values from 0 to 496, as said below
- out_grad: bfloat16 [8, 512, 2048], P('rows', 'seq'), may hold values from -6 to 6
Outputs:
- block_out: bfloat16 [8, 512, 2048], P('rows', 'seq')
- hidden_grad: float32 [8, 512, 2048], P('rows', 'seq')
- attn_gain_grad: float32 [2048], P(('rows', 'seq'))
- query_weight_grad: float32 [2048, 2048], P(('rows', 'seq'))
- key_weight_grad: float32 [2048, 2048], P(('rows', 'seq'))
- value_weight_grad: float32 [2048, 2048], P(('rows', 'seq'))
- rate_weight_grad: float32 [2048, 32], P(('rows', 'seq'))
- gate_weight_grad: float32 [2048, 2048], P(('rows', 'seq'))
- init_weight_grad: float32 [2048, 64], P(('rows', 'seq'))
- init_bias_grad: float32 [2048], P(('rows', 'seq'))
- inner_gain_grad: float32 [2048], P(('rows', 'seq'))
- inner_shift_grad: float32 [2048], P(('rows', 'seq'))
- post_gain_grad: float32 [2048], P(('rows', 'seq'))
- post_shift_grad: float32 [2048], P(('rows', 'seq'))
- out_weight_grad: float32 [2048, 2048], P(('rows', 'seq'))
- ffn_gain_grad: float32 [2048], P(('rows', 'seq'))
- ffn_gate_weight_grad: float32 [2048, 5504], P(('rows', 'seq'))
- ffn_up_weight_grad: float32 [2048, 5504], P(('rows', 'seq'))
- ffn_down_weight_grad: float32 [5504, 2048], P(('rows', 'seq'))
The draws below stay inside these ranges and needn't reach their ends.
Inputs may be any that keep to these rules, and one draw needn't show every extreme that they name: `doc_starts`: every entry is a multiple of 16; entries of a row come in no particular order and may repeat. Position 0 of every row restarts as well. In each aligned block of 2 rows one row, drawn from the seed, has all its entries below 64 or above 448, with 0 and 496 among them.
All inputs are finite; a program needn't handle non-finite values.
Results may differ from the reference program's by a relative error of at most 0.0094.
Values may be sent and summed in bfloat16 or wider, within the bound.
No kernel may reach another device: no remote copies, remote signals or barrier semaphores. Data moves between devices by JAX's collectives and lax.ppermute only.
A program may use at most 448 MiB of HBM per device.

```python
from functools import partial
import jax
import jax.numpy as jnp
from jax import lax

D = 2048
HEADS = 32
HEAD = 64
FF = 5504
MINI = 16
ROWS_DEV = 2
STRETCH = 64
STARTS = 6
ROWS_TOTAL = 8
LENGTH = 512


def draw_doc_starts(key, part):
    key = jax.random.fold_in(key, 11)
    keys_list = jax.random.split(key, 5)
    blocks_count = ROWS_TOTAL // ROWS_DEV
    slots = STRETCH // MINI
    anywhere = jax.random.randint(keys_list[0], (ROWS_TOTAL, STARTS), 0, LENGTH // MINI) * MINI
    early = jax.random.randint(keys_list[1], (ROWS_TOTAL, STARTS), 0, slots) * MINI
    late = LENGTH - MINI * jax.random.randint(keys_list[2], (ROWS_TOTAL, STARTS), 1, slots)
    sides = jax.random.randint(keys_list[3], (ROWS_TOTAL, STARTS), 0, 2)
    spanning = jnp.where(sides == 0, early, late)
    column = jnp.arange(STARTS)[None, :]
    spanning = jnp.where(column == 0, 0, jnp.where(column == 1, LENGTH - MINI, spanning))
    chosen_row = jax.random.randint(keys_list[4], (blocks_count,), 0, ROWS_DEV)
    in_block = jnp.arange(ROWS_TOTAL) % ROWS_DEV
    chosen = jnp.repeat(chosen_row, ROWS_DEV, total_repeat_length=ROWS_TOTAL) == in_block
    return jnp.where(chosen[:, None], spanning, anywhere).astype(jnp.int32)


def shard_levels(key, extent, shards, least, top_value):
    gain = 1.0
    for dim, parts in shards:
        heights = jax.random.uniform(jax.random.fold_in(jax.random.fold_in(key, 6), dim), (parts,), jnp.float32, least / len(shards), top_value / len(shards))
        gain = gain * jnp.repeat(jnp.exp(heights), extent[dim] // parts).reshape((-1,) + (1,) * (len(extent) - 1 - dim))
    return gain


def centred(key, shape, scale, limit, cuts=(), kind=jnp.bfloat16):
    values = jax.random.normal(key, shape, jnp.float32) * scale
    if len(cuts) > 0:
        values = shard_levels(key, shape, cuts, -0.22, 0.18) * values
    return jnp.clip(values, min=-limit, max=limit).astype(kind)


def setup_inputs(seed: int = 0) -> dict:
    streams_of = jax.random.split(jax.random.key(seed), 21)
    hidden_in = centred(streams_of[0], (ROWS_TOTAL, LENGTH, D), 1.0, 6.0, ((0, 4), (1, 8)))
    attn_gain = jnp.clip(1.0 + 0.1 * jax.random.normal(streams_of[1], (D,), jnp.float32), 0.5, 1.5).astype(jnp.bfloat16)
    query_weight = centred(streams_of[2], (D, D), D ** -0.5, 0.125, ((0, 32),))
    key_weight = centred(streams_of[3], (D, D), D ** -0.5, 0.125, ((0, 32),))
    value_weight = centred(streams_of[4], (D, D), D ** -0.5, 0.125, ((0, 32),))
    rate_weight = centred(streams_of[5], (D, HEADS), D ** -0.5, 0.125, ((0, 32),))
    gate_weight = centred(streams_of[6], (D, D), D ** -0.5, 0.125, ((0, 32),))
    init_weight = centred(streams_of[7], (D, HEAD), HEAD ** -0.5, 0.75, ((0, 32),))
    init_bias = centred(streams_of[8], (D,), 0.3, 2.0, ((0, 32),))
    inner_gain = jnp.clip(1.0 + 0.1 * jax.random.normal(streams_of[9], (D,), jnp.float32), 0.5, 1.5).astype(jnp.bfloat16)
    inner_shift = centred(streams_of[10], (D,), 0.3, 2.0, ((0, 32),))
    post_gain = jnp.clip(1.0 + 0.1 * jax.random.normal(streams_of[11], (D,), jnp.float32), 0.5, 1.5).astype(jnp.bfloat16)
    post_shift = centred(streams_of[12], (D,), 0.3, 2.0, ((0, 32),))
    out_weight = centred(streams_of[13], (D, D), (D // 4) ** -0.5, 0.25, ((0, 32),))
    ffn_gain = jnp.clip(1.0 + 0.1 * jax.random.normal(streams_of[14], (D,), jnp.float32), 0.5, 1.5).astype(jnp.bfloat16)
    ffn_gate_weight = centred(streams_of[15], (D, FF), D ** -0.5, 0.125, ((0, 32),))
    ffn_up_weight = centred(streams_of[16], (D, FF), D ** -0.5, 0.125, ((0, 32),))
    ffn_down_weight = centred(streams_of[17], (FF, D), (FF // 4) ** -0.5, 0.15625, ((0, 32),))
    doc_starts = draw_doc_starts(jax.random.fold_in(streams_of[20], 71), 0)
    out_grad = centred(streams_of[19], (ROWS_TOTAL, LENGTH, D), 1.0, 6.0, ((0, 4), (1, 8)))
    return {"hidden_in": hidden_in, "attn_gain": attn_gain, "query_weight": query_weight, "key_weight": key_weight, "value_weight": value_weight, "rate_weight": rate_weight, "gate_weight": gate_weight, "init_weight": init_weight, "init_bias": init_bias, "inner_gain": inner_gain, "inner_shift": inner_shift, "post_gain": post_gain, "post_shift": post_shift, "out_weight": out_weight, "ffn_gain": ffn_gain, "ffn_gate_weight": ffn_gate_weight, "ffn_up_weight": ffn_up_weight, "ffn_down_weight": ffn_down_weight, "doc_starts": doc_starts, "out_grad": out_grad}


EPSILON = 1e-06
BASE_RATE = 1.0
HIGHEST = lax.Precision.HIGHEST

@jax.custom_vjp
def low(v):
    return lax.optimization_barrier(v.astype(jnp.bfloat16)).astype(jnp.float32)

@jax.custom_vjp
def low_back(v):
    return v

def low_keep(v):
    return (low(v), None)

def low_pass(kept, grad):
    return (grad,)

def back_keep(v):
    return (v, None)

def back_low(kept, grad):
    return (low(grad),)
low.defvjp(low_keep, low_pass)
low_back.defvjp(back_keep, back_low)

def standardize(values):
    center = values - lax.optimization_barrier(jnp.mean(values, axis=-1, keepdims=True))
    spread = jnp.sqrt(lax.optimization_barrier(jnp.mean(center * center, axis=-1, keepdims=True)) + EPSILON)
    return (center / spread, spread)

def inner_step(carried, inputs, init_weight, init_offset, inner_gain, inner_shift):
    queries, keys_in, values_in, logits, restart = inputs
    start_state = jnp.concatenate([init_weight, init_offset[:, None, :]], axis=1)
    carried = jnp.where(restart[:, None, None, None], start_state[None], carried)
    weight = carried[:, :, :-1, :]
    offset = carried[:, :, -1, :]
    first_pass = jnp.einsum('rthd,rhde->rthe', keys_in, weight, precision=HIGHEST) + offset[:, None]
    normed, spread = standardize(first_pass)
    residue = (normed * inner_gain + inner_shift - (values_in - keys_in)) * inner_gain
    inner_grad = (residue - lax.optimization_barrier(jnp.mean(residue, axis=-1, keepdims=True)) - normed * lax.optimization_barrier(jnp.mean(residue * normed, axis=-1, keepdims=True))) / spread
    batch_len = queries.shape[1]
    head_dim = queries.shape[-1]
    position = jnp.arange(batch_len)
    causal = (position[:, None] >= position[None, :]).astype(jnp.float32)
    token_scale = 1.0 / (position + 1).astype(jnp.float32)
    rate_values = jax.nn.sigmoid(logits) * (BASE_RATE / head_dim)
    step_sizes = (token_scale[:, None] * causal)[None, None] * jnp.transpose(rate_values, (0, 2, 1))[:, :, None, :]
    affinity = jnp.einsum('rthd,rshd->rhts', queries, keys_in, precision=HIGHEST)
    combined = jnp.einsum('rthd,rhde->rthe', queries, weight, precision=HIGHEST) + offset[:, None] - jnp.einsum('rhts,rshe->rthe', step_sizes * (affinity + 1.0), inner_grad, precision=HIGHEST)
    rebuilt, _ = standardize(combined)
    result = queries + rebuilt * inner_gain + inner_shift
    per_source = jnp.transpose(step_sizes[:, :, -1, :], (0, 2, 1))
    weighted = per_source[..., None] * keys_in
    new_weight = weight - jnp.einsum('rshd,rshe->rhde', weighted, inner_grad, precision=HIGHEST)
    new_offset = offset - lax.optimization_barrier(jnp.sum(per_source[..., None] * inner_grad, axis=1))
    return (jnp.concatenate([new_weight, new_offset[:, :, None, :]], axis=2), result)

def run_blocks(state, queries, keys_in, values_in, logits, restarts, init_weight, init_offset, inner_gain, inner_shift):

    def advance(carried, inputs):
        return jax.checkpoint(inner_step)(carried, inputs, init_weight, init_offset, inner_gain, inner_shift)
    return lax.scan(advance, state, (queries, keys_in, values_in, logits, restarts))

def rms_scale(values, scale_gain):
    return values * lax.rsqrt(lax.optimization_barrier(jnp.mean(values * values, axis=-1, keepdims=True)) + EPSILON) * scale_gain

def forward(restarts, hidden, attn_gain, query_weight, key_weight, value_weight, rate_weight, gate_weight, init_weight, init_bias, inner_gain, inner_shift, post_gain, post_shift, out_weight, ffn_gain, ffn_gate_weight, ffn_up_weight, ffn_down_weight):
    seqs_count, length, model_width = hidden.shape
    head_count = rate_weight.shape[1]
    head_dim = init_weight.shape[1]
    blocks = length // MINI
    tokens = hidden.reshape(-1, model_width)
    normed = low(rms_scale(tokens, attn_gain))

    def project(matrix):
        return jnp.dot(normed, matrix, precision=HIGHEST)
    queries = low_back(project(query_weight))
    keys_out = low_back(project(key_weight))
    values_out = low_back(project(value_weight))
    gate_pre = low_back(project(gate_weight))
    logits = low_back(project(rate_weight))

    def arrange(values):
        return values.reshape(seqs_count, blocks, MINI, head_count, -1).transpose(1, 0, 2, 3, 4)
    state = jnp.zeros((seqs_count, head_count, head_dim + 1, head_dim), jnp.float32)
    _, results = run_blocks(state, arrange(queries), arrange(keys_out), arrange(values_out), arrange(logits)[..., 0], restarts, init_weight.reshape(head_count, head_dim, head_dim), init_bias.reshape(head_count, head_dim), inner_gain.reshape(head_count, head_dim), inner_shift.reshape(head_count, head_dim))
    inner_out = results.transpose(1, 0, 2, 3, 4).reshape(-1, model_width)
    post_norm, _ = standardize(inner_out)
    gated = low(jax.nn.gelu(gate_pre, approximate=True) * (post_norm * post_gain + post_shift))
    residual = tokens + low_back(jnp.dot(gated, out_weight, precision=HIGHEST))
    ffn_in = low(rms_scale(residual, ffn_gain))
    gate_value = low_back(jnp.dot(ffn_in, ffn_gate_weight, precision=HIGHEST))
    up_value = low_back(jnp.dot(ffn_in, ffn_up_weight, precision=HIGHEST))
    active = low(jax.nn.silu(gate_value) * up_value)
    summed = residual + low_back(jnp.dot(active, ffn_down_weight, precision=HIGHEST))
    return summed.reshape(seqs_count, length, model_width)

def reference(hidden_in, attn_gain, query_weight, key_weight, value_weight, rate_weight, gate_weight, init_weight, init_bias, inner_gain, inner_shift, post_gain, post_shift, out_weight, ffn_gain, ffn_gate_weight, ffn_up_weight, ffn_down_weight, doc_starts, out_grad):
    length = hidden_in.shape[1]
    position = jnp.arange(length // MINI, dtype=jnp.int32) * MINI
    restarts = jnp.logical_or(position[None, :] == 0, jnp.any(doc_starts[:, :, None] == position[None, None, :], axis=1)).T
    floats = [hidden_in, attn_gain, query_weight, key_weight, value_weight, rate_weight, gate_weight, init_weight, init_bias, inner_gain, inner_shift, post_gain, post_shift, out_weight, ffn_gain, ffn_gate_weight, ffn_up_weight, ffn_down_weight]
    floats = [entry.astype(jnp.float32) for entry in floats]
    result, pullback = jax.vjp(partial(forward, restarts), *floats)
    gradients = pullback(out_grad.astype(jnp.float32))
    return (result.astype(jnp.bfloat16), gradients[0], gradients[1], gradients[2], gradients[3], gradients[4], gradients[5], gradients[6], gradients[7], gradients[8], gradients[9], gradients[10], gradients[11], gradients[12], gradients[13], gradients[14], gradients[15], gradients[16], gradients[17])
```

```python
import functools
import jax
import jax.numpy as jnp
from jax import lax
from jax.experimental import pallas as pl
from jax.experimental.pallas import tpu as pltpu
from jax.sharding import PartitionSpec as P

MINI = 16
EPSILON = 1e-06
BASE_RATE = 1.0
F32 = jnp.float32
BF16 = jnp.bfloat16
NN = (((1,), (0,)), ((), ()))
NT = (((1,), (1,)), ((), ()))
TN = (((0,), (0,)), ((), ()))


def mm(left, right, dims):
    return lax.dot_general(left, right, dims, preferred_element_type=F32)


def packed(block, heads, head_dim, parts):
    turned = block.T
    width = block.shape[0] // parts
    return [
        jnp.concatenate(
            [
                turned[h * head_dim : (h + 1) * head_dim, j * width : (j + 1) * width]
                for h in range(heads)
            ],
            axis=1,
        )
        for j in range(parts)
    ]


def unpacked(pieces, heads):
    width = pieces[0].shape[1] // heads
    turned = jnp.concatenate(
        [
            jnp.concatenate([piece[:, h * width : (h + 1) * width] for piece in pieces], axis=1)
            for h in range(heads)
        ],
        axis=0,
    )
    return turned.T


def mean0(values):
    return jnp.mean(values, axis=0, keepdims=True)


def masks(chains, head_dim, dtype):
    lanes = chains * MINI
    rows = lax.broadcasted_iota(jnp.int32, (chains * head_dim, lanes), 0) // head_dim
    cols = lax.broadcasted_iota(jnp.int32, (chains * head_dim, lanes), 1) // MINI
    spread = rows == cols
    source = lax.broadcasted_iota(jnp.int32, (lanes, lanes), 0)
    target = lax.broadcasted_iota(jnp.int32, (lanes, lanes), 1)
    together = (source // MINI) == (target // MINI)
    earlier = jnp.logical_and(together, source <= target)
    scale = jnp.where(earlier, 1.0 / ((target % MINI) + 1).astype(F32), 0.0)
    return spread, together, scale


def spread_out(values, spread, chains):
    return jnp.where(spread, jnp.concatenate([values] * chains, axis=0), jnp.zeros((), values.dtype))


def forward_kernel(
    heads, head_dim, parts,
    slot_ref, queries_ref, keys_ref, values_ref, rate_ref, again_ref, again_wide_ref,
    start_ref, start_bias_ref, gain_ref, shift_ref,
    out_ref, normed_ref, spread_ref, grad_ref, rebuilt_ref, respread_ref, mix_ref, weight_ref,
    state, bias,
):
    chains = rate_ref.shape[-1] // MINI
    spread, together, scale = masks(chains, head_dim, BF16)
    ones = jnp.where(together, 1.0 / MINI, 0.0).astype(BF16)
    gain, shift = gain_ref[...], shift_ref[...]

    @pl.when(pl.program_id(0) == 0)
    def _():
        state[...] = jnp.zeros_like(state)
        bias[...] = jnp.zeros_like(bias)

    all_queries = packed(queries_ref[...], heads, head_dim, parts)
    all_keys = packed(keys_ref[...], heads, head_dim, parts)
    all_values = packed(values_ref[...], heads, head_dim, parts)
    weight = state[...]
    offset = bias[...]
    results = []
    for j in range(parts):
        query, key, value = all_queries[j], all_keys[j], all_values[j]
        rate = rate_ref[0, j : j + 1, :]
        low_key, low_query = key.astype(BF16), query.astype(BF16)
        wide_key = spread_out(low_key, spread, chains)
        wide_query = spread_out(low_query, spread, chains)
        mix = ((mm(low_key, low_query, TN) + 1.0) * scale).astype(BF16)
        weight = jnp.where(again_wide_ref[0, j : j + 1, :] > 0.0, start_ref[...], weight)
        offset = jnp.where(again_ref[0, j : j + 1, :] > 0.0, start_bias_ref[...], offset)
        low_weight = weight.astype(BF16)
        first = mm(low_weight, wide_key, NN) + offset
        center = first - mean0(first)
        inverse = lax.rsqrt(mean0(center * center) + EPSILON)
        normed = center * inverse
        residue = (normed * gain + shift - (value - key)) * gain
        inner = (residue - mean0(residue) - normed * mean0(residue * normed)) * inverse
        rated = (inner * rate).astype(BF16)
        combined = mm(low_weight, wide_query, NN) + offset - mm(rated, mix, NN)
        centered = combined - mean0(combined)
        inverse_out = lax.rsqrt(mean0(centered * centered) + EPSILON)
        rebuilt = centered * inverse_out
        results.append(query + rebuilt * gain + shift)
        weight = weight - mm(rated, wide_key, NT) * (1.0 / MINI)
        offset = offset - mm(rated, ones, NN)
        normed_ref[0, j] = normed
        grad_ref[0, j] = inner
        rebuilt_ref[0, j] = rebuilt
        spread_ref[0, j : j + 1, :] = inverse
        respread_ref[0, j : j + 1, :] = inverse_out
        mix_ref[0, j] = mix
        weight_ref[0, j] = low_weight
    out_ref[...] = unpacked(results, heads)
    state[...] = weight
    bias[...] = offset


def gathered_back(wide, lane_chain, head_dim, chains):
    total = wide[:head_dim]
    for c in range(1, chains):
        total = jnp.where(lane_chain == c, wide[c * head_dim : (c + 1) * head_dim], total)
    return total


def backward_kernel(
    heads, head_dim, parts,
    slot_ref, queries_ref, keys_ref, values_ref, delta_ref, rate_ref, again_ref, again_wide_ref,
    gain_ref, shift_ref,
    normed_ref, spread_ref, grad_ref, rebuilt_ref, respread_ref, mix_ref, weight_ref,
    dquery_ref, dkey_ref, dvalue_ref, drate_ref, dstart_ref, dstart_bias_ref, dgain_ref, dshift_ref,
    state, bias,
):
    chains = rate_ref.shape[-1] // MINI
    lanes = chains * MINI
    spread, together, scale = masks(chains, head_dim, BF16)
    ones = jnp.where(together, 1.0, 0.0).astype(BF16)
    lane_chain = lax.broadcasted_iota(jnp.int32, (head_dim, lanes), 1) // MINI
    gain, shift = gain_ref[...], shift_ref[...]

    @pl.when(pl.program_id(0) == 0)
    def _():
        state[...] = jnp.zeros_like(state)
        bias[...] = jnp.zeros_like(bias)
        dstart_ref[...] = jnp.zeros_like(dstart_ref)
        dstart_bias_ref[...] = jnp.zeros_like(dstart_bias_ref)
        dgain_ref[...] = jnp.zeros_like(dgain_ref)
        dshift_ref[...] = jnp.zeros_like(dshift_ref)

    all_queries = packed(queries_ref[...], heads, head_dim, parts)
    all_keys = packed(keys_ref[...], heads, head_dim, parts)
    all_values = packed(values_ref[...], heads, head_dim, parts)
    all_deltas = packed(delta_ref[...], heads, head_dim, parts)
    dweight = state[...]
    doffset = bias[...]
    dstart, dstart_bias = dstart_ref[...], dstart_bias_ref[...]
    dgain, dshift = dgain_ref[...], dshift_ref[...]
    dqueries, dkeys, dvalues = [None] * parts, [None] * parts, [None] * parts
    for j in reversed(range(parts)):
        query, key, value, delta = all_queries[j], all_keys[j], all_values[j], all_deltas[j]
        rate = rate_ref[0, j : j + 1, :]
        normed, inner, rebuilt = normed_ref[0, j], grad_ref[0, j], rebuilt_ref[0, j]
        inverse, inverse_out = spread_ref[0, j : j + 1, :], respread_ref[0, j : j + 1, :]
        mix, weight = mix_ref[0, j], weight_ref[0, j]
        low_key, low_query = key.astype(BF16), query.astype(BF16)
        wide_key = spread_out(low_key, spread, chains)
        wide_query = spread_out(low_query, spread, chains)
        rated = (inner * rate).astype(BF16)
        dnorm = delta * gain
        dcombined = (dnorm - mean0(dnorm) - rebuilt * mean0(dnorm * rebuilt)) * inverse_out
        low_dcombined = dcombined.astype(BF16)
        drated = -mm(low_dcombined, mix, NT)
        dscore = (-mm(rated, low_dcombined, TN) * scale).astype(BF16)
        low_dweight = dweight.astype(BF16)
        drated = drated - (mm(low_dweight, wide_key, NN) + doffset) * (1.0 / MINI)
        dinner = drated * rate
        drate_ref[0, j : j + 1, :] = jnp.sum(drated * inner, axis=0, keepdims=True)
        scaled = dinner * inverse
        offset_residue = normed * gain + shift - (value - key)
        residue = offset_residue * gain
        along = mean0(scaled * normed)
        dresidue = scaled - mean0(scaled) - normed * along
        gained = dresidue * gain
        dnormed = gained * gain - scaled * mean0(residue * normed) - residue * along
        dfirst = (
            dnormed - mean0(dnormed) - normed * (mean0(dnormed * normed) + mean0(dinner * inner))
        ) * inverse
        low_dfirst = dfirst.astype(BF16)
        dvalues[j] = -gained
        back_key = gathered_back(mm(weight, low_dfirst, TN), lane_chain, head_dim, chains)
        back_query = gathered_back(mm(weight, low_dcombined, TN), lane_chain, head_dim, chains)
        back_state = gathered_back(mm(low_dweight, rated, TN), lane_chain, head_dim, chains)
        dkeys[j] = gained + back_key - back_state * (1.0 / MINI) + mm(low_query, dscore, NT)
        dqueries[j] = delta + back_query + mm(low_key, dscore, NN)
        dgain = dgain + delta * rebuilt + dresidue * offset_residue + gained * normed
        dshift = dshift + delta + gained
        dweight = dweight + mm(low_dfirst, wide_key, NT) + mm(low_dcombined, wide_query, NT)
        both = (dfirst + dcombined).astype(BF16)
        doffset = doffset + mm(both, ones, NN)
        again_wide = again_wide_ref[0, j : j + 1, :] > 0.0
        again = again_ref[0, j : j + 1, :] > 0.0
        dstart = dstart + jnp.where(again_wide, dweight, 0.0)
        dstart_bias = dstart_bias + jnp.where(again, doffset, 0.0)
        dweight = jnp.where(again_wide, 0.0, dweight)
        doffset = jnp.where(again, 0.0, doffset)
    dquery_ref[...] = unpacked(dqueries, heads).astype(dquery_ref.dtype)
    dkey_ref[...] = unpacked(dkeys, heads).astype(dkey_ref.dtype)
    dvalue_ref[...] = unpacked(dvalues, heads).astype(dvalue_ref.dtype)
    state[...] = dweight
    bias[...] = doffset
    dstart_ref[...] = dstart
    dstart_bias_ref[...] = dstart_bias
    dgain_ref[...] = dgain
    dshift_ref[...] = dshift


def whole(shape):
    return pl.BlockSpec(shape, lambda *_: (0,) * len(shape))


def inner_forward(slot, queries, keys, values, rates, again, again_wide, start, start_bias, gain, shift, heads, head_dim, parts):
    steps, _, lanes = rates.shape
    tokens = queries.shape[0] // steps
    wide = start.shape[1]
    at_slot = pl.BlockSpec((tokens, heads * head_dim), lambda i, s: (jnp.bitwise_xor(i, s[0]), 0))

    def stepped(*shape):
        return pl.BlockSpec((1,) + shape, lambda i, s: (i,) + (0,) * len(shape))

    saved = [
        ((parts, head_dim, lanes), F32), ((parts, lanes), F32), ((parts, head_dim, lanes), F32),
        ((parts, head_dim, lanes), F32), ((parts, lanes), F32),
        ((parts, lanes, lanes), BF16), ((parts, head_dim, wide), BF16),
    ]
    return pl.pallas_call(
        functools.partial(forward_kernel, heads, head_dim, parts),
        out_shape=[jax.ShapeDtypeStruct(queries.shape, F32)]
        + [jax.ShapeDtypeStruct((steps,) + shape, kind) for shape, kind in saved],
        grid_spec=pltpu.PrefetchScalarGridSpec(
            num_scalar_prefetch=1,
            grid=(steps,),
            in_specs=[at_slot] * 3
            + [stepped(parts, lanes), stepped(parts, lanes), stepped(parts, wide)]
            + [whole(start.shape), whole(start_bias.shape), whole(gain.shape), whole(shift.shape)],
            out_specs=[at_slot] + [stepped(*shape) for shape, _ in saved],
            scratch_shapes=[pltpu.VMEM(start.shape, F32), pltpu.VMEM(start_bias.shape, F32)],
        ),
        compiler_params=pltpu.CompilerParams(
            dimension_semantics=("arbitrary",), vmem_limit_bytes=40 * 1024 * 1024
        ),
        name="inner_forward",
    )(slot, queries, keys, values, rates, again, again_wide, start, start_bias, gain, shift)


def inner_backward(slot, queries, keys, values, deltas, rates, again, again_wide, gain, shift, saved, heads, head_dim, parts):
    steps, _, lanes = rates.shape
    tokens = queries.shape[0] // steps
    wide = again_wide.shape[-1]
    at_slot = pl.BlockSpec(
        (tokens, heads * head_dim), lambda i, s: (jnp.bitwise_xor(steps - 1 - i, s[0]), 0)
    )

    def stepped(*shape):
        return pl.BlockSpec((1,) + shape, lambda i, s: (steps - 1 - i,) + (0,) * len(shape))

    return pl.pallas_call(
        functools.partial(backward_kernel, heads, head_dim, parts),
        out_shape=[jax.ShapeDtypeStruct(queries.shape, BF16)] * 3
        + [
            jax.ShapeDtypeStruct(rates.shape, F32),
            jax.ShapeDtypeStruct((head_dim, wide), F32),
            jax.ShapeDtypeStruct((head_dim, lanes), F32),
            jax.ShapeDtypeStruct((head_dim, lanes), F32),
            jax.ShapeDtypeStruct((head_dim, lanes), F32),
        ],
        grid_spec=pltpu.PrefetchScalarGridSpec(
            num_scalar_prefetch=1,
            grid=(steps,),
            in_specs=[at_slot] * 4
            + [stepped(parts, lanes), stepped(parts, lanes), stepped(parts, wide)]
            + [whole(gain.shape), whole(shift.shape)]
            + [stepped(*array.shape[1:]) for array in saved],
            out_specs=[at_slot] * 3
            + [stepped(parts, lanes), whole((head_dim, wide))]
            + [whole((head_dim, lanes))] * 3,
            scratch_shapes=[pltpu.VMEM((head_dim, wide), F32), pltpu.VMEM((head_dim, lanes), F32)],
        ),
        compiler_params=pltpu.CompilerParams(
            dimension_semantics=("arbitrary",), vmem_limit_bytes=40 * 1024 * 1024
        ),
        name="inner_backward",
    )(slot, queries, keys, values, deltas, rates, again, again_wide, gain, shift, *saved)


def bit_exchange(value, axis, bit):
    count = lax.axis_size(axis)
    return lax.ppermute(value, axis, [(i, i ^ bit) for i in range(count)])


def seq_bits():
    count = lax.axis_size("seq")
    bits = [1 << p for p in range(count.bit_length() - 1)]
    return bits


def gather_blocks(block):
    bits = seq_bits()
    near, far = bits[0], bits[1:]
    ways = max(1, len(far))
    width = block.shape[-1]
    pieces = []
    for way in range(ways):
        low, high = way * width // ways, (way + 1) * width // ways
        held = {0: block[:, low:high]}
        for step in range(len(far)):
            bit = far[(way + step) % len(far)]
            keys = sorted(held)
            moved = bit_exchange(jnp.stack([held[k] for k in keys]), "seq", bit)
            for n, k in enumerate(keys):
                held[k | bit] = moved[n]
        pieces.append(jnp.stack([held[k] for k in sorted(held)]))
    half = jnp.concatenate(pieces, axis=-1)
    other = bit_exchange(half, "seq", near)
    return jnp.stack([half, other], axis=1).reshape((-1,) + block.shape)


def reduce_blocks(blocks):
    bits = seq_bits()
    near, far = bits[0], bits[1:]
    ways = max(1, len(far))
    width = blocks.shape[-1]
    blocks = blocks.reshape((-1, 2) + blocks.shape[1:])
    half = blocks[:, 0] + bit_exchange(blocks[:, 1].astype(BF16), "seq", near).astype(F32)
    pieces = []
    for way in range(ways):
        low, high = way * width // ways, (way + 1) * width // ways
        held = {2 * k: half[k, :, low:high] for k in range(half.shape[0])}
        for step in range(len(far)):
            bit = far[(way + step) % len(far)]
            away = sorted(k for k in held if k & bit)
            moved = bit_exchange(jnp.stack([held[k].astype(BF16) for k in away]), "seq", bit)
            for n, k in enumerate(away):
                held[k ^ bit] = held[k ^ bit] + moved[n].astype(F32)
                del held[k]
        pieces.append(held[0])
    return jnp.concatenate(pieces, axis=-1)


def gelu_tanh(values):
    return jax.nn.gelu(values, approximate=True)


def shards(
    hidden_in,
    attn_gain,
    query_weight,
    key_weight,
    value_weight,
    rate_weight,
    gate_weight,
    init_weight,
    init_bias,
    inner_gain,
    inner_shift,
    post_gain,
    post_shift,
    out_weight,
    ffn_gain,
    ffn_gate_weight,
    ffn_up_weight,
    ffn_down_weight,
    doc_starts,
    out_grad,
):
    rows_here, stretch, model = hidden_in.shape
    head_count = rate_weight.shape[1]
    head_dim = init_weight.shape[1]
    parts = stretch // MINI
    seq_count = lax.axis_size("seq")
    rows_count = lax.axis_size("rows")
    share = model // (seq_count * rows_count)
    hidden_share = ffn_down_weight.shape[0]
    heads = head_count // seq_count
    width = heads * head_dim
    aligned = share % head_dim == 0
    groups, span = (rows_count, share) if aligned else (1, width)
    me = lax.axis_index("seq")
    slots = jnp.bitwise_xor(jnp.arange(seq_count, dtype=jnp.int32), me)
    everywhere = ("rows", "seq")

    def by_owner(values, group, size):
        split = values.reshape(values.shape[0], group, seq_count, size)
        return split.transpose(2, 0, 1, 3).reshape(seq_count, values.shape[0], group * size)

    def columns_in(values):
        mine = lax.all_to_all(values, "seq", 0, 0, tiled=True)
        return lax.all_gather(mine.reshape(-1, values.shape[-1]), "rows", axis=0, tiled=True)

    def columns_out(values):
        summed = lax.psum_scatter(values.astype(BF16), "rows", scatter_dimension=0, tiled=True)
        return lax.all_to_all(summed.reshape(seq_count, share, -1), "seq", 0, 0, tiled=True)

    def from_owner(values, group, size):
        split = values.reshape(seq_count, share, group, size)
        return split.transpose(1, 2, 0, 3).reshape(share, -1).astype(F32)

    def own_part(values):
        split = values.reshape(groups, seq_count, span, -1)
        return lax.dynamic_index_in_dim(split, me, 1, keepdims=False).reshape(width, -1)

    def placed(values):
        split = values.reshape(groups, 1, span, -1)
        here = (jnp.arange(seq_count) == me).reshape(1, -1, 1, 1)
        return jnp.where(here, split, 0.0).reshape(model, -1)

    def reordered(values):
        return values.reshape(rows_here, parts, MINI, -1).transpose(1, 0, 2, 3).reshape(-1, model)

    def restored(values):
        return values.reshape(parts, rows_here, MINI, -1).transpose(1, 0, 2, 3).reshape(rows_here, stretch, -1)

    vectors = jnp.stack(
        [attn_gain, ffn_gain, init_bias, inner_gain, inner_shift, post_gain, post_shift], axis=1
    )
    count = vectors.shape[1]
    small = lax.all_gather(
        jnp.concatenate([init_weight, rate_weight, vectors], axis=1), everywhere, axis=0, tiled=True
    )
    qkv_weight = columns_in(
        jnp.concatenate([by_owner(w, groups, span) for w in (query_weight, key_weight, value_weight)], axis=2)
    )
    gate_own = columns_in(by_owner(gate_weight, groups, span))
    if aligned:
        out_own = lax.all_gather(out_weight, "rows", axis=0, tiled=True)
    else:
        out_own = own_part(lax.all_gather(out_weight, everywhere, axis=0, tiled=True))
    ffn_wide = columns_in(
        jnp.concatenate(
            [by_owner(w, rows_count, hidden_share) for w in (ffn_gate_weight, ffn_up_weight)], axis=2
        )
    )
    hidden_units = rows_count * hidden_share
    gate_wide, up_wide = ffn_wide[:, :hidden_units], ffn_wide[:, hidden_units:]
    down_wide = lax.all_gather(ffn_down_weight, "rows", axis=0, tiled=True)

    gain_attn = small[:, head_dim + head_count].astype(F32)
    gain_ffn = small[:, head_dim + head_count + 1].astype(F32)
    own_small = own_part(small)
    own_vectors = own_small[:, head_dim + head_count :].astype(F32)
    rate_all = small[:, head_dim : head_dim + head_count].reshape(model, groups, seq_count, -1)
    rate_own = lax.dynamic_index_in_dim(rate_all, me, 2, keepdims=False).reshape(model, heads)
    lanes = heads * rows_here * MINI

    def by_lane(values, repeat):
        turned = values.reshape(heads, head_dim).T
        return jnp.broadcast_to(turned[:, :, None], (head_dim, heads, repeat)).reshape(head_dim, -1)

    bias_lanes = by_lane(own_vectors[:, 2], rows_here * MINI)
    gain_lanes = by_lane(own_vectors[:, 3], rows_here * MINI)
    shift_lanes = by_lane(own_vectors[:, 4], rows_here * MINI)
    post_scale, post_offset = own_vectors[:, 5], own_vectors[:, 6]
    start = own_small[:, :head_dim].astype(F32).reshape(heads, head_dim, head_dim).transpose(2, 0, 1)
    start = jnp.broadcast_to(start[:, :, None], (head_dim, heads, rows_here, head_dim)).reshape(head_dim, -1)

    steps = seq_count
    position = jnp.arange(steps * parts, dtype=jnp.int32) * MINI
    restarts = jnp.logical_or(
        position[:, None] == 0, jnp.any(doc_starts[None] == position[:, None, None], axis=2)
    ).astype(F32)

    def by_chain(repeat):
        wide = jnp.broadcast_to(
            restarts[:, None, :, None], (steps * parts, heads, rows_here, repeat)
        )
        return wide.reshape(steps, parts, -1)

    again, again_wide = by_chain(MINI), by_chain(head_dim)

    hidden = reordered(hidden_in)
    cotangent = reordered(out_grad)
    tokens = hidden.astype(F32)
    tokens_all = gather_blocks(hidden).reshape(-1, model).astype(F32)
    inverse_all = lax.rsqrt(jnp.mean(tokens_all * tokens_all, axis=-1, keepdims=True) + EPSILON)
    plain_all = tokens_all * inverse_all
    normed = (plain_all * gain_attn).astype(BF16)

    def project(matrix):
        return jnp.dot(normed, matrix, preferred_element_type=F32)

    qkv = project(qkv_weight)
    queries, keys, values = (qkv[:, n * width : (n + 1) * width] for n in range(3))
    gate_pre = project(gate_own)
    logits = project(rate_own)
    slope = jax.nn.sigmoid(logits)

    def to_lanes(per_token):
        ordered = jnp.take(per_token.reshape(steps, -1, heads), slots, axis=0)
        ordered = ordered.reshape(steps, parts, rows_here * MINI, heads)
        return ordered.transpose(0, 1, 3, 2).reshape(steps, parts, lanes)

    def from_lanes(per_lane):
        ordered = per_lane.reshape(steps, parts, heads, rows_here * MINI).transpose(0, 1, 3, 2)
        return jnp.take(ordered.reshape(steps, -1, heads), slots, axis=0).reshape(-1, heads)

    rates = to_lanes(slope * (BASE_RATE / head_dim))
    slot = me.astype(jnp.int32).reshape(1)
    inner_out, *saved = inner_forward(
        slot, queries, keys, values, rates, again, again_wide, start, bias_lanes, gain_lanes,
        shift_lanes, heads, head_dim, parts,
    )
    def feature_mean(*values):
        sums = jnp.stack([jnp.sum(v, axis=1) for v in values]).reshape(len(values), steps, -1)
        total = lax.psum(jnp.take(sums, slots, axis=1), "seq") / model
        return jnp.take(total, slots, axis=1).reshape(len(values), -1, 1)

    moments = feature_mean(inner_out, inner_out * inner_out)
    post_mean = moments[0]
    post_inverse = lax.rsqrt(moments[1] - post_mean * post_mean + EPSILON)
    post_norm = (inner_out - post_mean) * post_inverse
    post_out = post_norm * post_scale + post_offset
    gelu_value, gelu_pull = jax.vjp(gelu_tanh, gate_pre)
    gated = (gelu_value * post_out).astype(BF16)
    branch = jnp.dot(gated, out_own, preferred_element_type=F32)
    residual = tokens + reduce_blocks(branch.reshape(steps, -1, model))

    inverse_two = lax.rsqrt(jnp.mean(residual * residual, axis=-1, keepdims=True) + EPSILON)
    ffn_in = gather_blocks((residual * inverse_two * gain_ffn).astype(BF16)).reshape(-1, model)
    cot_all = gather_blocks(cotangent).reshape(-1, model)
    gate_value = jnp.dot(ffn_in, gate_wide, preferred_element_type=F32)
    up_value = jnp.dot(ffn_in, up_wide, preferred_element_type=F32)
    sigmoid_gate = jax.nn.sigmoid(gate_value)
    active = (gate_value * sigmoid_gate * up_value).astype(BF16)
    down = jnp.dot(active, down_wide, preferred_element_type=F32)
    delta_active = jnp.einsum("td,fd->tf", cot_all, down_wide, preferred_element_type=F32)
    delta_up = (delta_active * gate_value * sigmoid_gate).astype(BF16)
    delta_gate = (
        delta_active * up_value * sigmoid_gate * (1.0 + gate_value * (1.0 - sigmoid_gate))
    ).astype(BF16)
    delta_ffn = jnp.einsum("tf,df->td", delta_up, up_wide, preferred_element_type=F32) + jnp.einsum(
        "tf,df->td", delta_gate, gate_wide, preferred_element_type=F32
    )
    delta_ffn = reduce_blocks(delta_ffn.reshape(steps, -1, model))
    block_out = residual + reduce_blocks(down.reshape(steps, -1, model))

    def token_grad(left, right):
        return jnp.einsum("td,te->de", left, right, preferred_element_type=F32)

    grad_down = lax.psum_scatter(
        token_grad(active, cot_all).astype(BF16), "rows", scatter_dimension=0, tiled=True
    ).astype(F32)
    grad_gate = from_owner(columns_out(token_grad(ffn_in, delta_gate)), rows_count, hidden_share)
    grad_up = from_owner(columns_out(token_grad(ffn_in, delta_up)), rows_count, hidden_share)

    grad_gain_ffn = jnp.sum(delta_ffn * residual * inverse_two, axis=0)
    scaled_two = delta_ffn * gain_ffn
    delta_after = (
        cotangent.astype(F32)
        + inverse_two * scaled_two
        - residual * inverse_two**3 * jnp.mean(scaled_two * residual, axis=-1, keepdims=True)
    )
    delta_branch = gather_blocks(delta_after.astype(BF16)).reshape(-1, model)

    grad_out = token_grad(gated, delta_branch)
    if aligned:
        grad_out = lax.psum_scatter(grad_out.astype(BF16), "rows", scatter_dimension=0, tiled=True)
    else:
        grad_out = lax.psum_scatter(
            placed(grad_out).astype(BF16), everywhere, scatter_dimension=0, tiled=True
        )
    delta_gated = jnp.einsum("te,de->td", delta_branch, out_own, preferred_element_type=F32)
    delta_pre = gelu_pull(delta_gated * post_out)[0].astype(BF16)
    delta_post = delta_gated * gelu_value
    grad_post_scale = jnp.sum(delta_post * post_norm, axis=0)
    grad_post_shift = jnp.sum(delta_post, axis=0)
    delta_norm = delta_post * post_scale
    means = feature_mean(delta_norm, delta_norm * post_norm)
    delta_inner = (delta_norm - means[0] - post_norm * means[1]) * post_inverse
    (
        delta_queries, delta_keys, delta_values, delta_rates,
        grad_start, grad_bias, grad_inner_gain, grad_inner_shift,
    ) = inner_backward(
        slot, queries, keys, values, delta_inner, rates, again, again_wide, gain_lanes, shift_lanes,
        saved, heads, head_dim, parts,
    )
    delta_logits = (
        from_lanes(delta_rates) * slope * (1.0 - slope) * (BASE_RATE / head_dim)
    ).astype(BF16)
    delta_qkv = jnp.concatenate([delta_queries, delta_keys, delta_values], axis=1)

    def back_project(delta, matrix):
        return jnp.einsum("te,de->td", delta, matrix, preferred_element_type=F32)

    delta_normed = (
        back_project(delta_qkv, qkv_weight)
        + back_project(delta_pre, gate_own)
        + back_project(delta_logits, rate_own)
    )
    grad_gain_attn = jnp.sum(delta_normed * plain_all, axis=0)
    delta_normed = reduce_blocks(delta_normed.reshape(steps, -1, model))
    inverse_one = lax.rsqrt(jnp.mean(tokens * tokens, axis=-1, keepdims=True) + EPSILON)
    scaled_one = delta_normed * gain_attn
    hidden_grad = (
        delta_after
        + inverse_one * scaled_one
        - tokens * inverse_one**3 * jnp.mean(scaled_one * tokens, axis=-1, keepdims=True)
    )
    qkv_grads = columns_out(token_grad(normed, delta_qkv))
    grad_query, grad_key, grad_value = (
        from_owner(qkv_grads[:, :, n * width : (n + 1) * width], groups, span) for n in range(3)
    )
    grad_gate_weight = from_owner(columns_out(token_grad(normed, delta_pre)), groups, span)

    def lane_sum(per_lane, repeat):
        return per_lane.reshape(head_dim, heads, repeat).sum(axis=2).T.reshape(width, 1)

    grad_start = grad_start.reshape(head_dim, heads, rows_here, head_dim).sum(axis=2)
    grad_start = grad_start.transpose(1, 2, 0).reshape(width, head_dim)
    grad_bias = grad_bias.reshape(head_dim, heads, rows_here, MINI)[..., 0]
    grad_rate = token_grad(normed, delta_logits).reshape(model, groups, 1, -1)
    here = (jnp.arange(seq_count) == me).reshape(1, 1, -1, 1)
    grad_rate = jnp.where(here, grad_rate, 0.0).reshape(model, head_count)
    own_grads = jnp.concatenate(
        [
            grad_start,
            lane_sum(grad_bias, rows_here),
            lane_sum(grad_inner_gain, rows_here * MINI),
            lane_sum(grad_inner_shift, rows_here * MINI),
            grad_post_scale[:, None],
            grad_post_shift[:, None],
        ],
        axis=1,
    )
    small_grads = lax.psum_scatter(
        jnp.concatenate(
            [placed(own_grads), grad_rate, grad_gain_attn[:, None], grad_gain_ffn[:, None]], axis=1
        ),
        everywhere, scatter_dimension=0, tiled=True,
    )
    after = head_dim + 5
    return (
        restored(block_out).astype(BF16),
        restored(hidden_grad),
        small_grads[:, after + head_count],
        grad_query,
        grad_key,
        grad_value,
        small_grads[:, after : after + head_count],
        grad_gate_weight,
        small_grads[:, :head_dim],
        small_grads[:, head_dim],
        small_grads[:, head_dim + 1],
        small_grads[:, head_dim + 2],
        small_grads[:, head_dim + 3],
        small_grads[:, head_dim + 4],
        grad_out.astype(F32),
        small_grads[:, after + head_count + 1],
        grad_gate,
        grad_up,
        grad_down,
    )


def solution(mesh):
    split = P(("rows", "seq"))
    matrix = P(("rows", "seq"), None)
    tokens = P("rows", "seq", None)
    return jax.shard_map(
        shards,
        mesh=mesh,
        in_specs=(
            tokens, split, matrix, matrix, matrix, matrix, matrix, matrix, split, split, split, split,
            split, matrix, split, matrix, matrix, matrix, P("rows", None), tokens,
        ),
        out_specs=(
            tokens, tokens, split, matrix, matrix, matrix, matrix, matrix, matrix, split, split, split,
            split, split, matrix, split, matrix, matrix, matrix,
        ),
        check_vma=False,
    )
```

```python
import functools
import jax
import jax.numpy as jnp
from jax import lax
from jax.experimental import pallas as pl
from jax.experimental.pallas import tpu as pltpu
from jax.sharding import PartitionSpec as P

MINI = 16
EPSILON = 1e-06
BASE_RATE = 1.0
F32 = jnp.float32
BF16 = jnp.bfloat16
NN = (((1,), (0,)), ((), ()))
NT = (((1,), (1,)), ((), ()))
TN = (((0,), (0,)), ((), ()))


def mm(left, right, dims):
    return lax.dot_general(left, right, dims, preferred_element_type=F32)


def packed(block, heads, head_dim, parts):
    turned = block.T
    width = block.shape[0] // parts
    return [
        jnp.concatenate(
            [
                turned[h * head_dim : (h + 1) * head_dim, j * width : (j + 1) * width]
                for h in range(heads)
            ],
            axis=1,
        )
        for j in range(parts)
    ]


def unpacked(pieces, heads):
    width = pieces[0].shape[1] // heads
    turned = jnp.concatenate(
        [
            jnp.concatenate([piece[:, h * width : (h + 1) * width] for piece in pieces], axis=1)
            for h in range(heads)
        ],
        axis=0,
    )
    return turned.T


def mean0(values):
    return jnp.mean(values, axis=0, keepdims=True)


def masks(chains, head_dim, dtype):
    lanes = chains * MINI
    rows = lax.broadcasted_iota(jnp.int32, (chains * head_dim, lanes), 0) // head_dim
    cols = lax.broadcasted_iota(jnp.int32, (chains * head_dim, lanes), 1) // MINI
    spread = rows == cols
    source = lax.broadcasted_iota(jnp.int32, (lanes, lanes), 0)
    target = lax.broadcasted_iota(jnp.int32, (lanes, lanes), 1)
    together = (source // MINI) == (target // MINI)
    earlier = jnp.logical_and(together, source <= target)
    scale = jnp.where(earlier, 1.0 / ((target % MINI) + 1).astype(F32), 0.0)
    return spread, together, scale


def spread_out(values, spread, chains):
    return jnp.where(spread, jnp.concatenate([values] * chains, axis=0), jnp.zeros((), values.dtype))


def forward_kernel(
    heads, head_dim, parts,
    slot_ref, queries_ref, keys_ref, values_ref, rate_ref, again_ref, again_wide_ref,
    start_ref, start_bias_ref, gain_ref, shift_ref,
    out_ref, normed_ref, spread_ref, grad_ref, rebuilt_ref, respread_ref, mix_ref, weight_ref,
    state, bias,
):
    chains = rate_ref.shape[-1] // MINI
    spread, together, scale = masks(chains, head_dim, BF16)
    ones = jnp.where(together, 1.0 / MINI, 0.0).astype(BF16)
    gain, shift = gain_ref[...], shift_ref[...]

    @pl.when(pl.program_id(0) == 0)
    def _():
        state[...] = jnp.zeros_like(state)
        bias[...] = jnp.zeros_like(bias)

    all_queries = packed(queries_ref[...], heads, head_dim, parts)
    all_keys = packed(keys_ref[...], heads, head_dim, parts)
    all_values = packed(values_ref[...], heads, head_dim, parts)
    weight = state[...]
    offset = bias[...]
    results = []
    for j in range(parts):
        query, key, value = all_queries[j], all_keys[j], all_values[j]
        rate = rate_ref[0, j : j + 1, :]
        low_key, low_query = key.astype(BF16), query.astype(BF16)
        wide_key = spread_out(low_key, spread, chains)
        wide_query = spread_out(low_query, spread, chains)
        mix = ((mm(low_key, low_query, TN) + 1.0) * scale).astype(BF16)
        weight = jnp.where(again_wide_ref[0, j : j + 1, :] > 0.0, start_ref[...], weight)
        offset = jnp.where(again_ref[0, j : j + 1, :] > 0.0, start_bias_ref[...], offset)
        low_weight = weight.astype(BF16)
        first = mm(low_weight, wide_key, NN) + offset
        center = first - mean0(first)
        inverse = lax.rsqrt(mean0(center * center) + EPSILON)
        normed = center * inverse
        residue = (normed * gain + shift - (value - key)) * gain
        inner = (residue - mean0(residue) - normed * mean0(residue * normed)) * inverse
        rated = (inner * rate).astype(BF16)
        combined = mm(low_weight, wide_query, NN) + offset - mm(rated, mix, NN)
        centered = combined - mean0(combined)
        inverse_out = lax.rsqrt(mean0(centered * centered) + EPSILON)
        rebuilt = centered * inverse_out
        results.append(query + rebuilt * gain + shift)
        weight = weight - mm(rated, wide_key, NT) * (1.0 / MINI)
        offset = offset - mm(rated, ones, NN)
        normed_ref[0, j] = normed
        grad_ref[0, j] = inner
        rebuilt_ref[0, j] = rebuilt
        spread_ref[0, j : j + 1, :] = inverse
        respread_ref[0, j : j + 1, :] = inverse_out
        mix_ref[0, j] = mix
        weight_ref[0, j] = low_weight
    out_ref[...] = unpacked(results, heads)
    state[...] = weight
    bias[...] = offset


def gathered_back(wide, lane_chain, head_dim, chains):
    total = wide[:head_dim]
    for c in range(1, chains):
        total = jnp.where(lane_chain == c, wide[c * head_dim : (c + 1) * head_dim], total)
    return total


def backward_kernel(
    heads, head_dim, parts,
    slot_ref, queries_ref, keys_ref, values_ref, delta_ref, rate_ref, again_ref, again_wide_ref,
    gain_ref, shift_ref,
    normed_ref, spread_ref, grad_ref, rebuilt_ref, respread_ref, mix_ref, weight_ref,
    dquery_ref, dkey_ref, dvalue_ref, drate_ref, dstart_ref, dstart_bias_ref, dgain_ref, dshift_ref,
    state, bias,
):
    chains = rate_ref.shape[-1] // MINI
    lanes = chains * MINI
    spread, together, scale = masks(chains, head_dim, BF16)
    ones = jnp.where(together, 1.0, 0.0).astype(BF16)
    lane_chain = lax.broadcasted_iota(jnp.int32, (head_dim, lanes), 1) // MINI
    gain, shift = gain_ref[...], shift_ref[...]

    @pl.when(pl.program_id(0) == 0)
    def _():
        state[...] = jnp.zeros_like(state)
        bias[...] = jnp.zeros_like(bias)
        dstart_ref[...] = jnp.zeros_like(dstart_ref)
        dstart_bias_ref[...] = jnp.zeros_like(dstart_bias_ref)
        dgain_ref[...] = jnp.zeros_like(dgain_ref)
        dshift_ref[...] = jnp.zeros_like(dshift_ref)

    all_queries = packed(queries_ref[...], heads, head_dim, parts)
    all_keys = packed(keys_ref[...], heads, head_dim, parts)
    all_values = packed(values_ref[...], heads, head_dim, parts)
    all_deltas = packed(delta_ref[...], heads, head_dim, parts)
    dweight = state[...]
    doffset = bias[...]
    dstart, dstart_bias = dstart_ref[...], dstart_bias_ref[...]
    dgain, dshift = dgain_ref[...], dshift_ref[...]
    dqueries, dkeys, dvalues = [None] * parts, [None] * parts, [None] * parts
    for j in reversed(range(parts)):
        query, key, value, delta = all_queries[j], all_keys[j], all_values[j], all_deltas[j]
        rate = rate_ref[0, j : j + 1, :]
        normed, inner, rebuilt = normed_ref[0, j], grad_ref[0, j], rebuilt_ref[0, j]
        inverse, inverse_out = spread_ref[0, j : j + 1, :], respread_ref[0, j : j + 1, :]
        mix, weight = mix_ref[0, j], weight_ref[0, j]
        low_key, low_query = key.astype(BF16), query.astype(BF16)
        wide_key = spread_out(low_key, spread, chains)
        wide_query = spread_out(low_query, spread, chains)
        rated = (inner * rate).astype(BF16)
        dnorm = delta * gain
        dcombined = (dnorm - mean0(dnorm) - rebuilt * mean0(dnorm * rebuilt)) * inverse_out
        low_dcombined = dcombined.astype(BF16)
        drated = -mm(low_dcombined, mix, NT)
        dscore = (-mm(rated, low_dcombined, TN) * scale).astype(BF16)
        low_dweight = dweight.astype(BF16)
        drated = drated - (mm(low_dweight, wide_key, NN) + doffset) * (1.0 / MINI)
        dinner = drated * rate
        drate_ref[0, j : j + 1, :] = jnp.sum(drated * inner, axis=0, keepdims=True)
        scaled = dinner * inverse
        offset_residue = normed * gain + shift - (value - key)
        residue = offset_residue * gain
        along = mean0(scaled * normed)
        dresidue = scaled - mean0(scaled) - normed * along
        gained = dresidue * gain
        dnormed = gained * gain - scaled * mean0(residue * normed) - residue * along
        dfirst = (
            dnormed - mean0(dnormed) - normed * (mean0(dnormed * normed) + mean0(dinner * inner))
        ) * inverse
        low_dfirst = dfirst.astype(BF16)
        dvalues[j] = -gained
        back_key = gathered_back(mm(weight, low_dfirst, TN), lane_chain, head_dim, chains)
        back_query = gathered_back(mm(weight, low_dcombined, TN), lane_chain, head_dim, chains)
        back_state = gathered_back(mm(low_dweight, rated, TN), lane_chain, head_dim, chains)
        dkeys[j] = gained + back_key - back_state * (1.0 / MINI) + mm(low_query, dscore, NT)
        dqueries[j] = delta + back_query + mm(low_key, dscore, NN)
        dgain = dgain + delta * rebuilt + dresidue * offset_residue + gained * normed
        dshift = dshift + delta + gained
        dweight = dweight + mm(low_dfirst, wide_key, NT) + mm(low_dcombined, wide_query, NT)
        both = (dfirst + dcombined).astype(BF16)
        doffset = doffset + mm(both, ones, NN)
        again_wide = again_wide_ref[0, j : j + 1, :] > 0.0
        again = again_ref[0, j : j + 1, :] > 0.0
        dstart = dstart + jnp.where(again_wide, dweight, 0.0)
        dstart_bias = dstart_bias + jnp.where(again, doffset, 0.0)
        dweight = jnp.where(again_wide, 0.0, dweight)
        doffset = jnp.where(again, 0.0, doffset)
    dquery_ref[...] = unpacked(dqueries, heads).astype(dquery_ref.dtype)
    dkey_ref[...] = unpacked(dkeys, heads).astype(dkey_ref.dtype)
    dvalue_ref[...] = unpacked(dvalues, heads).astype(dvalue_ref.dtype)
    state[...] = dweight
    bias[...] = doffset
    dstart_ref[...] = dstart
    dstart_bias_ref[...] = dstart_bias
    dgain_ref[...] = dgain
    dshift_ref[...] = dshift


def whole(shape):
    return pl.BlockSpec(shape, lambda *_: (0,) * len(shape))


def place(step, own, count):
    apart = jnp.bitwise_xor(step, own)
    return jnp.bitwise_and(apart, 1) * (count // 2) + lax.shift_right_logical(apart, 1)


def inner_forward(slot, queries, keys, values, rates, again, again_wide, start, start_bias, gain, shift, heads, head_dim, parts):
    steps, _, lanes = rates.shape
    tokens = queries.shape[0] // steps
    wide = start.shape[1]
    at_slot = pl.BlockSpec((tokens, heads * head_dim), lambda i, s: (place(i, s[0], steps), 0))

    def stepped(*shape):
        return pl.BlockSpec((1,) + shape, lambda i, s: (i,) + (0,) * len(shape))

    saved = [
        ((parts, head_dim, lanes), F32), ((parts, lanes), F32), ((parts, head_dim, lanes), F32),
        ((parts, head_dim, lanes), F32), ((parts, lanes), F32),
        ((parts, lanes, lanes), BF16), ((parts, head_dim, wide), BF16),
    ]
    return pl.pallas_call(
        functools.partial(forward_kernel, heads, head_dim, parts),
        out_shape=[jax.ShapeDtypeStruct(queries.shape, F32)]
        + [jax.ShapeDtypeStruct((steps,) + shape, kind) for shape, kind in saved],
        grid_spec=pltpu.PrefetchScalarGridSpec(
            num_scalar_prefetch=1,
            grid=(steps,),
            in_specs=[at_slot] * 3
            + [stepped(parts, lanes), stepped(parts, lanes), stepped(parts, wide)]
            + [whole(start.shape), whole(start_bias.shape), whole(gain.shape), whole(shift.shape)],
            out_specs=[at_slot] + [stepped(*shape) for shape, _ in saved],
            scratch_shapes=[pltpu.VMEM(start.shape, F32), pltpu.VMEM(start_bias.shape, F32)],
        ),
        compiler_params=pltpu.CompilerParams(
            dimension_semantics=("arbitrary",), vmem_limit_bytes=40 * 1024 * 1024
        ),
        name="inner_forward",
    )(slot, queries, keys, values, rates, again, again_wide, start, start_bias, gain, shift)


def inner_backward(slot, queries, keys, values, deltas, rates, again, again_wide, gain, shift, saved, heads, head_dim, parts):
    steps, _, lanes = rates.shape
    tokens = queries.shape[0] // steps
    wide = again_wide.shape[-1]
    at_slot = pl.BlockSpec(
        (tokens, heads * head_dim), lambda i, s: (place(steps - 1 - i, s[0], steps), 0)
    )

    def stepped(*shape):
        return pl.BlockSpec((1,) + shape, lambda i, s: (steps - 1 - i,) + (0,) * len(shape))

    return pl.pallas_call(
        functools.partial(backward_kernel, heads, head_dim, parts),
        out_shape=[jax.ShapeDtypeStruct(queries.shape, BF16)] * 3
        + [
            jax.ShapeDtypeStruct(rates.shape, F32),
            jax.ShapeDtypeStruct((head_dim, wide), F32),
            jax.ShapeDtypeStruct((head_dim, lanes), F32),
            jax.ShapeDtypeStruct((head_dim, lanes), F32),
            jax.ShapeDtypeStruct((head_dim, lanes), F32),
        ],
        grid_spec=pltpu.PrefetchScalarGridSpec(
            num_scalar_prefetch=1,
            grid=(steps,),
            in_specs=[at_slot] * 4
            + [stepped(parts, lanes), stepped(parts, lanes), stepped(parts, wide)]
            + [whole(gain.shape), whole(shift.shape)]
            + [stepped(*array.shape[1:]) for array in saved],
            out_specs=[at_slot] * 3
            + [stepped(parts, lanes), whole((head_dim, wide))]
            + [whole((head_dim, lanes))] * 3,
            scratch_shapes=[pltpu.VMEM((head_dim, wide), F32), pltpu.VMEM((head_dim, lanes), F32)],
        ),
        compiler_params=pltpu.CompilerParams(
            dimension_semantics=("arbitrary",), vmem_limit_bytes=40 * 1024 * 1024
        ),
        name="inner_backward",
    )(slot, queries, keys, values, deltas, rates, again, again_wide, gain, shift, *saved)


def cut_heads_kernel(groups, seq_count, span, *refs):
    out_ref = refs[-1]
    for s in range(seq_count):
        pieces = [
            ref[:, at : at + span].astype(F32)
            for ref in refs[:-1]
            for at in ((g * seq_count + s) * span for g in range(groups))
        ]
        out_ref[s] = jnp.concatenate(pieces, axis=1).astype(out_ref.dtype)


def cut_heads(weights, groups, seq_count, span):
    rows = weights[0].shape[0]
    return pl.pallas_call(
        functools.partial(cut_heads_kernel, groups, seq_count, span),
        out_shape=jax.ShapeDtypeStruct((seq_count, rows, len(weights) * groups * span), BF16),
        compiler_params=pltpu.CompilerParams(vmem_limit_bytes=40 * 1024 * 1024),
        name="cut_heads",
    )(*weights)


def join_heads_kernel(groups, seq_count, span, parts_ref, *refs):
    for n, ref in enumerate(refs):
        pieces = []
        for g in range(groups):
            for s in range(seq_count):
                at = (n * groups + g) * span
                pieces.append(parts_ref[s, :, at : at + span].astype(F32))
        ref[...] = jnp.concatenate(pieces, axis=1)


def join_heads(parts, count, groups, seq_count, span):
    whole_row = jax.ShapeDtypeStruct((parts.shape[1], groups * seq_count * span), F32)
    return pl.pallas_call(
        functools.partial(join_heads_kernel, groups, seq_count, span),
        out_shape=[whole_row] * count,
        compiler_params=pltpu.CompilerParams(vmem_limit_bytes=40 * 1024 * 1024),
        name="join_heads",
    )(parts)


def exchange(value, axis, bit):
    count = lax.axis_size(axis)
    return lax.ppermute(value, axis, [(i, i ^ bit) for i in range(count)])


def bits_of(axis):
    return [(axis, 1 << p) for p in range(lax.axis_size(axis).bit_length() - 1)]


def cuts_of(width, ways):
    unit = 128 if width >= 128 * ways else 1
    return [unit * (n * (width // unit) // ways) for n in range(ways)] + [width]


def gather_blocks(block, bits, tied=None):
    near, far = bits[0], bits[1:]
    ways = max(1, len(far))
    cuts = cuts_of(block.shape[-1], ways)
    held = [{0: block[:, cuts[way] : cuts[way + 1]]} for way in range(ways)]
    for step in range(len(far)):
        for way in range(ways):
            bit = (way + step) % len(far)
            keys = sorted(held[way])
            moved = exchange(jnp.stack([held[way][k] for k in keys]), *far[bit])
            for n, k in enumerate(keys):
                held[way][k | 1 << bit] = moved[n]
    half = jnp.concatenate([jnp.stack([h[k] for k in sorted(h)]) for h in held], axis=-1)
    if tied is not None:
        half, tied = lax.optimization_barrier((half, tied))
    whole = jnp.concatenate([half, exchange(half, *near)], axis=0)
    return whole if tied is None else (whole, tied)


def reduce_blocks(own, away, bits, kind=BF16):
    near, far = bits[0], bits[1:]
    ways = max(1, len(far))
    cuts = cuts_of(own.shape[-1], ways)
    half = own.astype(F32) + exchange(away.astype(kind), *near).astype(F32)
    held = [
        {k: half[k, :, cuts[way] : cuts[way + 1]] for k in range(half.shape[0])} for way in range(ways)
    ]
    for step in range(len(far)):
        for way in range(ways):
            bit = (way + step) % len(far)
            gone = sorted(k for k in held[way] if k >> bit & 1)
            moved = exchange(jnp.stack([held[way][k].astype(kind) for k in gone]), *far[bit])
            for n, k in enumerate(gone):
                held[way][k ^ 1 << bit] = held[way][k ^ 1 << bit] + moved[n].astype(F32)
                del held[way][k]
    return jnp.concatenate([h[0] for h in held], axis=-1)


def has_bit(axis, bit):
    return jnp.bitwise_and(lax.axis_index(axis), bit) > 0


def gather_natural(value, bits):
    for axis, bit in bits:
        other = exchange(value, axis, bit)
        high = has_bit(axis, bit)
        value = jnp.concatenate([jnp.where(high, other, value), jnp.where(high, value, other)], axis=0)
    return value


def halved(value, dim, axis, bit):
    half = value.shape[dim] // 2
    high = has_bit(axis, bit)
    low_half = lax.slice_in_dim(value, 0, half, axis=dim)
    high_half = lax.slice_in_dim(value, half, 2 * half, axis=dim)
    other = exchange(jnp.where(high, low_half, high_half), axis, bit)
    return jnp.where(high, high_half, low_half) + other


def gelu_tanh(values):
    return jax.nn.gelu(values, approximate=True)


def shards(
    hidden_in,
    attn_gain,
    query_weight,
    key_weight,
    value_weight,
    rate_weight,
    gate_weight,
    init_weight,
    init_bias,
    inner_gain,
    inner_shift,
    post_gain,
    post_shift,
    out_weight,
    ffn_gain,
    ffn_gate_weight,
    ffn_up_weight,
    ffn_down_weight,
    doc_starts,
    out_grad,
):
    rows_here, stretch, model = hidden_in.shape
    head_count = rate_weight.shape[1]
    head_dim = init_weight.shape[1]
    parts = stretch // MINI
    local = rows_here * stretch
    seq_count = lax.axis_size("seq")
    rows_count = lax.axis_size("rows")
    share = model // (seq_count * rows_count)
    unit_share = ffn_down_weight.shape[0]
    heads = head_count // seq_count
    width = heads * head_dim
    aligned = share % head_dim == 0
    groups, span = (rows_count, share) if aligned else (1, width)
    me = lax.axis_index("seq")
    everywhere = ("rows", "seq")
    seq_bits = bits_of("seq")
    row_bits = bits_of("rows")
    units = rows_count * unit_share
    spare = -unit_share % 16

    def shuffled(values):
        return lax.all_to_all(values, "seq", 0, 0, tiled=True).reshape(-1, values.shape[-1])

    def row_sums(values):
        summed = lax.psum_scatter(values, "rows", scatter_dimension=0, tiled=True)
        return summed.reshape(seq_count, share, -1)

    def columns_out(values):
        return lax.all_to_all(values, "seq", 0, 0, tiled=True)

    def own_part(values):
        split = values.reshape(groups, seq_count, span, -1)
        return lax.dynamic_index_in_dim(split, me, 1, keepdims=False).reshape(width, -1)

    def placed(values):
        split = values.reshape(groups, 1, span, -1)
        here = (jnp.arange(seq_count) == me).reshape(1, -1, 1, 1)
        return jnp.where(here, split, 0.0).reshape(model, -1)

    def reordered(values):
        return values.reshape(rows_here, parts, MINI, -1).transpose(1, 0, 2, 3).reshape(-1, model)

    def restored(values):
        return values.reshape(parts, rows_here, MINI, -1).transpose(1, 0, 2, 3).reshape(rows_here, stretch, -1)

    real = jnp.min(doc_starts) >= 0

    def apart(part, *operands):
        shapes = jax.eval_shape(part, *operands)
        blank = lambda *_: jax.tree.map(lambda s: jnp.zeros(s.shape, s.dtype), shapes)
        return lax.cond(real, part, blank, *operands)

    vectors = jnp.stack(
        [attn_gain, ffn_gain, init_bias, inner_gain, inner_shift, post_gain, post_shift], axis=1
    )
    small = jnp.concatenate([init_weight, rate_weight, vectors], axis=1)
    small = jnp.pad(small, ((0, 0), (0, -small.shape[1] % 128)))
    hidden, cotangent = reordered(hidden_in), reordered(out_grad)
    if aligned:
        out_own = lax.all_gather(out_weight, "rows", axis=0, tiled=True)
    else:
        out_own = own_part(lax.all_gather(out_weight, everywhere, axis=0, tiled=True))
    mixer_cut = shuffled(
        cut_heads((query_weight, key_weight, value_weight, gate_weight), groups, seq_count, span)
    )
    mixer_cut, hidden, cotangent, small, ffn_gate_weight, ffn_up_weight = lax.optimization_barrier(
        (mixer_cut, hidden, cotangent, small, ffn_gate_weight, ffn_up_weight)
    )
    mixer_weight = lax.all_gather(mixer_cut, "rows", axis=0, tiled=True)
    ffn_cut = cut_heads((ffn_gate_weight, ffn_up_weight), rows_count, seq_count, unit_share)

    def gather_inputs(hidden, cotangent, small, ffn_cut):
        hidden_all = gather_blocks(hidden, seq_bits).reshape(-1, model)
        cot_all = gather_blocks(cotangent, seq_bits).reshape(-1, model)
        small = gather_natural(small, row_bits).reshape(rows_count, share, -1)
        small = small.transpose(1, 0, 2).reshape(share, -1)
        small = gather_natural(small, seq_bits).reshape(seq_count, share, rows_count, -1)
        small = small.transpose(2, 0, 1, 3).reshape(model, -1)
        return hidden_all, cot_all, small, shuffled(ffn_cut)

    hidden_all, cot_all, small, ffn_cut = apart(gather_inputs, hidden, cotangent, small, ffn_cut)
    ffn_wide = lax.all_gather(ffn_cut, "rows", axis=0, tiled=True)

    gain_attn = small[:, head_dim + head_count].astype(F32)
    gain_ffn = small[:, head_dim + head_count + 1].astype(F32)
    own_small = own_part(small)
    own_vectors = own_small[:, head_dim + head_count :].astype(F32)
    rate_all = small[:, head_dim : head_dim + head_count].reshape(model, groups, seq_count, -1)
    rate_own = lax.dynamic_index_in_dim(rate_all, me, 2, keepdims=False).reshape(model, heads)
    lanes = heads * rows_here * MINI

    def by_lane(values, repeat):
        turned = values.reshape(heads, head_dim).T
        return jnp.broadcast_to(turned[:, :, None], (head_dim, heads, repeat)).reshape(head_dim, -1)

    bias_lanes = by_lane(own_vectors[:, 2], rows_here * MINI)
    gain_lanes = by_lane(own_vectors[:, 3], rows_here * MINI)
    shift_lanes = by_lane(own_vectors[:, 4], rows_here * MINI)
    post_scale, post_offset = own_vectors[:, 5], own_vectors[:, 6]
    start = own_small[:, :head_dim].astype(F32).reshape(heads, head_dim, head_dim).transpose(2, 0, 1)
    start = jnp.broadcast_to(start[:, :, None], (head_dim, heads, rows_here, head_dim)).reshape(head_dim, -1)

    steps = seq_count
    position = jnp.arange(steps * parts, dtype=jnp.int32) * MINI
    restarts = jnp.logical_or(
        position[:, None] == 0, jnp.any(doc_starts[None] == position[:, None, None], axis=2)
    ).astype(F32)

    def by_chain(repeat):
        wide = jnp.broadcast_to(
            restarts[:, None, :, None], (steps * parts, heads, rows_here, repeat)
        )
        return wide.reshape(steps, parts, -1)

    again, again_wide = by_chain(MINI), by_chain(head_dim)

    order = jnp.arange(steps, dtype=jnp.int32)
    slots = place(order, me, steps)
    blocks = jnp.bitwise_xor(order % (steps // 2) * 2 + order // (steps // 2), me)

    tokens_all = hidden_all.astype(F32)
    inverse_all = lax.rsqrt(jnp.mean(tokens_all * tokens_all, axis=-1, keepdims=True) + EPSILON)
    plain_all = tokens_all * inverse_all
    normed = (plain_all * gain_attn).astype(BF16)


    def project(matrix):
        return jnp.dot(normed, matrix, preferred_element_type=F32)

    qkv = project(mixer_weight[:, : 3 * width])
    qkv, ffn_down_weight = lax.optimization_barrier((qkv, ffn_down_weight))
    down_wide = lax.all_gather(ffn_down_weight, "rows", axis=0, tiled=True)
    queries, keys, values = (qkv[:, n * width : (n + 1) * width] for n in range(3))
    gate_pre = project(mixer_weight[:, 3 * width :])
    logits = project(rate_own)
    slope = jax.nn.sigmoid(logits)

    def to_lanes(per_token):
        ordered = jnp.take(per_token.reshape(steps, -1, heads), slots, axis=0)
        ordered = ordered.reshape(steps, parts, rows_here * MINI, heads)
        return ordered.transpose(0, 1, 3, 2).reshape(steps, parts, lanes)

    def from_lanes(per_lane):
        ordered = per_lane.reshape(steps, parts, heads, rows_here * MINI).transpose(0, 1, 3, 2)
        return jnp.take(ordered.reshape(steps, -1, heads), blocks, axis=0).reshape(-1, heads)

    rates = to_lanes(slope * (BASE_RATE / head_dim))
    slot = me.astype(jnp.int32).reshape(1)

    inner_out, *saved = inner_forward(
        slot, queries, keys, values, rates, again, again_wide, start, bias_lanes, gain_lanes,
        shift_lanes, heads, head_dim, parts,
    )

    def feature_mean(*arrays):
        sums = jnp.stack([jnp.sum(v, axis=1) for v in arrays]).reshape(len(arrays), steps, -1)
        total = lax.psum(jnp.take(sums, slots, axis=1), "seq") / model
        return jnp.take(total, blocks, axis=1).reshape(len(arrays), -1, 1)

    moments = feature_mean(inner_out, inner_out * inner_out)
    post_mean = moments[0]
    post_inverse = lax.rsqrt(moments[1] - post_mean * post_mean + EPSILON)
    post_norm = (inner_out - post_mean) * post_inverse
    post_out = post_norm * post_scale + post_offset
    gelu_value, gelu_pull = jax.vjp(gelu_tanh, gate_pre)
    gated = (gelu_value * post_out).astype(BF16)

    def reduced(left, matrix, dims, bits):
        half = left.shape[0] // 2
        away = lax.dot_general(left[half:], matrix, dims, preferred_element_type=F32).astype(BF16)
        own = lax.dot_general(left[:half], matrix, dims, preferred_element_type=F32)
        return reduce_blocks(
            own.reshape(-1, local, model), away.reshape(-1, local, model), bits
        )

    def rms_inverse(values):
        return lax.rsqrt(jnp.mean(values * values, axis=-1, keepdims=True) + EPSILON)

    def into_ffn(gated, out_own, hidden, gain_ffn):
        residual = hidden.astype(F32) + reduced(gated, out_own, NN, seq_bits)
        scaled = (residual * rms_inverse(residual) * gain_ffn).astype(BF16)
        return residual, gather_blocks(scaled, seq_bits).reshape(-1, model)

    residual, ffn_in = apart(into_ffn, gated, out_own, hidden, gain_ffn)
    gate_up = jnp.dot(ffn_in, ffn_wide, preferred_element_type=F32)
    gate_value, up_value = gate_up[:, :units], gate_up[:, units:]
    sigmoid_gate = jax.nn.sigmoid(gate_value)
    active = (gate_value * sigmoid_gate * up_value).astype(BF16)

    def token_grad(left, right):
        return lax.dot_general(left, right, TN, preferred_element_type=F32)

    grad_down = token_grad(active, cot_all).astype(BF16).reshape(rows_count, unit_share, model)
    grad_down = jnp.pad(grad_down, ((0, 0), (0, spare), (0, 0))).reshape(-1, model)
    grad_down, down_wide = lax.optimization_barrier((grad_down, down_wide))
    grad_down = lax.psum_scatter(grad_down, "rows", scatter_dimension=0, tiled=True)
    grad_down = grad_down[:unit_share].astype(F32)
    delta_active = lax.dot_general(cot_all, down_wide, NT, preferred_element_type=F32)
    delta_up = (delta_active * gate_value * sigmoid_gate).astype(BF16)
    delta_gate = (
        delta_active * up_value * sigmoid_gate * (1.0 + gate_value * (1.0 - sigmoid_gate))
    ).astype(BF16)
    delta_both = jnp.concatenate([delta_gate, delta_up], axis=1)

    def out_of_ffn(delta_both, ffn_wide, active, down_wide, residual, gain_ffn, cotangent):
        delta_ffn = reduced(delta_both, ffn_wide, NT, seq_bits)
        inverse_two = rms_inverse(residual)
        grad_gain_ffn = jnp.sum(delta_ffn * residual * inverse_two, axis=0)
        scaled_two = delta_ffn * gain_ffn
        delta_after = (
            cotangent.astype(F32)
            + inverse_two * scaled_two
            - residual * inverse_two**3 * jnp.mean(scaled_two * residual, axis=-1, keepdims=True)
        )
        delta_branch = gather_blocks(delta_after.astype(BF16), seq_bits).reshape(-1, model)
        block_out = residual + reduced(active, down_wide, NN, seq_bits)
        return grad_gain_ffn, delta_after, delta_branch, block_out

    grad_ffn = token_grad(ffn_in, delta_both).astype(BF16)
    delta_both, grad_ffn = lax.optimization_barrier((delta_both, grad_ffn))
    ffn_sums = row_sums(grad_ffn)
    grad_gain_ffn, delta_after, delta_branch, block_out = apart(
        out_of_ffn, delta_both, ffn_wide, active, down_wide, residual, gain_ffn, cotangent
    )

    grad_out = token_grad(gated, delta_branch).astype(BF16)
    delta_gated = lax.dot_general(delta_branch, out_own, NT, preferred_element_type=F32)
    delta_pre = gelu_pull(delta_gated * post_out)[0].astype(BF16)
    grad_gate_weight = token_grad(normed, delta_pre).astype(BF16)
    delta_gated, grad_out, grad_gate_weight = lax.optimization_barrier(
        (delta_gated, grad_out, grad_gate_weight)
    )
    gate_sums = row_sums(grad_gate_weight)
    delta_post = delta_gated * gelu_value
    grad_post_scale = jnp.sum(delta_post * post_norm, axis=0)
    grad_post_shift = jnp.sum(delta_post, axis=0)
    delta_norm = delta_post * post_scale
    means = feature_mean(delta_norm, delta_norm * post_norm)
    delta_inner = (delta_norm - means[0] - post_norm * means[1]) * post_inverse

    delta_inner, ffn_sums, grad_down = lax.optimization_barrier((delta_inner, ffn_sums, grad_down))
    (
        delta_queries, delta_keys, delta_values, delta_rates,
        grad_start, grad_bias, grad_inner_gain, grad_inner_shift,
    ) = inner_backward(
        slot, queries, keys, values, delta_inner, rates, again, again_wide, gain_lanes, shift_lanes,
        saved, heads, head_dim, parts,
    )
    delta_logits = (
        from_lanes(delta_rates) * slope * (1.0 - slope) * (BASE_RATE / head_dim)
    ).astype(BF16)
    delta_qkv = jnp.concatenate([delta_queries, delta_keys, delta_values], axis=1)
    delta_qkv, gate_sums = lax.optimization_barrier((delta_qkv, gate_sums))
    grad_qkv = token_grad(normed, delta_qkv).astype(BF16)
    delta_qkv, delta_logits, grad_qkv = lax.optimization_barrier((delta_qkv, delta_logits, grad_qkv))
    qkv_sums = row_sums(grad_qkv)
    grad_rate = token_grad(normed, delta_logits)
    grad_rate, grad_out = lax.optimization_barrier((grad_rate, grad_out))
    if aligned:
        grad_out = lax.psum_scatter(grad_out, "rows", scatter_dimension=0, tiled=True)
    else:
        grad_out = lax.psum_scatter(placed(grad_out), everywhere, scatter_dimension=0, tiled=True)

    def back_project(delta, matrix):
        return lax.dot_general(delta, matrix, NT, preferred_element_type=F32)

    def lane_sum(per_lane, repeat):
        return per_lane.reshape(head_dim, heads, repeat).sum(axis=2).T.reshape(width, 1)

    grad_start = grad_start.reshape(head_dim, heads, rows_here, head_dim).sum(axis=2)
    grad_start = grad_start.transpose(1, 2, 0).reshape(width, head_dim)
    grad_bias = grad_bias.reshape(head_dim, heads, rows_here, MINI)[..., 0]
    grad_rate = grad_rate.reshape(model, groups, 1, -1)
    here = (jnp.arange(seq_count) == me).reshape(1, 1, -1, 1)
    grad_rate = jnp.where(here, grad_rate, 0.0).reshape(model, head_count)
    own_grads = jnp.concatenate(
        [
            grad_start,
            lane_sum(grad_bias, rows_here),
            lane_sum(grad_inner_gain, rows_here * MINI),
            lane_sum(grad_inner_shift, rows_here * MINI),
            grad_post_scale[:, None],
            grad_post_shift[:, None],
        ],
        axis=1,
    )
    small_grads = jnp.concatenate([placed(own_grads), grad_rate, grad_gain_ffn[:, None]], axis=1)

    def out_of_mixer(
        delta_mixer, mixer_weight, delta_logits, rate_own, plain_all, hidden, delta_after, gain_attn,
        small_grads, ffn_sums, gate_sums,
    ):
        delta_normed = back_project(delta_mixer, mixer_weight) + back_project(delta_logits, rate_own)
        grad_gain_attn = jnp.sum(delta_normed * plain_all, axis=0)
        small_grads = jnp.concatenate([small_grads, grad_gain_attn[:, None]], axis=1)
        small_grads = jnp.pad(small_grads, ((0, 0), (0, -small_grads.shape[1] % 128)))
        small_grads = small_grads.reshape(rows_count, seq_count, share, -1)
        for axis, bit in reversed(seq_bits):
            small_grads = halved(small_grads, 1, axis, bit)
        for axis, bit in reversed(row_bits):
            small_grads = halved(small_grads, 0, axis, bit)
        small_grads = small_grads.reshape(share, -1)
        grad_gate, grad_up = join_heads(
            columns_out(ffn_sums), 2, rows_count, seq_count, unit_share
        )
        grad_gate_weight, = join_heads(columns_out(gate_sums), 1, groups, seq_count, span)
        delta_normed = delta_normed.reshape(2, -1, local, model)
        delta_normed = reduce_blocks(delta_normed[0], delta_normed[1], seq_bits)
        tokens = hidden.astype(F32)
        inverse_one = rms_inverse(tokens)
        scaled_one = delta_normed * gain_attn
        hidden_grad = (
            delta_after
            + inverse_one * scaled_one
            - tokens * inverse_one**3 * jnp.mean(scaled_one * tokens, axis=-1, keepdims=True)
        )
        return hidden_grad, small_grads, grad_gate, grad_up, grad_gate_weight

    hidden_grad, small_grads, grad_gate, grad_up, grad_gate_weight = apart(
        out_of_mixer, jnp.concatenate([delta_qkv, delta_pre], axis=1), mixer_weight, delta_logits,
        rate_own, plain_all, hidden, delta_after, gain_attn, small_grads, ffn_sums, gate_sums,
    )
    grad_query, grad_key, grad_value = join_heads(
        columns_out(qkv_sums), 3, groups, seq_count, span
    )
    after = head_dim + 5
    return (
        restored(block_out).astype(BF16),
        restored(hidden_grad),
        small_grads[:, after + head_count + 1],
        grad_query,
        grad_key,
        grad_value,
        small_grads[:, after : after + head_count],
        grad_gate_weight,
        small_grads[:, :head_dim],
        small_grads[:, head_dim],
        small_grads[:, head_dim + 1],
        small_grads[:, head_dim + 2],
        small_grads[:, head_dim + 3],
        small_grads[:, head_dim + 4],
        grad_out.astype(F32),
        small_grads[:, after + head_count],
        grad_gate,
        grad_up,
        grad_down,
    )


def solution(mesh):
    split = P(("rows", "seq"))
    matrix = P(("rows", "seq"), None)
    tokens = P("rows", "seq", None)
    return jax.shard_map(
        shards,
        mesh=mesh,
        in_specs=(
            tokens, split, matrix, matrix, matrix, matrix, matrix, matrix, split, split, split, split,
            split, matrix, split, matrix, matrix, matrix, P("rows", None), tokens,
        ),
        out_specs=(
            tokens, tokens, split, matrix, matrix, matrix, matrix, matrix, matrix, split, split, split,
            split, split, matrix, split, matrix, matrix, matrix,
        ),
        check_vma=False,
    )
```

```python
import functools
import jax
import jax.numpy as jnp
from jax import lax
from jax.experimental import pallas as pl
from jax.experimental.pallas import tpu as pltpu
from jax.sharding import PartitionSpec as P

MINI = 16
EPSILON = 1e-06
BASE_RATE = 1.0
GELU_SCALE = (2.0 / 3.141592653589793) ** 0.5
GELU_CUBE = 0.044715
F32 = jnp.float32
BF16 = jnp.bfloat16
NN = (((1,), (0,)), ((), ()))
NT = (((1,), (1,)), ((), ()))
TN = (((0,), (0,)), ((), ()))


def mm(left, right, dims):
    return lax.dot_general(left, right, dims, preferred_element_type=F32)


def packed(block, heads, head_dim, parts):
    turned = block.T
    width = block.shape[0] // parts
    return [
        jnp.concatenate(
            [
                turned[h * head_dim : (h + 1) * head_dim, j * width : (j + 1) * width]
                for h in range(heads)
            ],
            axis=1,
        )
        for j in range(parts)
    ]


def unpacked(pieces, heads):
    width = pieces[0].shape[1] // heads
    turned = jnp.concatenate(
        [
            jnp.concatenate([piece[:, h * width : (h + 1) * width] for piece in pieces], axis=1)
            for h in range(heads)
        ],
        axis=0,
    )
    return turned.T


def mean0(values):
    return jnp.mean(values, axis=0, keepdims=True)


def masks(chains, head_dim, dtype):
    lanes = chains * MINI
    rows = lax.broadcasted_iota(jnp.int32, (chains * head_dim, lanes), 0) // head_dim
    cols = lax.broadcasted_iota(jnp.int32, (chains * head_dim, lanes), 1) // MINI
    spread = rows == cols
    source = lax.broadcasted_iota(jnp.int32, (lanes, lanes), 0)
    target = lax.broadcasted_iota(jnp.int32, (lanes, lanes), 1)
    together = (source // MINI) == (target // MINI)
    earlier = jnp.logical_and(together, source <= target)
    scale = jnp.where(earlier, 1.0 / ((target % MINI) + 1).astype(F32), 0.0)
    return spread, together, scale


def spread_out(values, spread, chains):
    return jnp.where(spread, jnp.concatenate([values] * chains, axis=0), jnp.zeros((), values.dtype))


def forward_kernel(
    heads, head_dim, parts,
    slot_ref, queries_ref, keys_ref, values_ref, rate_ref, again_ref, again_wide_ref,
    start_ref, start_bias_ref, gain_ref, shift_ref,
    out_ref, sums_ref, normed_ref, spread_ref, grad_ref, rebuilt_ref, respread_ref, mix_ref, weight_ref,
    state, bias,
):
    chains = rate_ref.shape[-1] // MINI
    spread, together, scale = masks(chains, head_dim, BF16)
    ones = jnp.where(together, 1.0 / MINI, 0.0).astype(BF16)
    gain, shift = gain_ref[...], shift_ref[...]

    @pl.when(pl.program_id(0) == 0)
    def _():
        state[...] = jnp.zeros_like(state)
        bias[...] = jnp.zeros_like(bias)

    all_queries = packed(queries_ref[...], heads, head_dim, parts)
    all_keys = packed(keys_ref[...], heads, head_dim, parts)
    all_values = packed(values_ref[...], heads, head_dim, parts)
    weight = state[...]
    offset = bias[...]
    results = []
    for j in range(parts):
        query, key, value = all_queries[j], all_keys[j], all_values[j]
        rate = rate_ref[0, j : j + 1, :]
        low_key, low_query = key.astype(BF16), query.astype(BF16)
        wide_key = spread_out(low_key, spread, chains)
        wide_query = spread_out(low_query, spread, chains)
        mix = ((mm(low_key, low_query, TN) + 1.0) * scale).astype(BF16)
        weight = jnp.where(again_wide_ref[0, j : j + 1, :] > 0.0, start_ref[...], weight)
        offset = jnp.where(again_ref[0, j : j + 1, :] > 0.0, start_bias_ref[...], offset)
        low_weight = weight.astype(BF16)
        first = mm(low_weight, wide_key, NN) + offset
        center = first - mean0(first)
        inverse = lax.rsqrt(mean0(center * center) + EPSILON)
        normed = center * inverse
        residue = (normed * gain + shift - (value - key)) * gain
        inner = (residue - mean0(residue) - normed * mean0(residue * normed)) * inverse
        rated = (inner * rate).astype(BF16)
        combined = mm(low_weight, wide_query, NN) + offset - mm(rated, mix, NN)
        centered = combined - mean0(combined)
        inverse_out = lax.rsqrt(mean0(centered * centered) + EPSILON)
        rebuilt = centered * inverse_out
        results.append(query + rebuilt * gain + shift)
        weight = weight - mm(rated, wide_key, NT) * (1.0 / MINI)
        offset = offset - mm(rated, ones, NN)
        normed_ref[0, j] = normed
        grad_ref[0, j] = inner
        rebuilt_ref[0, j] = rebuilt
        spread_ref[0, j : j + 1, :] = inverse
        respread_ref[0, j : j + 1, :] = inverse_out
        mix_ref[0, j] = mix
        weight_ref[0, j] = low_weight
    out = unpacked(results, heads)
    out_ref[...] = out
    sums_ref[:, 0:1] = jnp.sum(out, axis=1, keepdims=True)
    sums_ref[:, 1:2] = jnp.sum(out * out, axis=1, keepdims=True)
    state[...] = weight
    bias[...] = offset


def gathered_back(wide, lane_chain, head_dim, chains):
    total = wide[:head_dim]
    for c in range(1, chains):
        total = jnp.where(lane_chain == c, wide[c * head_dim : (c + 1) * head_dim], total)
    return total


def backward_kernel(
    heads, head_dim, parts,
    slot_ref, queries_ref, keys_ref, values_ref, pre_ref, post_ref, out_ref, token_ref,
    rate_ref, again_ref, again_wide_ref, gain_ref, shift_ref,
    normed_ref, spread_ref, grad_ref, rebuilt_ref, respread_ref, mix_ref, weight_ref,
    inputs_ref, all_ref, dstart_ref, dstart_bias_ref, dgain_ref, dshift_ref,
    state, bias,
):
    chains = rate_ref.shape[-1] // MINI
    lanes = chains * MINI
    spread, together, scale = masks(chains, head_dim, BF16)
    ones = jnp.where(together, 1.0, 0.0).astype(BF16)
    lane_chain = lax.broadcasted_iota(jnp.int32, (head_dim, lanes), 1) // MINI
    gain, shift = gain_ref[...], shift_ref[...]

    @pl.when(pl.program_id(0) == 0)
    def _():
        state[...] = jnp.zeros_like(state)
        bias[...] = jnp.zeros_like(bias)
        dstart_ref[...] = jnp.zeros_like(dstart_ref)
        dstart_bias_ref[...] = jnp.zeros_like(dstart_bias_ref)
        dgain_ref[...] = jnp.zeros_like(dgain_ref)
        dshift_ref[...] = jnp.zeros_like(dshift_ref)

    all_queries = packed(queries_ref[...], heads, head_dim, parts)
    all_keys = packed(keys_ref[...], heads, head_dim, parts)
    all_values = packed(values_ref[...], heads, head_dim, parts)
    center, inverse_all = token_ref[:, 0:1], token_ref[:, 1:2]
    along_post = (out_ref[...] - center) * inverse_all
    delta_post = (post_ref[...] - token_ref[:, 2:3] - along_post * token_ref[:, 3:4]) * inverse_all
    all_deltas = packed(delta_post, heads, head_dim, parts)
    dweight = state[...]
    doffset = bias[...]
    dstart, dstart_bias = dstart_ref[...], dstart_bias_ref[...]
    dgain, dshift = dgain_ref[...], dshift_ref[...]
    dqueries, dkeys, dvalues, dlogits = ([None] * parts for _ in range(4))
    for j in reversed(range(parts)):
        query, key, value, delta = all_queries[j], all_keys[j], all_values[j], all_deltas[j]
        rate = rate_ref[0, j : j + 1, :]
        normed, inner, rebuilt = normed_ref[0, j], grad_ref[0, j], rebuilt_ref[0, j]
        inverse, inverse_out = spread_ref[0, j : j + 1, :], respread_ref[0, j : j + 1, :]
        mix, weight = mix_ref[0, j], weight_ref[0, j]
        low_key, low_query = key.astype(BF16), query.astype(BF16)
        wide_key = spread_out(low_key, spread, chains)
        wide_query = spread_out(low_query, spread, chains)
        rated = (inner * rate).astype(BF16)
        dnorm = delta * gain
        dcombined = (dnorm - mean0(dnorm) - rebuilt * mean0(dnorm * rebuilt)) * inverse_out
        low_dcombined = dcombined.astype(BF16)
        drated = -mm(low_dcombined, mix, NT)
        dscore = (-mm(rated, low_dcombined, TN) * scale).astype(BF16)
        low_dweight = dweight.astype(BF16)
        drated = drated - (mm(low_dweight, wide_key, NN) + doffset) * (1.0 / MINI)
        dinner = drated * rate
        bent = rate * (1.0 - rate * (head_dim / BASE_RATE))
        dlogits[j] = jnp.sum(drated * inner, axis=0, keepdims=True) * bent
        scaled = dinner * inverse
        offset_residue = normed * gain + shift - (value - key)
        residue = offset_residue * gain
        along = mean0(scaled * normed)
        dresidue = scaled - mean0(scaled) - normed * along
        gained = dresidue * gain
        dnormed = gained * gain - scaled * mean0(residue * normed) - residue * along
        dfirst = (
            dnormed - mean0(dnormed) - normed * (mean0(dnormed * normed) + mean0(dinner * inner))
        ) * inverse
        low_dfirst = dfirst.astype(BF16)
        dvalues[j] = -gained
        back_key = gathered_back(mm(weight, low_dfirst, TN), lane_chain, head_dim, chains)
        back_query = gathered_back(mm(weight, low_dcombined, TN), lane_chain, head_dim, chains)
        back_state = gathered_back(mm(low_dweight, rated, TN), lane_chain, head_dim, chains)
        dkeys[j] = gained + back_key - back_state * (1.0 / MINI) + mm(low_query, dscore, NT)
        dqueries[j] = delta + back_query + mm(low_key, dscore, NN)
        dgain = dgain + delta * rebuilt + dresidue * offset_residue + gained * normed
        dshift = dshift + delta + gained
        dweight = dweight + mm(low_dfirst, wide_key, NT) + mm(low_dcombined, wide_query, NT)
        both = (dfirst + dcombined).astype(BF16)
        doffset = doffset + mm(both, ones, NN)
        again_wide = again_wide_ref[0, j : j + 1, :] > 0.0
        again = again_ref[0, j : j + 1, :] > 0.0
        dstart = dstart + jnp.where(again_wide, dweight, 0.0)
        dstart_bias = dstart_bias + jnp.where(again, doffset, 0.0)
        dweight = jnp.where(again_wide, 0.0, dweight)
        doffset = jnp.where(again, 0.0, doffset)
    width = heads * head_dim
    for n, pieces in enumerate((dqueries, dkeys, dvalues)):
        natural = unpacked(pieces, heads).astype(inputs_ref.dtype)
        inputs_ref[:, n * width : (n + 1) * width] = natural
        all_ref[:, n * width : (n + 1) * width] = natural
    all_ref[:, 3 * width : 4 * width] = pre_ref[...]
    natural = unpacked(dlogits, heads)
    spare = inputs_ref.shape[1] - 3 * width - heads
    if spare:
        natural = jnp.concatenate([natural, jnp.zeros((natural.shape[0], spare), F32)], axis=1)
    inputs_ref[:, 3 * width :] = natural.astype(inputs_ref.dtype)
    all_ref[:, 4 * width :] = natural.astype(all_ref.dtype)
    state[...] = dweight
    bias[...] = doffset
    dstart_ref[...] = dstart
    dstart_bias_ref[...] = dstart_bias
    dgain_ref[...] = dgain
    dshift_ref[...] = dshift


def whole(shape):
    return pl.BlockSpec(shape, lambda *_: (0,) * len(shape))


def place(step, own, count):
    apart = jnp.bitwise_xor(step, own)
    return jnp.bitwise_and(apart, 1) * (count // 2) + lax.shift_right_logical(apart, 1)


def inner_forward(slot, queries, keys, values, rates, again, again_wide, start, start_bias, gain, shift, heads, head_dim, parts):
    steps, _, lanes = rates.shape
    tokens = queries.shape[0] // steps
    wide = start.shape[1]
    at_slot = pl.BlockSpec((tokens, heads * head_dim), lambda i, s: (place(i, s[0], steps), 0))

    def stepped(*shape):
        return pl.BlockSpec((1,) + shape, lambda i, s: (i,) + (0,) * len(shape))

    saved = [
        ((parts, head_dim, lanes), F32), ((parts, lanes), F32), ((parts, head_dim, lanes), F32),
        ((parts, head_dim, lanes), F32), ((parts, lanes), F32),
        ((parts, lanes, lanes), BF16), ((parts, head_dim, wide), BF16),
    ]
    return pl.pallas_call(
        functools.partial(forward_kernel, heads, head_dim, parts),
        out_shape=[jax.ShapeDtypeStruct(queries.shape, F32), jax.ShapeDtypeStruct((steps * tokens, 2), F32)]
        + [jax.ShapeDtypeStruct((steps,) + shape, kind) for shape, kind in saved],
        grid_spec=pltpu.PrefetchScalarGridSpec(
            num_scalar_prefetch=1,
            grid=(steps,),
            in_specs=[at_slot] * 3
            + [stepped(parts, lanes), stepped(parts, lanes), stepped(parts, wide)]
            + [whole(start.shape), whole(start_bias.shape), whole(gain.shape), whole(shift.shape)],
            out_specs=[at_slot, pl.BlockSpec((tokens, 2), at_slot.index_map)]
            + [stepped(*shape) for shape, _ in saved],
            scratch_shapes=[pltpu.VMEM(start.shape, F32), pltpu.VMEM(start_bias.shape, F32)],
        ),
        compiler_params=pltpu.CompilerParams(
            dimension_semantics=("arbitrary",), vmem_limit_bytes=63 * 1024 * 1024
        ),
        name="inner_forward",
    )(slot, queries, keys, values, rates, again, again_wide, start, start_bias, gain, shift)


def inner_backward(slot, queries, keys, values, pre, deltas, outs, per_token, rates, again, again_wide, gain, shift, saved, heads, head_dim, parts):
    steps, _, lanes = rates.shape
    tokens = queries.shape[0] // steps
    wide = again_wide.shape[-1]
    inputs = 3 * heads * head_dim + heads + -heads % 16
    at_slot = pl.BlockSpec(
        (tokens, heads * head_dim), lambda i, s: (place(steps - 1 - i, s[0], steps), 0)
    )

    def stepped(*shape):
        return pl.BlockSpec((1,) + shape, lambda i, s: (steps - 1 - i,) + (0,) * len(shape))

    return pl.pallas_call(
        functools.partial(backward_kernel, heads, head_dim, parts),
        out_shape=[
            jax.ShapeDtypeStruct((steps * tokens, inputs), BF16),
            jax.ShapeDtypeStruct((steps * tokens, inputs + heads * head_dim), BF16),
            jax.ShapeDtypeStruct((head_dim, wide), F32),
            jax.ShapeDtypeStruct((head_dim, lanes), F32),
            jax.ShapeDtypeStruct((head_dim, lanes), F32),
            jax.ShapeDtypeStruct((head_dim, lanes), F32),
        ],
        grid_spec=pltpu.PrefetchScalarGridSpec(
            num_scalar_prefetch=1,
            grid=(steps,),
            in_specs=[at_slot] * 6
            + [pl.BlockSpec((tokens, per_token.shape[1]), at_slot.index_map)]
            + [stepped(parts, lanes), stepped(parts, lanes), stepped(parts, wide)]
            + [whole(gain.shape), whole(shift.shape)]
            + [stepped(*array.shape[1:]) for array in saved],
            out_specs=[
                pl.BlockSpec((tokens, inputs), at_slot.index_map),
                pl.BlockSpec((tokens, inputs + heads * head_dim), at_slot.index_map),
                whole((head_dim, wide)),
            ]
            + [whole((head_dim, lanes))] * 3,
            scratch_shapes=[pltpu.VMEM((head_dim, wide), F32), pltpu.VMEM((head_dim, lanes), F32)],
        ),
        compiler_params=pltpu.CompilerParams(
            dimension_semantics=("arbitrary",), vmem_limit_bytes=63 * 1024 * 1024
        ),
        name="inner_backward",
    )(slot, queries, keys, values, pre, deltas, outs, per_token, rates, again, again_wide, gain, shift, *saved)


def cut_kernel(seq_count, kinds, *refs):
    out_ref = refs[-1]
    for s in range(seq_count):
        pieces = []
        for ref, (groups, span, gap, rest) in zip(refs, kinds):
            rows = ref.shape[0]
            for g in range(groups):
                at = (g * seq_count + s) * span
                pieces.append(ref[:, at : at + span].astype(F32))
                if gap:
                    pieces.append(jnp.zeros((rows, gap), F32))
            if rest:
                pieces.append(jnp.zeros((rows, rest), F32))
        out_ref[s] = jnp.concatenate(pieces, axis=1).astype(out_ref.dtype)


def cut_columns(weights, kinds, seq_count):
    rows = weights[0].shape[0]
    columns = sum(groups * (span + gap) + rest for groups, span, gap, rest in kinds)
    return pl.pallas_call(
        functools.partial(cut_kernel, seq_count, kinds),
        out_shape=jax.ShapeDtypeStruct((seq_count, rows, columns), BF16),
        compiler_params=pltpu.CompilerParams(vmem_limit_bytes=40 * 1024 * 1024),
        name="cut_columns",
    )(*weights)


def join_kernel(seq_count, kinds, *refs):
    count = len(kinds)
    parts_ref, weights, grads, sums_ref = refs[0], refs[1 : 1 + count], refs[1 + count : -1], refs[-1]
    total = 0.0
    base = 0
    for weight, ref, (groups, span, gap, rest) in zip(weights, grads, kinds):
        pieces = []
        for g in range(groups):
            at = base + g * (span + gap)
            pieces += [parts_ref[s, :, at : at + span].astype(F32) for s in range(seq_count)]
        whole_row = jnp.concatenate(pieces, axis=1)
        ref[...] = whole_row
        total = total + jnp.sum(whole_row * weight[...].astype(F32), axis=1, keepdims=True)
        base += groups * (span + gap) + rest
    sums_ref[...] = total


def join_columns(parts, weights, kinds):
    return pl.pallas_call(
        functools.partial(join_kernel, parts.shape[0], kinds),
        out_shape=[jax.ShapeDtypeStruct(w.shape, F32) for w in weights]
        + [jax.ShapeDtypeStruct((parts.shape[1], 1), F32)],
        compiler_params=pltpu.CompilerParams(vmem_limit_bytes=40 * 1024 * 1024),
        name="join_columns",
    )(parts, *weights)


def branch_kernel(
    delta_ref, matrix_ref, pre_ref, out_ref, token_ref, scale_ref, offset_ref,
    dpre_ref, dnorm_ref, sums_ref, dscale_ref, doffset_ref,
):
    @pl.when(pl.program_id(0) == 0)
    def _():
        dscale_ref[...] = jnp.zeros_like(dscale_ref)
        doffset_ref[...] = jnp.zeros_like(doffset_ref)

    delta_gated = mm(delta_ref[...], matrix_ref[...], NT)
    scale = scale_ref[...]
    norm = (out_ref[...] - token_ref[:, 0:1]) * token_ref[:, 1:2]
    pre = pre_ref[...]
    square = pre * pre
    bend = jnp.tanh(GELU_SCALE * pre * (1.0 + GELU_CUBE * square))
    half = 0.5 * (1.0 + bend)
    slope = half + 0.5 * pre * (1.0 - bend * bend) * (GELU_SCALE * (1.0 + 3.0 * GELU_CUBE * square))
    dpre_ref[...] = (delta_gated * (norm * scale + offset_ref[...]) * slope).astype(dpre_ref.dtype)
    delta_post = delta_gated * (pre * half)
    dscale_ref[...] += jnp.sum(delta_post * norm, axis=0, keepdims=True)
    doffset_ref[...] += jnp.sum(delta_post, axis=0, keepdims=True)
    dnorm = delta_post * scale
    dnorm_ref[...] = dnorm
    sums_ref[:, 0:1] = jnp.sum(dnorm, axis=1, keepdims=True)
    sums_ref[:, 1:2] = jnp.sum(dnorm * norm, axis=1, keepdims=True)


def branch_backward(delta, matrix, pre, out, per_token, scale, offset, block):
    tokens, width = pre.shape

    def by_block(array):
        return pl.BlockSpec((block, array.shape[1]), lambda i: (i, 0))

    row = jax.ShapeDtypeStruct((1, width), F32)
    sums = jax.ShapeDtypeStruct((tokens, 2), F32)
    return pl.pallas_call(
        branch_kernel,
        grid=(tokens // block,),
        in_specs=[by_block(delta), whole(matrix.shape), by_block(pre), by_block(out), by_block(per_token)]
        + [whole((1, width))] * 2,
        out_shape=[jax.ShapeDtypeStruct(pre.shape, BF16), jax.ShapeDtypeStruct(pre.shape, F32), sums, row, row],
        out_specs=[by_block(pre), by_block(pre), by_block(sums), whole((1, width)), whole((1, width))],
        compiler_params=pltpu.CompilerParams(
            dimension_semantics=("arbitrary",), vmem_limit_bytes=63 * 1024 * 1024
        ),
        name="branch_backward",
    )(delta, matrix, pre, out, per_token, scale, offset)


def spread_kernel(delta_ref, weight_ref, rate_ref, out_ref):
    width = weight_ref.shape[1]
    total = mm(delta_ref[:, :width], weight_ref[...], NT)
    total = total + mm(delta_ref[:, width:], rate_ref[...], NT)
    out_ref[...] = total.astype(out_ref.dtype)


def spread_back(delta, first, tokens, weight, rate, kind, block):
    model = weight.shape[0]
    return pl.pallas_call(
        spread_kernel,
        grid=(model // block,),
        in_specs=[
            pl.BlockSpec((tokens, delta.shape[1]), lambda i: (first // tokens, 0)),
            pl.BlockSpec((block, weight.shape[1]), lambda i: (i, 0)),
            pl.BlockSpec((block, rate.shape[1]), lambda i: (i, 0)),
        ],
        out_specs=pl.BlockSpec((tokens, block), lambda i: (0, i)),
        out_shape=jax.ShapeDtypeStruct((tokens, model), kind),
        compiler_params=pltpu.CompilerParams(
            dimension_semantics=("arbitrary",), vmem_limit_bytes=40 * 1024 * 1024
        ),
        name="spread_back",
    )(delta, weight, rate)


def exchange(value, axis, bit):
    count = lax.axis_size(axis)
    return lax.ppermute(value, axis, [(i, i ^ bit) for i in range(count)])


def bits_of(axis):
    return [(axis, 1 << p) for p in range(lax.axis_size(axis).bit_length() - 1)]


def cuts_of(width, ways):
    unit = 128 if width >= 128 * ways else 1
    return [unit * (n * (width // unit) // ways) for n in range(ways)] + [width]


def gather_blocks(block, bits, tied=None):
    near, far = bits[0], bits[1:]
    ways = max(1, len(far))
    cuts = cuts_of(block.shape[-1], ways)
    held = [{0: block[:, cuts[way] : cuts[way + 1]]} for way in range(ways)]
    for step in range(len(far)):
        for way in range(ways):
            bit = (way + step) % len(far)
            keys = sorted(held[way])
            moved = exchange(jnp.stack([held[way][k] for k in keys]), *far[bit])
            for n, k in enumerate(keys):
                held[way][k | 1 << bit] = moved[n]
    half = jnp.concatenate([jnp.stack([h[k] for k in sorted(h)]) for h in held], axis=-1)
    if tied is not None:
        half, tied = lax.optimization_barrier((half, tied))
    whole = jnp.concatenate([half, exchange(half, *near)], axis=0)
    return whole if tied is None else (whole, tied)


def reduce_blocks(own, away, bits, kind=BF16):
    near, far = bits[0], bits[1:]
    ways = max(1, len(far))
    cuts = cuts_of(own.shape[-1], ways)
    half = own.astype(F32) + exchange(away.astype(kind), *near).astype(F32)
    held = [
        {k: half[k, :, cuts[way] : cuts[way + 1]] for k in range(half.shape[0])} for way in range(ways)
    ]
    for step in range(len(far)):
        for way in range(ways):
            bit = (way + step) % len(far)
            gone = sorted(k for k in held[way] if k >> bit & 1)
            moved = exchange(jnp.stack([held[way][k].astype(kind) for k in gone]), *far[bit])
            for n, k in enumerate(gone):
                held[way][k ^ 1 << bit] = held[way][k ^ 1 << bit] + moved[n].astype(F32)
                del held[way][k]
    return jnp.concatenate([h[0] for h in held], axis=-1)


def has_bit(axis, bit):
    return jnp.bitwise_and(lax.axis_index(axis), bit) > 0


def gather_natural(value, bits):
    for axis, bit in bits:
        other = exchange(value, axis, bit)
        high = has_bit(axis, bit)
        value = jnp.concatenate([jnp.where(high, other, value), jnp.where(high, value, other)], axis=0)
    return value


def halved(value, dim, axis, bit):
    half = value.shape[dim] // 2
    high = has_bit(axis, bit)
    low_half = lax.slice_in_dim(value, 0, half, axis=dim)
    high_half = lax.slice_in_dim(value, half, 2 * half, axis=dim)
    other = exchange(jnp.where(high, low_half, high_half), axis, bit)
    return jnp.where(high, high_half, low_half) + other


def gelu_tanh(values):
    return jax.nn.gelu(values, approximate=True)


def shards(
    hidden_in,
    attn_gain,
    query_weight,
    key_weight,
    value_weight,
    rate_weight,
    gate_weight,
    init_weight,
    init_bias,
    inner_gain,
    inner_shift,
    post_gain,
    post_shift,
    out_weight,
    ffn_gain,
    ffn_gate_weight,
    ffn_up_weight,
    ffn_down_weight,
    doc_starts,
    out_grad,
):
    rows_here, stretch, model = hidden_in.shape
    head_count = rate_weight.shape[1]
    head_dim = init_weight.shape[1]
    parts = stretch // MINI
    local = rows_here * stretch
    seq_count = lax.axis_size("seq")
    rows_count = lax.axis_size("rows")
    share = model // (seq_count * rows_count)
    unit_share = ffn_down_weight.shape[0]
    heads = head_count // seq_count
    width = heads * head_dim
    aligned = share % head_dim == 0
    groups, span = (rows_count, share) if aligned else (1, width)
    me = lax.axis_index("seq")
    everywhere = ("rows", "seq")
    seq_bits = bits_of("seq")
    row_bits = bits_of("rows")
    spare = -unit_share % 16
    head_kind = (groups, span, 0, 0)
    rate_kind = (groups, heads // groups, 0, -heads % 16)
    unit_kind = (rows_count, unit_share, spare, 0)
    units = rows_count * (unit_share + spare)

    def shuffled(values):
        return lax.all_to_all(values, "seq", 0, 0, tiled=True).reshape(-1, values.shape[-1])

    def row_sums(values):
        summed = lax.psum_scatter(values, "rows", scatter_dimension=0, tiled=True)
        return summed.reshape(seq_count, share, -1)

    def columns_out(values):
        return lax.all_to_all(values, "seq", 0, 0, tiled=True)

    def own_part(values):
        split = values.reshape(groups, seq_count, span, -1)
        return lax.dynamic_index_in_dim(split, me, 1, keepdims=False).reshape(width, -1)

    def placed(values):
        split = values.reshape(groups, 1, span, -1)
        here = (jnp.arange(seq_count) == me).reshape(1, -1, 1, 1)
        return jnp.where(here, split, 0.0).reshape(model, -1)

    def reordered(values):
        return values.reshape(rows_here, parts, MINI, -1).transpose(1, 0, 2, 3).reshape(-1, model)

    def restored(values):
        return values.reshape(parts, rows_here, MINI, -1).transpose(1, 0, 2, 3).reshape(rows_here, stretch, -1)

    real = jnp.min(doc_starts) >= 0

    def apart(part, *operands):
        shapes = jax.eval_shape(part, *operands)
        blank = lambda *_: jax.tree.map(lambda s: jnp.zeros(s.shape, s.dtype), shapes)
        return lax.cond(real, part, blank, *operands)

    vectors = jnp.stack(
        [attn_gain, ffn_gain, init_bias, inner_gain, inner_shift, post_gain, post_shift], axis=1
    )
    small = jnp.concatenate([init_weight, rate_weight, vectors], axis=1)
    small = jnp.pad(small, ((0, 0), (0, -small.shape[1] % 128)))
    hidden, cotangent = reordered(hidden_in), reordered(out_grad)
    if aligned:
        out_own = lax.all_gather(out_weight, "rows", axis=0, tiled=True)
    else:
        out_own = own_part(lax.all_gather(out_weight, everywhere, axis=0, tiled=True))
    mixer_cut = shuffled(
        cut_columns((query_weight, key_weight, value_weight, gate_weight), (head_kind,) * 4, seq_count)
    )
    mixer_cut, hidden, cotangent, small, ffn_gate_weight, ffn_up_weight = lax.optimization_barrier(
        (mixer_cut, hidden, cotangent, small, ffn_gate_weight, ffn_up_weight)
    )
    late_cut, out_own = lax.optimization_barrier((mixer_cut, out_own))
    mixer_weight = lax.all_gather(late_cut, "rows", axis=0, tiled=True)
    ffn_cut = cut_columns((ffn_gate_weight, ffn_up_weight), (unit_kind,) * 2, seq_count)

    def gather_inputs(hidden, cotangent, small, ffn_cut):
        hidden_all = gather_blocks(hidden, seq_bits).reshape(-1, model)
        cot_all = gather_blocks(cotangent, seq_bits).reshape(-1, model)
        small = gather_natural(small, row_bits).reshape(rows_count, share, -1)
        small = small.transpose(1, 0, 2).reshape(share, -1)
        small = gather_natural(small, seq_bits).reshape(seq_count, share, rows_count, -1)
        small = small.transpose(2, 0, 1, 3).reshape(model, -1)
        return hidden_all, cot_all, small, shuffled(ffn_cut)

    hidden_all, cot_all, small, ffn_cut = apart(gather_inputs, hidden, cotangent, small, ffn_cut)
    ffn_wide = lax.all_gather(ffn_cut, "rows", axis=0, tiled=True)

    gain_attn = small[:, head_dim + head_count].astype(F32)
    gain_ffn = small[:, head_dim + head_count + 1].astype(F32)
    own_small = own_part(small)
    own_vectors = own_small[:, head_dim + head_count :].astype(F32)
    rate_all = small[:, head_dim : head_dim + head_count].reshape(model, groups, seq_count, -1)
    rate_own = lax.dynamic_index_in_dim(rate_all, me, 2, keepdims=False).reshape(model, heads)
    lanes = heads * rows_here * MINI

    def by_lane(values, repeat):
        turned = values.reshape(heads, head_dim).T
        return jnp.broadcast_to(turned[:, :, None], (head_dim, heads, repeat)).reshape(head_dim, -1)

    bias_lanes = by_lane(own_vectors[:, 2], rows_here * MINI)
    gain_lanes = by_lane(own_vectors[:, 3], rows_here * MINI)
    shift_lanes = by_lane(own_vectors[:, 4], rows_here * MINI)
    post_scale, post_offset = own_vectors[:, 5], own_vectors[:, 6]
    start = own_small[:, :head_dim].astype(F32).reshape(heads, head_dim, head_dim).transpose(2, 0, 1)
    start = jnp.broadcast_to(start[:, :, None], (head_dim, heads, rows_here, head_dim)).reshape(head_dim, -1)

    steps = seq_count
    position = jnp.arange(steps * parts, dtype=jnp.int32) * MINI
    restarts = jnp.logical_or(
        position[:, None] == 0, jnp.any(doc_starts[None] == position[:, None, None], axis=2)
    ).astype(F32)

    def by_chain(repeat):
        wide = jnp.broadcast_to(
            restarts[:, None, :, None], (steps * parts, heads, rows_here, repeat)
        )
        return wide.reshape(steps, parts, -1)

    again, again_wide = by_chain(MINI), by_chain(head_dim)

    order = jnp.arange(steps, dtype=jnp.int32)
    slots = place(order, me, steps)
    blocks = jnp.bitwise_xor(order % (steps // 2) * 2 + order // (steps // 2), me)

    tokens_all = hidden_all.astype(F32)
    inverse_all = lax.rsqrt(jnp.mean(tokens_all * tokens_all, axis=-1, keepdims=True) + EPSILON)
    plain_all = tokens_all * inverse_all
    normed = (plain_all * gain_attn).astype(BF16)


    projected = jnp.dot(normed, mixer_weight, preferred_element_type=F32)
    projected, ffn_down_weight = lax.optimization_barrier((projected, ffn_down_weight))
    down_wide = lax.all_gather(
        jnp.pad(ffn_down_weight, ((0, spare), (0, 0))), "rows", axis=0, tiled=True
    )
    queries, keys, values, gate_pre = (projected[:, n * width : (n + 1) * width] for n in range(4))
    logits = jnp.dot(normed, rate_own, preferred_element_type=F32)

    def to_lanes(per_token):
        ordered = jnp.take(per_token.reshape(steps, -1, heads), slots, axis=0)
        ordered = ordered.reshape(steps, parts, rows_here * MINI, heads)
        return ordered.transpose(0, 1, 3, 2).reshape(steps, parts, lanes)

    rates = to_lanes(jax.nn.sigmoid(logits) * (BASE_RATE / head_dim))
    slot = me.astype(jnp.int32).reshape(1)

    inner_out, inner_sums, *saved = inner_forward(
        slot, queries, keys, values, rates, again, again_wide, start, bias_lanes, gain_lanes,
        shift_lanes, heads, head_dim, parts,
    )

    def feature_mean(sums):
        count = sums.shape[1]
        ordered = jnp.take(sums.T.reshape(count, steps, -1), slots, axis=1)
        total = lax.psum(ordered, "seq") / model
        return jnp.take(total, blocks, axis=1).reshape(count, -1, 1)

    moments = feature_mean(inner_sums)
    post_mean = moments[0]
    post_inverse = lax.rsqrt(moments[1] - post_mean * post_mean + EPSILON)
    post_norm = (inner_out - post_mean) * post_inverse
    post_out = post_norm * post_scale + post_offset
    gated = (gelu_tanh(gate_pre) * post_out).astype(BF16)

    def halves(left, matrix, dims):
        half = left.shape[0] // 2
        away = lax.dot_general(left[half:], matrix, dims, preferred_element_type=F32).astype(BF16)
        own = lax.dot_general(left[:half], matrix, dims, preferred_element_type=F32)
        return own.reshape(-1, local, model), away.reshape(-1, local, model)

    def rms_inverse(values):
        return lax.rsqrt(jnp.mean(values * values, axis=-1, keepdims=True) + EPSILON)

    def into_ffn(own, away, hidden, gain_ffn):
        residual = hidden.astype(F32) + reduce_blocks(own, away, seq_bits)
        scaled = (residual * rms_inverse(residual) * gain_ffn).astype(BF16)
        return residual, gather_blocks(scaled, seq_bits).reshape(-1, model)

    residual, ffn_in = apart(into_ffn, *halves(gated, out_own, NN), hidden, gain_ffn)
    gate_up = jnp.dot(ffn_in, ffn_wide, preferred_element_type=F32)
    gate_value, up_value = gate_up[:, :units], gate_up[:, units:]
    sigmoid_gate = jax.nn.sigmoid(gate_value)
    active = (gate_value * sigmoid_gate * up_value).astype(BF16)

    def token_grad(left, right):
        return lax.dot_general(left, right, TN, preferred_element_type=F32)

    grad_down = token_grad(active, cot_all).astype(BF16)
    grad_down, down_wide = lax.optimization_barrier((grad_down, down_wide))
    grad_down = lax.psum_scatter(grad_down, "rows", scatter_dimension=0, tiled=True)
    grad_down = grad_down[:unit_share].astype(F32)
    delta_active = lax.dot_general(cot_all, down_wide, NT, preferred_element_type=F32)
    delta_up = (delta_active * gate_value * sigmoid_gate).astype(BF16)
    delta_gate = (
        delta_active * up_value * sigmoid_gate * (1.0 + gate_value * (1.0 - sigmoid_gate))
    ).astype(BF16)
    delta_both = jnp.concatenate([delta_gate, delta_up], axis=1)

    def out_of_ffn(own, away, own_down, away_down, residual, gain_ffn, cotangent):
        delta_ffn = reduce_blocks(own, away, seq_bits)
        inverse_two = rms_inverse(residual)
        scaled_two = delta_ffn * gain_ffn
        delta_after = (
            cotangent.astype(F32)
            + inverse_two * scaled_two
            - residual * inverse_two**3 * jnp.mean(scaled_two * residual, axis=-1, keepdims=True)
        )
        delta_branch = gather_blocks(delta_after.astype(BF16), seq_bits).reshape(-1, model)
        block_out = restored(residual + reduce_blocks(own_down, away_down, seq_bits)).astype(BF16)
        return delta_after, delta_branch, block_out

    grad_ffn = token_grad(ffn_in, delta_both).astype(BF16)
    delta_both, grad_ffn = lax.optimization_barrier((delta_both, grad_ffn))
    ffn_sums = row_sums(grad_ffn)
    delta_after, delta_branch, block_out = apart(
        out_of_ffn, *halves(delta_both, ffn_wide, NT), *halves(active, down_wide, NN), residual, gain_ffn,
        cotangent,
    )

    delta_pre, delta_norm, norm_sums, grad_post_scale, grad_post_shift = branch_backward(
        delta_branch, out_own, gate_pre, inner_out, jnp.concatenate([post_mean, post_inverse], axis=1),
        post_scale[None], post_offset[None], local,
    )
    grad_gate_weight = token_grad(normed, delta_pre).astype(BF16)
    norm_sums, grad_gate_weight = lax.optimization_barrier((norm_sums, grad_gate_weight))
    means = feature_mean(norm_sums)
    grad_out = token_grad(gated, delta_branch).astype(BF16)
    per_token = jnp.concatenate([post_mean, post_inverse, means[0], means[1]], axis=1)

    per_token, grad_out, grad_gate_weight, ffn_sums, grad_down = lax.optimization_barrier(
        (per_token, grad_out, grad_gate_weight, ffn_sums, grad_down)
    )
    gate_sums = row_sums(grad_gate_weight)
    (
        delta_inputs, delta_all,
        grad_start, grad_bias, grad_inner_gain, grad_inner_shift,
    ) = inner_backward(
        slot, queries, keys, values, delta_pre, delta_norm, inner_out, per_token, rates, again, again_wide,
        gain_lanes, shift_lanes, saved, heads, head_dim, parts,
    )
    ffn_parts = columns_out(ffn_sums)
    delta_inputs, delta_all, ffn_parts = lax.optimization_barrier((delta_inputs, delta_all, ffn_parts))
    grad_inputs = token_grad(normed, delta_inputs).astype(BF16)
    delta_all, grad_inputs, grad_out = lax.optimization_barrier((delta_all, grad_inputs, grad_out))
    input_sums = row_sums(grad_inputs)
    if aligned:
        grad_out = lax.psum_scatter(grad_out, "rows", scatter_dimension=0, tiled=True).astype(F32)

    half = delta_all.shape[0] // 2
    rate_wide = jnp.pad(rate_own, ((0, 0), (0, -heads % 16)))
    away = spread_back(delta_all, half, half, mixer_weight, rate_wide, BF16, model // 4)
    own = spread_back(delta_all, 0, half, mixer_weight, rate_wide, F32, model // 4)
    away, own = away.reshape(-1, local, model), own.reshape(-1, local, model)

    def lane_sum(per_lane, repeat):
        return per_lane.reshape(head_dim, heads, repeat).sum(axis=2).T.reshape(width, 1)

    grad_start = grad_start.reshape(head_dim, heads, rows_here, head_dim).sum(axis=2)
    grad_start = grad_start.transpose(1, 2, 0).reshape(width, head_dim)
    grad_bias = grad_bias.reshape(head_dim, heads, rows_here, MINI)[..., 0]
    own_grads = jnp.concatenate(
        [
            grad_start,
            lane_sum(grad_bias, rows_here),
            lane_sum(grad_inner_gain, rows_here * MINI),
            lane_sum(grad_inner_shift, rows_here * MINI),
            grad_post_scale.T,
            grad_post_shift.T,
        ],
        axis=1,
    )
    if aligned:
        own_grads = jnp.pad(own_grads, ((0, 0), (0, -own_grads.shape[1] % 128)))
    else:
        own_grads = lax.psum_scatter(
            placed(jnp.concatenate([own_grads.astype(BF16), grad_out], axis=1)),
            everywhere, scatter_dimension=0, tiled=True,
        ).astype(F32)

    def out_of_mixer(own, away, hidden, delta_after, gain_attn, ffn_parts, gate_sums, own_grads):
        grad_gate, grad_up, ffn_products = join_columns(
            ffn_parts, (ffn_gate_weight, ffn_up_weight), (unit_kind,) * 2
        )
        grad_gate_weight, gate_products = join_columns(
            columns_out(gate_sums), (gate_weight,), (head_kind,)
        )
        delta_normed = reduce_blocks(own, away, seq_bits)
        if aligned:
            for axis, bit in reversed(row_bits):
                own_grads = halved(own_grads, 0, axis, bit)
        tokens = hidden.astype(F32)
        inverse_one = rms_inverse(tokens)
        scaled_one = delta_normed * gain_attn
        hidden_grad = (
            delta_after
            + inverse_one * scaled_one
            - tokens * inverse_one**3 * jnp.mean(scaled_one * tokens, axis=-1, keepdims=True)
        )
        return (
            restored(hidden_grad), grad_gate, grad_up, ffn_products, grad_gate_weight, gate_products,
            own_grads,
        )

    (
        hidden_grad, grad_gate, grad_up, ffn_products, grad_gate_weight, gate_products, own_grads
    ) = apart(
        out_of_mixer, own, away, hidden, delta_after, gain_attn, ffn_parts, gate_sums, own_grads
    )
    grad_query, grad_key, grad_value, grad_rate, input_products = join_columns(
        columns_out(input_sums), (query_weight, key_weight, value_weight, rate_weight),
        (head_kind,) * 3 + (rate_kind,),
    )
    grad_gain_attn = (input_products[:, 0] + gate_products[:, 0]) / attn_gain.astype(F32)
    grad_gain_ffn = ffn_products[:, 0] / ffn_gain.astype(F32)
    if not aligned:
        grad_out = own_grads[:, head_dim + 5 :]
    own_vectors_grads = list(own_grads[:, head_dim : head_dim + 5].T)
    return (
        block_out,
        hidden_grad,
        grad_gain_attn,
        grad_query,
        grad_key,
        grad_value,
        grad_rate,
        grad_gate_weight,
        own_grads[:, :head_dim],
        *own_vectors_grads,
        grad_out,
        grad_gain_ffn,
        grad_gate,
        grad_up,
        grad_down,
    )


def solution(mesh):
    split = P(("rows", "seq"))
    matrix = P(("rows", "seq"), None)
    tokens = P("rows", "seq", None)
    return jax.shard_map(
        shards,
        mesh=mesh,
        in_specs=(
            tokens, split, matrix, matrix, matrix, matrix, matrix, matrix, split, split, split, split,
            split, matrix, split, matrix, matrix, matrix, P("rows", None), tokens,
        ),
        out_specs=(
            tokens, tokens, split, matrix, matrix, matrix, matrix, matrix, matrix, split, split, split,
            split, split, matrix, split, matrix, matrix, matrix,
        ),
        check_vma=False,
    )
```

```python
import functools
import jax
import jax.numpy as jnp
from jax import lax
from jax.experimental import pallas as pl
from jax.experimental.pallas import tpu as pltpu
from jax.sharding import PartitionSpec as P

MINI = 16
EPSILON = 1e-06
BASE_RATE = 1.0
GELU_SCALE = (2.0 / 3.141592653589793) ** 0.5
GELU_CUBE = 0.044715
F32 = jnp.float32
BF16 = jnp.bfloat16
NN = (((1,), (0,)), ((), ()))
NT = (((1,), (1,)), ((), ()))
TN = (((0,), (0,)), ((), ()))


def mm(left, right, dims):
    return lax.dot_general(left, right, dims, preferred_element_type=F32)


def in_two(values):
    high = values.astype(BF16)
    return high, (values - high.astype(F32)).astype(BF16)


def mm_two(left, right, dims):
    return mm(left[0], right[0], dims) + (mm(left[1], right[0], dims) + mm(left[0], right[1], dims))


def packed(block, heads, head_dim, parts):
    turned = block.T
    width = block.shape[0] // parts
    return [
        jnp.concatenate(
            [
                turned[h * head_dim : (h + 1) * head_dim, j * width : (j + 1) * width]
                for h in range(heads)
            ],
            axis=1,
        )
        for j in range(parts)
    ]


def unpacked(pieces, heads):
    width = pieces[0].shape[1] // heads
    turned = jnp.concatenate(
        [
            jnp.concatenate([piece[:, h * width : (h + 1) * width] for piece in pieces], axis=1)
            for h in range(heads)
        ],
        axis=0,
    )
    return turned.T


def mean0(values):
    return jnp.mean(values, axis=0, keepdims=True)


def masks(chains, head_dim, dtype):
    lanes = chains * MINI
    rows = lax.broadcasted_iota(jnp.int32, (chains * head_dim, lanes), 0) // head_dim
    cols = lax.broadcasted_iota(jnp.int32, (chains * head_dim, lanes), 1) // MINI
    spread = rows == cols
    source = lax.broadcasted_iota(jnp.int32, (lanes, lanes), 0)
    target = lax.broadcasted_iota(jnp.int32, (lanes, lanes), 1)
    together = (source // MINI) == (target // MINI)
    earlier = jnp.logical_and(together, source <= target)
    scale = jnp.where(earlier, 1.0 / ((target % MINI) + 1).astype(F32), 0.0)
    return spread, together, scale


def spread_out(values, spread, chains):
    return jnp.where(spread, jnp.concatenate([values] * chains, axis=0), jnp.zeros((), values.dtype))


def forward_kernel(
    heads, head_dim, parts,
    slot_ref, inputs_ref, rate_ref, again_ref, again_wide_ref,
    start_ref, start_bias_ref, gain_ref, shift_ref,
    out_ref, sums_ref, kept_ref, spreads_ref, mix_ref, weight_ref,
    state, bias,
):
    chains = rate_ref.shape[-1] // MINI
    spread, together, scale = masks(chains, head_dim, BF16)
    ones = jnp.where(together, 1.0 / MINI, 0.0).astype(BF16)
    gain, shift = gain_ref[...], shift_ref[...]

    @pl.when(pl.program_id(0) == 0)
    def _():
        state[...] = jnp.zeros_like(state)
        bias[...] = jnp.zeros_like(bias)

    width = heads * head_dim
    all_queries, all_keys, all_values = (
        packed(inputs_ref[:, n * width : (n + 1) * width], heads, head_dim, parts) for n in range(3)
    )
    weight = state[...]
    offset = bias[...]
    results = []
    for j in range(parts):
        query, key, value = all_queries[j], all_keys[j], all_values[j]
        rate = rate_ref[0, j : j + 1, :]
        two_keys, two_queries = in_two(key), in_two(query)
        wide_keys = [spread_out(k, spread, chains) for k in two_keys]
        wide_both = [
            jnp.concatenate([k, spread_out(q, spread, chains)], axis=1)
            for k, q in zip(wide_keys, two_queries)
        ]
        mix = in_two((mm_two(two_keys, two_queries, TN) + 1.0) * scale)
        weight = jnp.where(again_wide_ref[0, j : j + 1, :] > 0.0, start_ref[...], weight)
        offset = jnp.where(again_ref[0, j : j + 1, :] > 0.0, start_bias_ref[...], offset)
        two_weights = in_two(weight)
        both = mm_two(two_weights, wide_both, NN)
        lanes = offset.shape[1]
        first = both[:, :lanes] + offset
        center = first - mean0(first)
        inverse = lax.rsqrt(mean0(center * center) + EPSILON)
        normed = center * inverse
        residue = (normed * gain + shift - (value - key)) * gain
        inner = (residue - mean0(residue) - normed * mean0(residue * normed)) * inverse
        rated = in_two(inner * rate)
        combined = both[:, lanes:] + offset - mm_two(rated, mix, NN)
        centered = combined - mean0(combined)
        inverse_out = lax.rsqrt(mean0(centered * centered) + EPSILON)
        rebuilt = centered * inverse_out
        results.append(query + rebuilt * gain + shift)
        weight = weight - mm_two(rated, wide_keys, NT) * (1.0 / MINI)
        offset = offset - (mm(rated[0], ones, NN) + mm(rated[1], ones, NN))
        kept_ref[0, 0, j] = normed
        kept_ref[0, 1, j] = inner
        kept_ref[0, 2, j] = rebuilt
        spreads_ref[0, j : j + 1, :] = inverse
        spreads_ref[0, parts + j : parts + j + 1, :] = inverse_out
        mix_ref[0, j] = mix[0]
        weight_ref[0, j] = two_weights[0]
    out = unpacked(results, heads)
    out_ref[...] = out
    sums_ref[:, 0:1] = jnp.sum(out, axis=1, keepdims=True)
    sums_ref[:, 1:2] = jnp.sum(out * out, axis=1, keepdims=True)
    state[...] = weight
    bias[...] = offset


def gathered_back(wide, lane_chain, head_dim, chains):
    total = wide[:head_dim]
    for c in range(1, chains):
        total = jnp.where(lane_chain == c, wide[c * head_dim : (c + 1) * head_dim], total)
    return total


def backward_kernel(
    heads, head_dim, parts,
    slot_ref, inputs_ref, pre_ref, post_ref, out_ref, token_ref,
    rate_ref, again_ref, again_wide_ref, gain_ref, shift_ref,
    kept_ref, spreads_ref, mix_ref, weight_ref,
    all_ref, logits_ref, dstart_ref, dstart_bias_ref, dgain_ref, dshift_ref,
    state, bias,
):
    chains = rate_ref.shape[-1] // MINI
    lanes = chains * MINI
    spread, together, scale = masks(chains, head_dim, BF16)
    ones = jnp.where(together, 1.0, 0.0).astype(BF16)
    lane_chain = lax.broadcasted_iota(jnp.int32, (head_dim, lanes), 1) // MINI
    gain, shift = gain_ref[...], shift_ref[...]

    @pl.when(pl.program_id(0) == 0)
    def _():
        state[...] = jnp.zeros_like(state)
        bias[...] = jnp.zeros_like(bias)
        dstart_ref[...] = jnp.zeros_like(dstart_ref)
        dstart_bias_ref[...] = jnp.zeros_like(dstart_bias_ref)
        dgain_ref[...] = jnp.zeros_like(dgain_ref)
        dshift_ref[...] = jnp.zeros_like(dshift_ref)

    width = heads * head_dim
    all_queries, all_keys, all_values = (
        packed(inputs_ref[:, n * width : (n + 1) * width], heads, head_dim, parts) for n in range(3)
    )
    center, inverse_all = token_ref[:, 0:1], token_ref[:, 1:2]
    along_post = (out_ref[...] - center) * inverse_all
    delta_post = (post_ref[...] - token_ref[:, 2:3] - along_post * token_ref[:, 3:4]) * inverse_all
    all_deltas = packed(delta_post, heads, head_dim, parts)
    dweight = state[...]
    doffset = bias[...]
    dstart, dstart_bias = dstart_ref[...], dstart_bias_ref[...]
    dgain, dshift = dgain_ref[...], dshift_ref[...]
    dqueries, dkeys, dvalues, dlogits = ([None] * parts for _ in range(4))
    for j in reversed(range(parts)):
        query, key, value, delta = all_queries[j], all_keys[j], all_values[j], all_deltas[j]
        rate = rate_ref[0, j : j + 1, :]
        normed, inner, rebuilt = (kept_ref[0, n, j] for n in range(3))
        inverse, inverse_out = (spreads_ref[0, n * parts + j : n * parts + j + 1, :] for n in range(2))
        mix, weight = mix_ref[0, j], weight_ref[0, j]
        low_key, low_query = key.astype(BF16), query.astype(BF16)
        wide_key = spread_out(low_key, spread, chains)
        wide_query = spread_out(low_query, spread, chains)
        rated = (inner * rate).astype(BF16)
        dnorm = delta * gain
        dcombined = (dnorm - mean0(dnorm) - rebuilt * mean0(dnorm * rebuilt)) * inverse_out
        low_dcombined = dcombined.astype(BF16)
        drated = -mm(low_dcombined, mix, NT)
        dscore = (-mm(rated, low_dcombined, TN) * scale).astype(BF16)
        low_dweight = dweight.astype(BF16)
        drated = drated - (mm(low_dweight, wide_key, NN) + doffset) * (1.0 / MINI)
        dinner = drated * rate
        bent = rate * (1.0 - rate * (head_dim / BASE_RATE))
        dlogits[j] = jnp.sum(drated * inner, axis=0, keepdims=True) * bent
        scaled = dinner * inverse
        offset_residue = normed * gain + shift - (value - key)
        residue = offset_residue * gain
        along = mean0(scaled * normed)
        dresidue = scaled - mean0(scaled) - normed * along
        gained = dresidue * gain
        dnormed = gained * gain - scaled * mean0(residue * normed) - residue * along
        dfirst = (
            dnormed - mean0(dnormed) - normed * (mean0(dnormed * normed) + mean0(dinner * inner))
        ) * inverse
        low_dfirst = dfirst.astype(BF16)
        dvalues[j] = -gained
        back_key = gathered_back(mm(weight, low_dfirst, TN), lane_chain, head_dim, chains)
        back_query = gathered_back(mm(weight, low_dcombined, TN), lane_chain, head_dim, chains)
        back_state = gathered_back(mm(low_dweight, rated, TN), lane_chain, head_dim, chains)
        dkeys[j] = gained + back_key - back_state * (1.0 / MINI) + mm(low_query, dscore, NT)
        dqueries[j] = delta + back_query + mm(low_key, dscore, NN)
        dgain = dgain + delta * rebuilt + dresidue * offset_residue + gained * normed
        dshift = dshift + delta + gained
        dweight = dweight + mm(low_dfirst, wide_key, NT) + mm(low_dcombined, wide_query, NT)
        both = (dfirst + dcombined).astype(BF16)
        doffset = doffset + mm(both, ones, NN)
        again_wide = again_wide_ref[0, j : j + 1, :] > 0.0
        again = again_ref[0, j : j + 1, :] > 0.0
        dstart = dstart + jnp.where(again_wide, dweight, 0.0)
        dstart_bias = dstart_bias + jnp.where(again, doffset, 0.0)
        dweight = jnp.where(again_wide, 0.0, dweight)
        doffset = jnp.where(again, 0.0, doffset)
    for n, pieces in enumerate((dqueries, dkeys, dvalues)):
        natural = unpacked(pieces, heads).astype(all_ref.dtype)
        all_ref[:, n * width : (n + 1) * width] = natural
    all_ref[:, 3 * width : 4 * width] = pre_ref[...]
    natural = unpacked(dlogits, heads)
    spare = logits_ref.shape[1] - heads
    if spare:
        natural = jnp.concatenate([natural, jnp.zeros((natural.shape[0], spare), F32)], axis=1)
    logits_ref[...] = natural.astype(logits_ref.dtype)
    state[...] = dweight
    bias[...] = doffset
    dstart_ref[...] = dstart
    dstart_bias_ref[...] = dstart_bias
    dgain_ref[...] = dgain
    dshift_ref[...] = dshift


def whole(shape):
    return pl.BlockSpec(shape, lambda *_: (0,) * len(shape))


def place(step, own, count):
    apart = jnp.bitwise_xor(step, own)
    return jnp.bitwise_and(apart, 1) * (count // 2) + lax.shift_right_logical(apart, 1)


def inner_forward(slot, projected, rates, again, again_wide, start, start_bias, gain, shift, heads, head_dim, parts):
    steps, _, lanes = rates.shape
    tokens = projected.shape[0] // steps
    wide = start.shape[1]
    at_slot = pl.BlockSpec((tokens, heads * head_dim), lambda i, s: (place(i, s[0], steps), 0))

    def stepped(*shape):
        return pl.BlockSpec((1,) + shape, lambda i, s: (i,) + (0,) * len(shape))

    saved = [
        ((3, parts, head_dim, lanes), F32), ((2 * parts, lanes), F32),
        ((parts, lanes, lanes), BF16), ((parts, head_dim, wide), BF16),
    ]
    return pl.pallas_call(
        functools.partial(forward_kernel, heads, head_dim, parts),
        out_shape=[jax.ShapeDtypeStruct((steps * tokens, heads * head_dim), F32), jax.ShapeDtypeStruct((steps * tokens, 2), F32)]
        + [jax.ShapeDtypeStruct((steps,) + shape, kind) for shape, kind in saved],
        grid_spec=pltpu.PrefetchScalarGridSpec(
            num_scalar_prefetch=1,
            grid=(steps,),
            in_specs=[pl.BlockSpec((tokens, 3 * heads * head_dim), at_slot.index_map)]
            + [stepped(parts, lanes), stepped(parts, lanes), stepped(parts, wide)]
            + [whole(start.shape), whole(start_bias.shape), whole(gain.shape), whole(shift.shape)],
            out_specs=[at_slot, pl.BlockSpec((tokens, 2), at_slot.index_map)]
            + [stepped(*shape) for shape, _ in saved],
            scratch_shapes=[pltpu.VMEM(start.shape, F32), pltpu.VMEM(start_bias.shape, F32)],
        ),
        compiler_params=pltpu.CompilerParams(
            dimension_semantics=("arbitrary",), vmem_limit_bytes=63 * 1024 * 1024
        ),
        name="inner_forward",
    )(slot, projected, rates, again, again_wide, start, start_bias, gain, shift)


def inner_backward(slot, projected, pre, deltas, outs, per_token, rates, again, again_wide, gain, shift, saved, heads, head_dim, parts):
    steps, _, lanes = rates.shape
    tokens = projected.shape[0] // steps
    wide = again_wide.shape[-1]
    inputs, logits = 4 * heads * head_dim, heads + -heads % 16
    at_slot = pl.BlockSpec(
        (tokens, heads * head_dim), lambda i, s: (place(steps - 1 - i, s[0], steps), 0)
    )

    def stepped(*shape):
        return pl.BlockSpec((1,) + shape, lambda i, s: (steps - 1 - i,) + (0,) * len(shape))

    return pl.pallas_call(
        functools.partial(backward_kernel, heads, head_dim, parts),
        out_shape=[
            jax.ShapeDtypeStruct((steps * tokens, inputs), BF16),
            jax.ShapeDtypeStruct((steps * tokens, logits), BF16),
            jax.ShapeDtypeStruct((head_dim, wide), F32),
            jax.ShapeDtypeStruct((head_dim, lanes), F32),
            jax.ShapeDtypeStruct((head_dim, lanes), F32),
            jax.ShapeDtypeStruct((head_dim, lanes), F32),
        ],
        grid_spec=pltpu.PrefetchScalarGridSpec(
            num_scalar_prefetch=1,
            grid=(steps,),
            in_specs=[pl.BlockSpec((tokens, 3 * heads * head_dim), at_slot.index_map)]
            + [at_slot] * 3
            + [pl.BlockSpec((tokens, per_token.shape[1]), at_slot.index_map)]
            + [stepped(parts, lanes), stepped(parts, lanes), stepped(parts, wide)]
            + [whole(gain.shape), whole(shift.shape)]
            + [stepped(*array.shape[1:]) for array in saved],
            out_specs=[
                pl.BlockSpec((tokens, inputs), at_slot.index_map),
                pl.BlockSpec((tokens, logits), at_slot.index_map),
                whole((head_dim, wide)),
            ]
            + [whole((head_dim, lanes))] * 3,
            scratch_shapes=[pltpu.VMEM((head_dim, wide), F32), pltpu.VMEM((head_dim, lanes), F32)],
        ),
        compiler_params=pltpu.CompilerParams(
            dimension_semantics=("arbitrary",), vmem_limit_bytes=63 * 1024 * 1024
        ),
        name="inner_backward",
    )(slot, projected, pre, deltas, outs, per_token, rates, again, again_wide, gain, shift, *saved)


def cut_kernel(seq_count, kinds, *refs):
    out_ref = refs[-1]
    for s in range(seq_count):
        pieces = []
        for ref, (groups, span, gap, rest) in zip(refs, kinds):
            rows = ref.shape[0]
            for g in range(groups):
                at = (g * seq_count + s) * span
                pieces.append(ref[:, at : at + span].astype(F32))
                if gap:
                    pieces.append(jnp.zeros((rows, gap), F32))
            if rest:
                pieces.append(jnp.zeros((rows, rest), F32))
        out_ref[s] = jnp.concatenate(pieces, axis=1).astype(out_ref.dtype)


def cut_columns(weights, kinds, seq_count):
    rows = weights[0].shape[0]
    columns = sum(groups * (span + gap) + rest for groups, span, gap, rest in kinds)
    return pl.pallas_call(
        functools.partial(cut_kernel, seq_count, kinds),
        out_shape=jax.ShapeDtypeStruct((seq_count, rows, columns), BF16),
        compiler_params=pltpu.CompilerParams(vmem_limit_bytes=40 * 1024 * 1024),
        name="cut_columns",
    )(*weights)


def join_kernel(seq_count, kinds, *refs):
    count = len(kinds)
    parts_ref, weights, grads, sums_ref = refs[0], refs[1 : 1 + count], refs[1 + count : -1], refs[-1]
    total = 0.0
    base = 0
    for weight, ref, (groups, span, gap, rest) in zip(weights, grads, kinds):
        pieces = []
        for g in range(groups):
            at = base + g * (span + gap)
            pieces += [parts_ref[s, :, at : at + span].astype(F32) for s in range(seq_count)]
        whole_row = jnp.concatenate(pieces, axis=1)
        ref[...] = whole_row
        total = total + jnp.sum(whole_row * weight[...].astype(F32), axis=1, keepdims=True)
        base += groups * (span + gap) + rest
    sums_ref[...] = total


def join_columns(parts, weights, kinds):
    return pl.pallas_call(
        functools.partial(join_kernel, parts.shape[0], kinds),
        out_shape=[jax.ShapeDtypeStruct(w.shape, F32) for w in weights]
        + [jax.ShapeDtypeStruct((parts.shape[1], 1), F32)],
        compiler_params=pltpu.CompilerParams(vmem_limit_bytes=40 * 1024 * 1024),
        name="join_columns",
    )(parts, *weights)


def branch_kernel(
    delta_ref, matrix_ref, pre_ref, out_ref, token_ref, scale_ref, offset_ref,
    dpre_ref, dnorm_ref, sums_ref, dscale_ref, doffset_ref,
):
    @pl.when(pl.program_id(0) == 0)
    def _():
        dscale_ref[...] = jnp.zeros_like(dscale_ref)
        doffset_ref[...] = jnp.zeros_like(doffset_ref)

    delta_gated = mm(delta_ref[...], matrix_ref[...], NT)
    scale = scale_ref[...]
    norm = (out_ref[...] - token_ref[:, 0:1]) * token_ref[:, 1:2]
    pre = pre_ref[...]
    square = pre * pre
    bend = jnp.tanh(GELU_SCALE * pre * (1.0 + GELU_CUBE * square))
    half = 0.5 * (1.0 + bend)
    slope = half + 0.5 * pre * (1.0 - bend * bend) * (GELU_SCALE * (1.0 + 3.0 * GELU_CUBE * square))
    dpre_ref[...] = (delta_gated * (norm * scale + offset_ref[...]) * slope).astype(dpre_ref.dtype)
    delta_post = delta_gated * (pre * half)
    dscale_ref[...] += jnp.sum(delta_post * norm, axis=0, keepdims=True)
    doffset_ref[...] += jnp.sum(delta_post, axis=0, keepdims=True)
    dnorm = delta_post * scale
    dnorm_ref[...] = dnorm
    sums_ref[:, 0:1] = jnp.sum(dnorm, axis=1, keepdims=True)
    sums_ref[:, 1:2] = jnp.sum(dnorm * norm, axis=1, keepdims=True)


def branch_backward(delta, matrix, projected, out, per_token, scale, offset, block):
    tokens, width = out.shape
    gate = pl.BlockSpec((block, width), lambda i: (i, 3))

    def by_block(array):
        return pl.BlockSpec((block, array.shape[1]), lambda i: (i, 0))

    row = jax.ShapeDtypeStruct((1, width), F32)
    sums = jax.ShapeDtypeStruct((tokens, 2), F32)
    return pl.pallas_call(
        branch_kernel,
        grid=(tokens // block,),
        in_specs=[by_block(delta), whole(matrix.shape), gate, by_block(out), by_block(per_token)]
        + [whole((1, width))] * 2,
        out_shape=[jax.ShapeDtypeStruct(out.shape, BF16), jax.ShapeDtypeStruct(out.shape, F32), sums, row, row],
        out_specs=[by_block(out), by_block(out), by_block(sums), whole((1, width)), whole((1, width))],
        compiler_params=pltpu.CompilerParams(
            dimension_semantics=("arbitrary",), vmem_limit_bytes=63 * 1024 * 1024
        ),
        name="branch_backward",
    )(delta, matrix, projected, out, per_token, scale, offset)


def spread_kernel(delta_ref, logits_ref, weight_ref, rate_ref, out_ref):
    total = mm(delta_ref[...], weight_ref[...], NT) + mm(logits_ref[...], rate_ref[...], NT)
    out_ref[...] = total.astype(out_ref.dtype)


def spread_back(delta, logits, first, tokens, weight, rate, kind, block):
    model = weight.shape[0]
    return pl.pallas_call(
        spread_kernel,
        grid=(model // block,),
        in_specs=[
            pl.BlockSpec((tokens, delta.shape[1]), lambda i: (first // tokens, 0)),
            pl.BlockSpec((tokens, logits.shape[1]), lambda i: (first // tokens, 0)),
            pl.BlockSpec((block, weight.shape[1]), lambda i: (i, 0)),
            pl.BlockSpec((block, rate.shape[1]), lambda i: (i, 0)),
        ],
        out_specs=pl.BlockSpec((tokens, block), lambda i: (0, i)),
        out_shape=jax.ShapeDtypeStruct((tokens, model), kind),
        compiler_params=pltpu.CompilerParams(
            dimension_semantics=("arbitrary",), vmem_limit_bytes=40 * 1024 * 1024
        ),
        name="spread_back",
    )(delta, logits, weight, rate)


def exchange(value, axis, bit):
    count = lax.axis_size(axis)
    return lax.ppermute(value, axis, [(i, i ^ bit) for i in range(count)])


def bits_of(axis):
    return [(axis, 1 << p) for p in range(lax.axis_size(axis).bit_length() - 1)]


def cuts_of(width, ways):
    unit = 128 if width >= 128 * ways else 1
    return [unit * (n * (width // unit) // ways) for n in range(ways)] + [width]


def gather_blocks(block, bits, tied=None):
    near, far = bits[0], bits[1:]
    ways = max(1, len(far))
    cuts = cuts_of(block.shape[-1], ways)
    held = [{0: block[:, cuts[way] : cuts[way + 1]]} for way in range(ways)]
    for step in range(len(far)):
        for way in range(ways):
            bit = (way + step) % len(far)
            keys = sorted(held[way])
            moved = exchange(jnp.stack([held[way][k] for k in keys]), *far[bit])
            for n, k in enumerate(keys):
                held[way][k | 1 << bit] = moved[n]
    half = jnp.concatenate([jnp.stack([h[k] for k in sorted(h)]) for h in held], axis=-1)
    if tied is not None:
        half, tied = lax.optimization_barrier((half, tied))
    whole = jnp.concatenate([half, exchange(half, *near)], axis=0)
    return whole if tied is None else (whole, tied)


def reduce_blocks(own, away, bits, kind=BF16):
    near, far = bits[0], bits[1:]
    ways = max(1, len(far))
    cuts = cuts_of(own.shape[-1], ways)
    half = own.astype(F32) + exchange(away.astype(kind), *near).astype(F32)
    held = [
        {k: half[k, :, cuts[way] : cuts[way + 1]] for k in range(half.shape[0])} for way in range(ways)
    ]
    for step in range(len(far)):
        for way in range(ways):
            bit = (way + step) % len(far)
            gone = sorted(k for k in held[way] if k >> bit & 1)
            moved = exchange(jnp.stack([held[way][k].astype(kind) for k in gone]), *far[bit])
            for n, k in enumerate(gone):
                held[way][k ^ 1 << bit] = held[way][k ^ 1 << bit] + moved[n].astype(F32)
                del held[way][k]
    return jnp.concatenate([h[0] for h in held], axis=-1)


def has_bit(axis, bit):
    return jnp.bitwise_and(lax.axis_index(axis), bit) > 0


def gather_natural(value, bits):
    for axis, bit in bits:
        other = exchange(value, axis, bit)
        high = has_bit(axis, bit)
        value = jnp.concatenate([jnp.where(high, other, value), jnp.where(high, value, other)], axis=0)
    return value


def halved(value, dim, axis, bit):
    half = value.shape[dim] // 2
    high = has_bit(axis, bit)
    low_half = lax.slice_in_dim(value, 0, half, axis=dim)
    high_half = lax.slice_in_dim(value, half, 2 * half, axis=dim)
    other = exchange(jnp.where(high, low_half, high_half), axis, bit)
    return jnp.where(high, high_half, low_half) + other


def gelu_tanh(values):
    return jax.nn.gelu(values, approximate=True)


def shards(
    hidden_in,
    attn_gain,
    query_weight,
    key_weight,
    value_weight,
    rate_weight,
    gate_weight,
    init_weight,
    init_bias,
    inner_gain,
    inner_shift,
    post_gain,
    post_shift,
    out_weight,
    ffn_gain,
    ffn_gate_weight,
    ffn_up_weight,
    ffn_down_weight,
    doc_starts,
    out_grad,
):
    rows_here, stretch, model = hidden_in.shape
    head_count = rate_weight.shape[1]
    head_dim = init_weight.shape[1]
    parts = stretch // MINI
    local = rows_here * stretch
    seq_count = lax.axis_size("seq")
    rows_count = lax.axis_size("rows")
    share = model // (seq_count * rows_count)
    unit_share = ffn_down_weight.shape[0]
    heads = head_count // seq_count
    width = heads * head_dim
    aligned = share % head_dim == 0
    groups, span = (rows_count, share) if aligned else (1, width)
    me = lax.axis_index("seq")
    everywhere = ("rows", "seq")
    seq_bits = bits_of("seq")
    row_bits = bits_of("rows")
    spare = -unit_share % 16
    head_kind = (groups, span, 0, 0)
    rate_kind = (groups, heads // groups, 0, -heads % 16)
    unit_kind = (rows_count, unit_share, spare, 0)
    units = rows_count * (unit_share + spare)

    def shuffled(values):
        return lax.all_to_all(values, "seq", 0, 0, tiled=True).reshape(-1, values.shape[-1])

    def row_sums(values):
        summed = lax.psum_scatter(values, "rows", scatter_dimension=0, tiled=True)
        return summed.reshape(seq_count, share, -1)

    def columns_out(values):
        return lax.all_to_all(values, "seq", 0, 0, tiled=True)

    def own_part(values):
        split = values.reshape(groups, seq_count, span, -1)
        return lax.dynamic_index_in_dim(split, me, 1, keepdims=False).reshape(width, -1)

    def placed(values):
        split = values.reshape(groups, 1, span, -1)
        here = (jnp.arange(seq_count) == me).reshape(1, -1, 1, 1)
        return jnp.where(here, split, 0.0).reshape(model, -1)

    def reordered(values):
        return values.reshape(rows_here, parts, MINI, -1).transpose(1, 0, 2, 3).reshape(-1, model)

    def restored(values):
        return values.reshape(parts, rows_here, MINI, -1).transpose(1, 0, 2, 3).reshape(rows_here, stretch, -1)

    real = jnp.min(doc_starts) >= 0

    def apart(part, *operands):
        shapes = jax.eval_shape(part, *operands)
        blank = lambda *_: jax.tree.map(lambda s: jnp.zeros(s.shape, s.dtype), shapes)
        return lax.cond(real, part, blank, *operands)

    vectors = jnp.stack(
        [attn_gain, ffn_gain, init_bias, inner_gain, inner_shift, post_gain, post_shift], axis=1
    )
    small = jnp.concatenate([init_weight, rate_weight, vectors], axis=1)
    small = jnp.pad(small, ((0, 0), (0, -small.shape[1] % 128)))
    hidden, cotangent = reordered(hidden_in), reordered(out_grad)
    if aligned:
        out_own = lax.all_gather(out_weight, "rows", axis=0, tiled=True)
    else:
        out_own = own_part(lax.all_gather(out_weight, everywhere, axis=0, tiled=True))
    mixer_cut = shuffled(
        cut_columns((query_weight, key_weight, value_weight, gate_weight), (head_kind,) * 4, seq_count)
    )
    mixer_cut, hidden, cotangent, small, ffn_gate_weight, ffn_up_weight = lax.optimization_barrier(
        (mixer_cut, hidden, cotangent, small, ffn_gate_weight, ffn_up_weight)
    )
    late_cut, out_own = lax.optimization_barrier((mixer_cut, out_own))
    mixer_weight = lax.all_gather(late_cut, "rows", axis=0, tiled=True)
    ffn_cut = cut_columns((ffn_gate_weight, ffn_up_weight), (unit_kind,) * 2, seq_count)

    def gather_inputs(hidden, cotangent, small, ffn_cut):
        hidden_all = gather_blocks(hidden, seq_bits).reshape(-1, model)
        cot_all = gather_blocks(cotangent, seq_bits).reshape(-1, model)
        small = gather_natural(small, row_bits).reshape(rows_count, share, -1)
        small = small.transpose(1, 0, 2).reshape(share, -1)
        small = gather_natural(small, seq_bits).reshape(seq_count, share, rows_count, -1)
        small = small.transpose(2, 0, 1, 3).reshape(model, -1)
        return hidden_all, cot_all, small, shuffled(ffn_cut)

    hidden_all, cot_all, small, ffn_cut = apart(gather_inputs, hidden, cotangent, small, ffn_cut)
    ffn_wide = lax.all_gather(ffn_cut, "rows", axis=0, tiled=True)

    gain_attn = small[:, head_dim + head_count].astype(F32)
    gain_ffn = small[:, head_dim + head_count + 1].astype(F32)
    own_small = own_part(small)
    own_vectors = own_small[:, head_dim + head_count :].astype(F32)
    rate_all = small[:, head_dim : head_dim + head_count].reshape(model, groups, seq_count, -1)
    rate_own = lax.dynamic_index_in_dim(rate_all, me, 2, keepdims=False).reshape(model, heads)
    lanes = heads * rows_here * MINI

    def by_lane(values, repeat):
        turned = values.reshape(heads, head_dim).T
        return jnp.broadcast_to(turned[:, :, None], (head_dim, heads, repeat)).reshape(head_dim, -1)

    bias_lanes = by_lane(own_vectors[:, 2], rows_here * MINI)
    gain_lanes = by_lane(own_vectors[:, 3], rows_here * MINI)
    shift_lanes = by_lane(own_vectors[:, 4], rows_here * MINI)
    post_scale, post_offset = own_vectors[:, 5], own_vectors[:, 6]
    start = own_small[:, :head_dim].astype(F32).reshape(heads, head_dim, head_dim).transpose(2, 0, 1)
    start = jnp.broadcast_to(start[:, :, None], (head_dim, heads, rows_here, head_dim)).reshape(head_dim, -1)

    steps = seq_count
    position = jnp.arange(steps * parts, dtype=jnp.int32) * MINI
    restarts = jnp.logical_or(
        position[:, None] == 0, jnp.any(doc_starts[None] == position[:, None, None], axis=2)
    ).astype(F32)

    def by_chain(repeat):
        wide = jnp.broadcast_to(
            restarts[:, None, :, None], (steps * parts, heads, rows_here, repeat)
        )
        return wide.reshape(steps, parts, -1)

    again, again_wide = by_chain(MINI), by_chain(head_dim)

    order = jnp.arange(steps, dtype=jnp.int32)
    slots = place(order, me, steps)
    blocks = jnp.bitwise_xor(order % (steps // 2) * 2 + order // (steps // 2), me)

    tokens_all = hidden_all.astype(F32)
    inverse_all = lax.rsqrt(jnp.mean(tokens_all * tokens_all, axis=-1, keepdims=True) + EPSILON)
    plain_all = tokens_all * inverse_all
    normed = (plain_all * gain_attn).astype(BF16)


    projected = jnp.dot(normed, mixer_weight, preferred_element_type=F32)
    projected, ffn_down_weight = lax.optimization_barrier((projected, ffn_down_weight))
    down_wide = lax.all_gather(
        jnp.pad(ffn_down_weight, ((0, spare), (0, 0))), "rows", axis=0, tiled=True
    )
    gate_pre = projected[:, 3 * width :]
    logits = jnp.dot(normed, rate_own, preferred_element_type=F32)

    def to_lanes(per_token):
        ordered = jnp.take(per_token.reshape(steps, -1, heads), slots, axis=0)
        ordered = ordered.reshape(steps, parts, rows_here * MINI, heads)
        return ordered.transpose(0, 1, 3, 2).reshape(steps, parts, lanes)

    rates = to_lanes(jax.nn.sigmoid(logits) * (BASE_RATE / head_dim))
    slot = me.astype(jnp.int32).reshape(1)

    inner_out, inner_sums, *saved = inner_forward(
        slot, projected, rates, again, again_wide, start, bias_lanes, gain_lanes,
        shift_lanes, heads, head_dim, parts,
    )

    def feature_mean(sums):
        count = sums.shape[1]
        ordered = jnp.take(sums.T.reshape(count, steps, -1), slots, axis=1)
        total = lax.psum(ordered, "seq") / model
        return jnp.take(total, blocks, axis=1).reshape(count, -1, 1)

    moments = feature_mean(inner_sums)
    post_mean = moments[0]
    post_inverse = lax.rsqrt(moments[1] - post_mean * post_mean + EPSILON)
    post_norm = (inner_out - post_mean) * post_inverse
    post_out = post_norm * post_scale + post_offset
    gated = (gelu_tanh(gate_pre) * post_out).astype(BF16)

    def halves(left, matrix, dims):
        half = left.shape[0] // 2
        away = lax.dot_general(left[half:], matrix, dims, preferred_element_type=F32).astype(BF16)
        own = lax.dot_general(left[:half], matrix, dims, preferred_element_type=F32)
        return own.reshape(-1, local, model), away.reshape(-1, local, model)

    def rms_inverse(values):
        return lax.rsqrt(jnp.mean(values * values, axis=-1, keepdims=True) + EPSILON)

    def into_ffn(own, away, hidden, gain_ffn):
        residual = hidden.astype(F32) + reduce_blocks(own, away, seq_bits)
        scaled = (residual * rms_inverse(residual) * gain_ffn).astype(BF16)
        return residual, gather_blocks(scaled, seq_bits).reshape(-1, model)

    residual, ffn_in = apart(into_ffn, *halves(gated, out_own, NN), hidden, gain_ffn)
    gate_up = jnp.dot(ffn_in, ffn_wide, preferred_element_type=F32)
    gate_value, up_value = gate_up[:, :units], gate_up[:, units:]
    sigmoid_gate = jax.nn.sigmoid(gate_value)
    active = (gate_value * sigmoid_gate * up_value).astype(BF16)

    def token_grad(left, right):
        return lax.dot_general(left, right, TN, preferred_element_type=F32)

    grad_down = token_grad(active, cot_all).astype(BF16)
    grad_down, down_wide = lax.optimization_barrier((grad_down, down_wide))
    grad_down = lax.psum_scatter(grad_down, "rows", scatter_dimension=0, tiled=True)
    delta_active = lax.dot_general(cot_all, down_wide, NT, preferred_element_type=F32)
    delta_up = (delta_active * gate_value * sigmoid_gate).astype(BF16)
    delta_gate = (
        delta_active * up_value * sigmoid_gate * (1.0 + gate_value * (1.0 - sigmoid_gate))
    ).astype(BF16)
    delta_both = jnp.concatenate([delta_gate, delta_up], axis=1)

    def out_of_ffn(own, away, residual, gain_ffn, cotangent):
        delta_ffn = reduce_blocks(own, away, seq_bits)
        inverse_two = rms_inverse(residual)
        scaled_two = delta_ffn * gain_ffn
        delta_after = (
            cotangent.astype(F32)
            + inverse_two * scaled_two
            - residual * inverse_two**3 * jnp.mean(scaled_two * residual, axis=-1, keepdims=True)
        )
        delta_branch = gather_blocks(delta_after.astype(BF16), seq_bits).reshape(-1, model)
        return delta_after, delta_branch

    grad_ffn = token_grad(ffn_in, delta_both).astype(BF16)
    delta_both, grad_ffn = lax.optimization_barrier((delta_both, grad_ffn))
    ffn_sums = row_sums(grad_ffn)
    delta_after, delta_branch = apart(
        out_of_ffn, *halves(delta_both, ffn_wide, NT), residual, gain_ffn, cotangent
    )

    delta_pre, delta_norm, norm_sums, grad_post_scale, grad_post_shift = branch_backward(
        delta_branch, out_own, projected, inner_out, jnp.concatenate([post_mean, post_inverse], axis=1),
        post_scale[None], post_offset[None], max(local, steps * local // 2),
    )
    means = feature_mean(norm_sums)
    per_token = jnp.concatenate([post_mean, post_inverse, means[0], means[1]], axis=1)

    (
        delta_all, delta_logits,
        grad_start, grad_bias, grad_inner_gain, grad_inner_shift,
    ) = inner_backward(
        slot, projected, delta_pre, delta_norm, inner_out, per_token, rates, again, again_wide,
        gain_lanes, shift_lanes, saved, heads, head_dim, parts,
    )
    grad_inputs = token_grad(normed, delta_all).astype(BF16)
    delta_all, grad_inputs = lax.optimization_barrier((delta_all, grad_inputs))
    half = delta_all.shape[0] // 2
    rate_wide = jnp.pad(rate_own, ((0, 0), (0, -heads % 16)))
    away = spread_back(delta_all, delta_logits, half, half, mixer_weight, rate_wide, BF16, model // 4)
    own = spread_back(delta_all, delta_logits, 0, half, mixer_weight, rate_wide, F32, model // 4)
    away, own = away.reshape(-1, local, model), own.reshape(-1, local, model)
    away, own, grad_inputs, gated, active, ffn_sums, grad_down = lax.optimization_barrier(
        (away, own, grad_inputs, gated, active, ffn_sums, grad_down)
    )
    input_sums = row_sums(grad_inputs)
    grad_rate = token_grad(normed, delta_logits[:, :heads])
    grad_out = token_grad(gated, delta_branch).astype(BF16)
    if aligned:
        grad_out = lax.psum_scatter(grad_out, "rows", scatter_dimension=0, tiled=True)

    def out_of_mixer(
        own, away, own_down, away_down, residual, hidden, delta_after, gain_attn, ffn_sums, grad_out, grad_start,
        grad_bias, grad_inner_gain, grad_inner_shift, grad_post_scale, grad_post_shift, grad_rate,
    ):
        def lane_sum(per_lane, repeat):
            return per_lane.reshape(head_dim, heads, repeat).sum(axis=2).T.reshape(width, 1)

        grad_start = grad_start.reshape(head_dim, heads, rows_here, head_dim).sum(axis=2)
        grad_start = grad_start.transpose(1, 2, 0).reshape(width, head_dim)
        grad_bias = grad_bias.reshape(head_dim, heads, rows_here, MINI)[..., 0]
        own_grads = jnp.concatenate(
            [
                grad_start,
                lane_sum(grad_bias, rows_here),
                lane_sum(grad_inner_gain, rows_here * MINI),
                lane_sum(grad_inner_shift, rows_here * MINI),
                grad_post_scale.T,
                grad_post_shift.T,
            ],
            axis=1,
        )
        grad_gate, grad_up, ffn_products = join_columns(
            columns_out(ffn_sums), (ffn_gate_weight, ffn_up_weight), (unit_kind,) * 2
        )
        delta_normed = reduce_blocks(own, away, seq_bits)
        block_out = restored(residual + reduce_blocks(own_down, away_down, seq_bits)).astype(BF16)
        if aligned:
            rates = grad_rate.reshape(rows_count, seq_count, share, heads).transpose(0, 2, 1, 3)
            own_grads = jnp.concatenate([own_grads, rates.reshape(width, -1)], axis=1)
            own_grads = jnp.pad(own_grads, ((0, 0), (0, -own_grads.shape[1] % 128)))
            for axis, bit in reversed(row_bits):
                own_grads = halved(own_grads, 0, axis, bit)
            rates = own_grads[:, head_dim + 5 : head_dim + 5 + seq_count * heads]
            rates = rates.reshape(share, seq_count, heads).transpose(1, 0, 2)
        else:
            rates = lax.psum_scatter(grad_rate, "rows", scatter_dimension=0, tiled=True)
            rates = rates.reshape(seq_count, share, heads)
            own_grads = lax.psum_scatter(
                placed(jnp.concatenate([own_grads.astype(BF16), grad_out], axis=1)),
                everywhere, scatter_dimension=0, tiled=True,
            ).astype(F32)
        tokens = hidden.astype(F32)
        inverse_one = rms_inverse(tokens)
        scaled_one = delta_normed * gain_attn
        hidden_grad = (
            delta_after
            + inverse_one * scaled_one
            - tokens * inverse_one**3 * jnp.mean(scaled_one * tokens, axis=-1, keepdims=True)
        )
        rates = jnp.pad(rates.astype(BF16), ((0, 0), (0, 0), (0, -heads % 16)))
        return block_out, restored(hidden_grad), grad_gate, grad_up, ffn_products, own_grads, rates

    block_out, hidden_grad, grad_gate, grad_up, ffn_products, own_grads, rates = apart(
        out_of_mixer, own, away, *halves(active, down_wide, NN), residual, hidden, delta_after, gain_attn,
        ffn_sums, grad_out, grad_start, grad_bias, grad_inner_gain, grad_inner_shift, grad_post_scale, grad_post_shift, grad_rate,
    )
    grad_query, grad_key, grad_value, grad_gate_weight, grad_rate, input_products = join_columns(
        columns_out(jnp.concatenate([input_sums, rates], axis=2)), (query_weight, key_weight, value_weight, gate_weight, rate_weight),
        (head_kind,) * 4 + (rate_kind,),
    )
    grad_gain_attn = input_products[:, 0] / attn_gain.astype(F32)
    grad_gain_ffn = ffn_products[:, 0] / ffn_gain.astype(F32)
    if not aligned:
        grad_out = own_grads[:, head_dim + 5 :]
    grad_out, grad_rate, grad_down, own_grads, grad_gain_attn, grad_gain_ffn = lax.optimization_barrier(
        (grad_out, grad_rate, grad_down, own_grads, grad_gain_attn, grad_gain_ffn)
    )
    grad_out = grad_out.astype(F32)
    own_vectors_grads = list(own_grads[:, head_dim : head_dim + 5].T)
    return (
        block_out,
        hidden_grad,
        grad_gain_attn,
        grad_query,
        grad_key,
        grad_value,
        grad_rate,
        grad_gate_weight,
        own_grads[:, :head_dim],
        *own_vectors_grads,
        grad_out,
        grad_gain_ffn,
        grad_gate,
        grad_up,
        grad_down[:unit_share].astype(F32),
    )


def solution(mesh):
    split = P(("rows", "seq"))
    matrix = P(("rows", "seq"), None)
    tokens = P("rows", "seq", None)
    return jax.shard_map(
        shards,
        mesh=mesh,
        in_specs=(
            tokens, split, matrix, matrix, matrix, matrix, matrix, matrix, split, split, split, split,
            split, matrix, split, matrix, matrix, matrix, P("rows", None), tokens,
        ),
        out_specs=(
            tokens, tokens, split, matrix, matrix, matrix, matrix, matrix, matrix, split, split, split,
            split, split, matrix, split, matrix, matrix, matrix,
        ),
        check_vma=False,
    )
```

```python
import functools
import jax
import jax.numpy as jnp
from jax import lax
from jax.experimental import pallas as pl
from jax.experimental.pallas import tpu as pltpu
from jax.sharding import PartitionSpec as P

MINI = 16
EPSILON = 1e-06
BASE_RATE = 1.0
GELU_SCALE = (2.0 / 3.141592653589793) ** 0.5
GELU_CUBE = 0.044715
F32 = jnp.float32
BF16 = jnp.bfloat16
NN = (((1,), (0,)), ((), ()))
NT = (((1,), (1,)), ((), ()))
TN = (((0,), (0,)), ((), ()))


def mm(left, right, dims):
    return lax.dot_general(left, right, dims, preferred_element_type=F32)


def in_two(values):
    high = values.astype(BF16)
    return high, (values - high.astype(F32)).astype(BF16)


def mm_two(left, right, dims):
    return mm(left[0], right[0], dims) + (mm(left[1], right[0], dims) + mm(left[0], right[1], dims))


def packed(block, heads, head_dim, parts):
    turned = block.T
    width = block.shape[0] // parts
    return [
        jnp.concatenate(
            [
                turned[h * head_dim : (h + 1) * head_dim, j * width : (j + 1) * width]
                for h in range(heads)
            ],
            axis=1,
        )
        for j in range(parts)
    ]


def unpacked(pieces, heads):
    width = pieces[0].shape[1] // heads
    turned = jnp.concatenate(
        [
            jnp.concatenate([piece[:, h * width : (h + 1) * width] for piece in pieces], axis=1)
            for h in range(heads)
        ],
        axis=0,
    )
    return turned.T


def mean0(values):
    return jnp.mean(values, axis=0, keepdims=True)


def masks(chains, head_dim, dtype):
    lanes = chains * MINI
    rows = lax.broadcasted_iota(jnp.int32, (chains * head_dim, lanes), 0) // head_dim
    cols = lax.broadcasted_iota(jnp.int32, (chains * head_dim, lanes), 1) // MINI
    spread = rows == cols
    source = lax.broadcasted_iota(jnp.int32, (lanes, lanes), 0)
    target = lax.broadcasted_iota(jnp.int32, (lanes, lanes), 1)
    together = (source // MINI) == (target // MINI)
    earlier = jnp.logical_and(together, source <= target)
    scale = jnp.where(earlier, 1.0 / ((target % MINI) + 1).astype(F32), 0.0)
    return spread, together, scale


def spread_out(values, spread, chains):
    return jnp.where(spread, jnp.concatenate([values] * chains, axis=0), jnp.zeros((), values.dtype))


def forward_kernel(
    heads, head_dim, parts,
    slot_ref, inputs_ref, rate_ref, again_ref, again_wide_ref,
    start_ref, start_bias_ref, gain_ref, shift_ref,
    out_ref, sums_ref, kept_ref, spreads_ref, mix_ref, weight_ref,
    state, bias,
):
    chains = rate_ref.shape[-1] // MINI
    spread, together, scale = masks(chains, head_dim, BF16)
    ones = jnp.where(together, 1.0 / MINI, 0.0).astype(BF16)
    gain, shift = gain_ref[...], shift_ref[...]

    @pl.when(pl.program_id(0) == 0)
    def _():
        state[...] = jnp.zeros_like(state)
        bias[...] = jnp.zeros_like(bias)

    width = heads * head_dim
    all_queries, all_keys, all_values = (
        packed(inputs_ref[:, n * width : (n + 1) * width], heads, head_dim, parts) for n in range(3)
    )
    weight = state[...]
    offset = bias[...]
    results = []
    for j in range(parts):
        query, key, value = all_queries[j], all_keys[j], all_values[j]
        rate = rate_ref[0, j : j + 1, :]
        two_keys, two_queries = in_two(key), in_two(query)
        wide_keys = [spread_out(k, spread, chains) for k in two_keys]
        wide_both = [
            jnp.concatenate([k, spread_out(q, spread, chains)], axis=1)
            for k, q in zip(wide_keys, two_queries)
        ]
        mix = in_two((mm_two(two_keys, two_queries, TN) + 1.0) * scale)
        weight = jnp.where(again_wide_ref[0, j : j + 1, :] > 0.0, start_ref[...], weight)
        offset = jnp.where(again_ref[0, j : j + 1, :] > 0.0, start_bias_ref[...], offset)
        two_weights = in_two(weight)
        both = mm_two(two_weights, wide_both, NN)
        lanes = offset.shape[1]
        first = both[:, :lanes] + offset
        center = first - mean0(first)
        inverse = lax.rsqrt(mean0(center * center) + EPSILON)
        normed = center * inverse
        residue = (normed * gain + shift - (value - key)) * gain
        inner = (residue - mean0(residue) - normed * mean0(residue * normed)) * inverse
        rated = in_two(inner * rate)
        combined = both[:, lanes:] + offset - mm_two(rated, mix, NN)
        centered = combined - mean0(combined)
        inverse_out = lax.rsqrt(mean0(centered * centered) + EPSILON)
        rebuilt = centered * inverse_out
        results.append(query + rebuilt * gain + shift)
        weight = weight - mm_two(rated, wide_keys, NT) * (1.0 / MINI)
        offset = offset - (mm(rated[0], ones, NN) + mm(rated[1], ones, NN))
        kept_ref[0, 0, j] = normed
        kept_ref[0, 1, j] = inner
        kept_ref[0, 2, j] = rebuilt
        spreads_ref[0, j : j + 1, :] = inverse
        spreads_ref[0, parts + j : parts + j + 1, :] = inverse_out
        mix_ref[0, j] = mix[0]
        weight_ref[0, j] = two_weights[0]
    out = unpacked(results, heads)
    out_ref[...] = out
    sums_ref[:, 0:1] = jnp.sum(out, axis=1, keepdims=True)
    sums_ref[:, 1:2] = jnp.sum(out * out, axis=1, keepdims=True)
    state[...] = weight
    bias[...] = offset


def gathered_back(wide, lane_chain, head_dim, chains):
    total = wide[:head_dim]
    for c in range(1, chains):
        total = jnp.where(lane_chain == c, wide[c * head_dim : (c + 1) * head_dim], total)
    return total


def backward_kernel(
    heads, head_dim, parts,
    slot_ref, inputs_ref, pre_ref, post_ref, out_ref, token_ref,
    rate_ref, again_ref, again_wide_ref, gain_ref, shift_ref,
    kept_ref, spreads_ref, mix_ref, weight_ref,
    all_ref, logits_ref, dstart_ref, dstart_bias_ref, dgain_ref, dshift_ref,
    state, bias,
):
    chains = rate_ref.shape[-1] // MINI
    lanes = chains * MINI
    spread, together, scale = masks(chains, head_dim, BF16)
    ones = jnp.where(together, 1.0, 0.0).astype(BF16)
    lane_chain = lax.broadcasted_iota(jnp.int32, (head_dim, lanes), 1) // MINI
    gain, shift = gain_ref[...], shift_ref[...]

    @pl.when(pl.program_id(0) == 0)
    def _():
        state[...] = jnp.zeros_like(state)
        bias[...] = jnp.zeros_like(bias)
        dstart_ref[...] = jnp.zeros_like(dstart_ref)
        dstart_bias_ref[...] = jnp.zeros_like(dstart_bias_ref)
        dgain_ref[...] = jnp.zeros_like(dgain_ref)
        dshift_ref[...] = jnp.zeros_like(dshift_ref)

    width = heads * head_dim
    all_queries, all_keys, all_values = (
        packed(inputs_ref[:, n * width : (n + 1) * width], heads, head_dim, parts) for n in range(3)
    )
    center, inverse_all = token_ref[:, 0:1], token_ref[:, 1:2]
    along_post = (out_ref[...] - center) * inverse_all
    delta_post = (post_ref[...] - token_ref[:, 2:3] - along_post * token_ref[:, 3:4]) * inverse_all
    all_deltas = packed(delta_post, heads, head_dim, parts)
    dweight = state[...]
    doffset = bias[...]
    dstart, dstart_bias = dstart_ref[...], dstart_bias_ref[...]
    dgain, dshift = dgain_ref[...], dshift_ref[...]
    dqueries, dkeys, dvalues, dlogits = ([None] * parts for _ in range(4))
    for j in reversed(range(parts)):
        query, key, value, delta = all_queries[j], all_keys[j], all_values[j], all_deltas[j]
        rate = rate_ref[0, j : j + 1, :]
        normed, inner, rebuilt = (kept_ref[0, n, j] for n in range(3))
        inverse, inverse_out = (spreads_ref[0, n * parts + j : n * parts + j + 1, :] for n in range(2))
        mix, weight = mix_ref[0, j], weight_ref[0, j]
        low_key, low_query = key.astype(BF16), query.astype(BF16)
        wide_key = spread_out(low_key, spread, chains)
        wide_query = spread_out(low_query, spread, chains)
        rated = (inner * rate).astype(BF16)
        dnorm = delta * gain
        dcombined = (dnorm - mean0(dnorm) - rebuilt * mean0(dnorm * rebuilt)) * inverse_out
        low_dcombined = dcombined.astype(BF16)
        drated = -mm(low_dcombined, mix, NT)
        dscore = (-mm(rated, low_dcombined, TN) * scale).astype(BF16)
        low_dweight = dweight.astype(BF16)
        drated = drated - (mm(low_dweight, wide_key, NN) + doffset) * (1.0 / MINI)
        dinner = drated * rate
        bent = rate * (1.0 - rate * (head_dim / BASE_RATE))
        dlogits[j] = jnp.sum(drated * inner, axis=0, keepdims=True) * bent
        scaled = dinner * inverse
        offset_residue = normed * gain + shift - (value - key)
        residue = offset_residue * gain
        along = mean0(scaled * normed)
        dresidue = scaled - mean0(scaled) - normed * along
        gained = dresidue * gain
        dnormed = gained * gain - scaled * mean0(residue * normed) - residue * along
        dfirst = (
            dnormed - mean0(dnormed) - normed * (mean0(dnormed * normed) + mean0(dinner * inner))
        ) * inverse
        low_dfirst = dfirst.astype(BF16)
        dvalues[j] = -gained
        back_key = gathered_back(mm(weight, low_dfirst, TN), lane_chain, head_dim, chains)
        back_query = gathered_back(mm(weight, low_dcombined, TN), lane_chain, head_dim, chains)
        back_state = gathered_back(mm(low_dweight, rated, TN), lane_chain, head_dim, chains)
        dkeys[j] = gained + back_key - back_state * (1.0 / MINI) + mm(low_query, dscore, NT)
        dqueries[j] = delta + back_query + mm(low_key, dscore, NN)
        dgain = dgain + delta * rebuilt + dresidue * offset_residue + gained * normed
        dshift = dshift + delta + gained
        dweight = dweight + mm(low_dfirst, wide_key, NT) + mm(low_dcombined, wide_query, NT)
        both = (dfirst + dcombined).astype(BF16)
        doffset = doffset + mm(both, ones, NN)
        again_wide = again_wide_ref[0, j : j + 1, :] > 0.0
        again = again_ref[0, j : j + 1, :] > 0.0
        dstart = dstart + jnp.where(again_wide, dweight, 0.0)
        dstart_bias = dstart_bias + jnp.where(again, doffset, 0.0)
        dweight = jnp.where(again_wide, 0.0, dweight)
        doffset = jnp.where(again, 0.0, doffset)
    for n, pieces in enumerate((dqueries, dkeys, dvalues)):
        natural = unpacked(pieces, heads).astype(all_ref.dtype)
        all_ref[:, n * width : (n + 1) * width] = natural
    all_ref[:, 3 * width : 4 * width] = pre_ref[...]
    natural = unpacked(dlogits, heads)
    spare = logits_ref.shape[1] - heads
    if spare:
        natural = jnp.concatenate([natural, jnp.zeros((natural.shape[0], spare), F32)], axis=1)
    logits_ref[...] = natural.astype(logits_ref.dtype)
    state[...] = dweight
    bias[...] = doffset
    dstart_ref[...] = dstart
    dstart_bias_ref[...] = dstart_bias
    dgain_ref[...] = dgain
    dshift_ref[...] = dshift


def whole(shape):
    return pl.BlockSpec(shape, lambda *_: (0,) * len(shape))


def place(step, own, count):
    apart = jnp.bitwise_xor(step, own)
    return jnp.bitwise_and(apart, 1) * (count // 2) + lax.shift_right_logical(apart, 1)


def inner_forward(slot, projected, rates, again, again_wide, start, start_bias, gain, shift, heads, head_dim, parts):
    steps, _, lanes = rates.shape
    tokens = projected.shape[0] // steps
    wide = start.shape[1]
    at_slot = pl.BlockSpec((tokens, heads * head_dim), lambda i, s: (place(i, s[0], steps), 0))

    def stepped(*shape):
        return pl.BlockSpec((1,) + shape, lambda i, s: (i,) + (0,) * len(shape))

    saved = [
        ((3, parts, head_dim, lanes), F32), ((2 * parts, lanes), F32),
        ((parts, lanes, lanes), BF16), ((parts, head_dim, wide), BF16),
    ]
    return pl.pallas_call(
        functools.partial(forward_kernel, heads, head_dim, parts),
        out_shape=[jax.ShapeDtypeStruct((steps * tokens, heads * head_dim), F32), jax.ShapeDtypeStruct((steps * tokens, 2), F32)]
        + [jax.ShapeDtypeStruct((steps,) + shape, kind) for shape, kind in saved],
        grid_spec=pltpu.PrefetchScalarGridSpec(
            num_scalar_prefetch=1,
            grid=(steps,),
            in_specs=[pl.BlockSpec((tokens, 3 * heads * head_dim), at_slot.index_map)]
            + [stepped(parts, lanes), stepped(parts, lanes), stepped(parts, wide)]
            + [whole(start.shape), whole(start_bias.shape), whole(gain.shape), whole(shift.shape)],
            out_specs=[at_slot, pl.BlockSpec((tokens, 2), at_slot.index_map)]
            + [stepped(*shape) for shape, _ in saved],
            scratch_shapes=[pltpu.VMEM(start.shape, F32), pltpu.VMEM(start_bias.shape, F32)],
        ),
        compiler_params=pltpu.CompilerParams(
            dimension_semantics=("arbitrary",), vmem_limit_bytes=63 * 1024 * 1024
        ),
        name="inner_forward",
    )(slot, projected, rates, again, again_wide, start, start_bias, gain, shift)


def inner_backward(slot, projected, pre, deltas, outs, per_token, rates, again, again_wide, gain, shift, saved, heads, head_dim, parts):
    steps, _, lanes = rates.shape
    tokens = projected.shape[0] // steps
    wide = again_wide.shape[-1]
    inputs, logits = 4 * heads * head_dim, heads + -heads % 16
    at_slot = pl.BlockSpec(
        (tokens, heads * head_dim), lambda i, s: (place(steps - 1 - i, s[0], steps), 0)
    )

    def stepped(*shape):
        return pl.BlockSpec((1,) + shape, lambda i, s: (steps - 1 - i,) + (0,) * len(shape))

    return pl.pallas_call(
        functools.partial(backward_kernel, heads, head_dim, parts),
        out_shape=[
            jax.ShapeDtypeStruct((steps * tokens, inputs), BF16),
            jax.ShapeDtypeStruct((steps * tokens, logits), BF16),
            jax.ShapeDtypeStruct((head_dim, wide), F32),
            jax.ShapeDtypeStruct((head_dim, lanes), F32),
            jax.ShapeDtypeStruct((head_dim, lanes), F32),
            jax.ShapeDtypeStruct((head_dim, lanes), F32),
        ],
        grid_spec=pltpu.PrefetchScalarGridSpec(
            num_scalar_prefetch=1,
            grid=(steps,),
            in_specs=[pl.BlockSpec((tokens, 3 * heads * head_dim), at_slot.index_map)]
            + [at_slot] * 3
            + [pl.BlockSpec((tokens, per_token.shape[1]), at_slot.index_map)]
            + [stepped(parts, lanes), stepped(parts, lanes), stepped(parts, wide)]
            + [whole(gain.shape), whole(shift.shape)]
            + [stepped(*array.shape[1:]) for array in saved],
            out_specs=[
                pl.BlockSpec((tokens, inputs), at_slot.index_map),
                pl.BlockSpec((tokens, logits), at_slot.index_map),
                whole((head_dim, wide)),
            ]
            + [whole((head_dim, lanes))] * 3,
            scratch_shapes=[pltpu.VMEM((head_dim, wide), F32), pltpu.VMEM((head_dim, lanes), F32)],
        ),
        compiler_params=pltpu.CompilerParams(
            dimension_semantics=("arbitrary",), vmem_limit_bytes=63 * 1024 * 1024
        ),
        name="inner_backward",
    )(slot, projected, pre, deltas, outs, per_token, rates, again, again_wide, gain, shift, *saved)


def cut_kernel(seq_count, kinds, *refs):
    out_ref = refs[-1]
    for s in range(seq_count):
        pieces = []
        for ref, (groups, span, gap, rest) in zip(refs, kinds):
            rows = ref.shape[0]
            for g in range(groups):
                at = (g * seq_count + s) * span
                pieces.append(ref[:, at : at + span].astype(F32))
                if gap:
                    pieces.append(jnp.zeros((rows, gap), F32))
            if rest:
                pieces.append(jnp.zeros((rows, rest), F32))
        out_ref[s] = jnp.concatenate(pieces, axis=1).astype(out_ref.dtype)


def cut_columns(weights, kinds, seq_count):
    rows = weights[0].shape[0]
    columns = sum(groups * (span + gap) + rest for groups, span, gap, rest in kinds)
    return pl.pallas_call(
        functools.partial(cut_kernel, seq_count, kinds),
        out_shape=jax.ShapeDtypeStruct((seq_count, rows, columns), BF16),
        compiler_params=pltpu.CompilerParams(vmem_limit_bytes=40 * 1024 * 1024),
        name="cut_columns",
    )(*weights)


def join_kernel(seq_count, kinds, *refs):
    count = len(kinds)
    parts_ref, weights, grads, sums_ref = refs[0], refs[1 : 1 + count], refs[1 + count : -1], refs[-1]
    total = 0.0
    base = 0
    for weight, ref, (groups, span, gap, rest) in zip(weights, grads, kinds):
        pieces = []
        for g in range(groups):
            at = base + g * (span + gap)
            pieces += [parts_ref[s, :, at : at + span].astype(F32) for s in range(seq_count)]
        whole_row = jnp.concatenate(pieces, axis=1)
        ref[...] = whole_row
        total = total + jnp.sum(whole_row * weight[...].astype(F32), axis=1, keepdims=True)
        base += groups * (span + gap) + rest
    sums_ref[...] = total


def join_columns(parts, weights, kinds):
    return pl.pallas_call(
        functools.partial(join_kernel, parts.shape[0], kinds),
        out_shape=[jax.ShapeDtypeStruct(w.shape, F32) for w in weights]
        + [jax.ShapeDtypeStruct((parts.shape[1], 1), F32)],
        compiler_params=pltpu.CompilerParams(vmem_limit_bytes=40 * 1024 * 1024),
        name="join_columns",
    )(parts, *weights)


def branch_kernel(
    delta_ref, matrix_ref, pre_ref, out_ref, token_ref, scale_ref, offset_ref,
    dpre_ref, dnorm_ref, sums_ref, dscale_ref, doffset_ref,
):
    @pl.when(pl.program_id(0) == 0)
    def _():
        dscale_ref[...] = jnp.zeros_like(dscale_ref)
        doffset_ref[...] = jnp.zeros_like(doffset_ref)

    delta_gated = mm(delta_ref[...], matrix_ref[...], NT)
    scale = scale_ref[...]
    norm = (out_ref[...] - token_ref[:, 0:1]) * token_ref[:, 1:2]
    pre = pre_ref[...]
    square = pre * pre
    bend = jnp.tanh(GELU_SCALE * pre * (1.0 + GELU_CUBE * square))
    half = 0.5 * (1.0 + bend)
    slope = half + 0.5 * pre * (1.0 - bend * bend) * (GELU_SCALE * (1.0 + 3.0 * GELU_CUBE * square))
    dpre_ref[...] = (delta_gated * (norm * scale + offset_ref[...]) * slope).astype(dpre_ref.dtype)
    delta_post = delta_gated * (pre * half)
    dscale_ref[...] += jnp.sum(delta_post * norm, axis=0, keepdims=True)
    doffset_ref[...] += jnp.sum(delta_post, axis=0, keepdims=True)
    dnorm = delta_post * scale
    dnorm_ref[...] = dnorm
    sums_ref[:, 0:1] = jnp.sum(dnorm, axis=1, keepdims=True)
    sums_ref[:, 1:2] = jnp.sum(dnorm * norm, axis=1, keepdims=True)


def branch_backward(delta, matrix, projected, out, per_token, scale, offset, block):
    tokens, width = out.shape
    gate = pl.BlockSpec((block, width), lambda i: (i, 3))

    def by_block(array):
        return pl.BlockSpec((block, array.shape[1]), lambda i: (i, 0))

    row = jax.ShapeDtypeStruct((1, width), F32)
    sums = jax.ShapeDtypeStruct((tokens, 2), F32)
    return pl.pallas_call(
        branch_kernel,
        grid=(tokens // block,),
        in_specs=[by_block(delta), whole(matrix.shape), gate, by_block(out), by_block(per_token)]
        + [whole((1, width))] * 2,
        out_shape=[jax.ShapeDtypeStruct(out.shape, BF16), jax.ShapeDtypeStruct(out.shape, F32), sums, row, row],
        out_specs=[by_block(out), by_block(out), by_block(sums), whole((1, width)), whole((1, width))],
        compiler_params=pltpu.CompilerParams(
            dimension_semantics=("arbitrary",), vmem_limit_bytes=63 * 1024 * 1024
        ),
        name="branch_backward",
    )(delta, matrix, projected, out, per_token, scale, offset)


def spread_kernel(delta_ref, logits_ref, weight_ref, rate_ref, out_ref):
    total = mm(delta_ref[...], weight_ref[...], NT) + mm(logits_ref[...], rate_ref[...], NT)
    out_ref[...] = total.astype(out_ref.dtype)


def spread_back(delta, logits, first, tokens, weight, rate, kind, block):
    model = weight.shape[0]
    return pl.pallas_call(
        spread_kernel,
        grid=(model // block,),
        in_specs=[
            pl.BlockSpec((tokens, delta.shape[1]), lambda i: (first // tokens, 0)),
            pl.BlockSpec((tokens, logits.shape[1]), lambda i: (first // tokens, 0)),
            pl.BlockSpec((block, weight.shape[1]), lambda i: (i, 0)),
            pl.BlockSpec((block, rate.shape[1]), lambda i: (i, 0)),
        ],
        out_specs=pl.BlockSpec((tokens, block), lambda i: (0, i)),
        out_shape=jax.ShapeDtypeStruct((tokens, model), kind),
        compiler_params=pltpu.CompilerParams(
            dimension_semantics=("arbitrary",), vmem_limit_bytes=40 * 1024 * 1024
        ),
        name="spread_back",
    )(delta, logits, weight, rate)


def exchange(value, axis, bit):
    count = lax.axis_size(axis)
    return lax.ppermute(value, axis, [(i, i ^ bit) for i in range(count)])


def bits_of(axis):
    return [(axis, 1 << p) for p in range(lax.axis_size(axis).bit_length() - 1)]


def cuts_of(width, ways):
    unit = 128 if width >= 128 * ways else 1
    return [unit * (n * (width // unit) // ways) for n in range(ways)] + [width]


def gather_blocks(block, bits, tied=None):
    near, far = bits[0], bits[1:]
    ways = max(1, len(far))
    cuts = cuts_of(block.shape[-1], ways)
    held = [{0: block[:, cuts[way] : cuts[way + 1]]} for way in range(ways)]
    for step in range(len(far)):
        for way in range(ways):
            bit = (way + step) % len(far)
            keys = sorted(held[way])
            moved = exchange(jnp.stack([held[way][k] for k in keys]), *far[bit])
            for n, k in enumerate(keys):
                held[way][k | 1 << bit] = moved[n]
    half = jnp.concatenate([jnp.stack([h[k] for k in sorted(h)]) for h in held], axis=-1)
    if tied is not None:
        half, tied = lax.optimization_barrier((half, tied))
    whole = jnp.concatenate([half, exchange(half, *near)], axis=0)
    return whole if tied is None else (whole, tied)


def reduce_blocks(own, away, bits, near_kind=BF16, last_kind=BF16):
    near, far = bits[0], bits[1:]
    ways = max(1, len(far))
    cuts = cuts_of(own.shape[-1], ways)
    half = own.astype(F32) + exchange(away.astype(near_kind), *near).astype(F32)
    held = [
        {k: half[k, :, cuts[way] : cuts[way + 1]] for k in range(half.shape[0])} for way in range(ways)
    ]
    for step in range(len(far)):
        for way in range(ways):
            bit = (way + step) % len(far)
            gone = sorted(k for k in held[way] if k >> bit & 1)
            kind = last_kind if step == len(far) - 1 else BF16
            moved = exchange(jnp.stack([held[way][k].astype(kind) for k in gone]), *far[bit])
            for n, k in enumerate(gone):
                held[way][k ^ 1 << bit] = held[way][k ^ 1 << bit] + moved[n].astype(F32)
                del held[way][k]
    return jnp.concatenate([h[0] for h in held], axis=-1)


def has_bit(axis, bit):
    return jnp.bitwise_and(lax.axis_index(axis), bit) > 0


def gather_natural(value, bits):
    for axis, bit in bits:
        other = exchange(value, axis, bit)
        high = has_bit(axis, bit)
        value = jnp.concatenate([jnp.where(high, other, value), jnp.where(high, value, other)], axis=0)
    return value


def halved(value, dim, axis, bit):
    half = value.shape[dim] // 2
    high = has_bit(axis, bit)
    low_half = lax.slice_in_dim(value, 0, half, axis=dim)
    high_half = lax.slice_in_dim(value, half, 2 * half, axis=dim)
    other = exchange(jnp.where(high, low_half, high_half), axis, bit)
    return jnp.where(high, high_half, low_half) + other


def gelu_tanh(values):
    return jax.nn.gelu(values, approximate=True)


def shards(
    hidden_in,
    attn_gain,
    query_weight,
    key_weight,
    value_weight,
    rate_weight,
    gate_weight,
    init_weight,
    init_bias,
    inner_gain,
    inner_shift,
    post_gain,
    post_shift,
    out_weight,
    ffn_gain,
    ffn_gate_weight,
    ffn_up_weight,
    ffn_down_weight,
    doc_starts,
    out_grad,
):
    rows_here, stretch, model = hidden_in.shape
    head_count = rate_weight.shape[1]
    head_dim = init_weight.shape[1]
    parts = stretch // MINI
    local = rows_here * stretch
    seq_count = lax.axis_size("seq")
    rows_count = lax.axis_size("rows")
    share = model // (seq_count * rows_count)
    unit_share = ffn_down_weight.shape[0]
    heads = head_count // seq_count
    width = heads * head_dim
    aligned = share % head_dim == 0
    groups, span = (rows_count, share) if aligned else (1, width)
    me = lax.axis_index("seq")
    everywhere = ("rows", "seq")
    seq_bits = bits_of("seq")
    row_bits = bits_of("rows")
    spare = -unit_share % 16
    head_kind = (groups, span, 0, 0)
    rate_kind = (groups, heads // groups, 0, -heads % 16)
    unit_kind = (rows_count, unit_share, spare, 0)
    units = rows_count * (unit_share + spare)

    def shuffled(values):
        return lax.all_to_all(values, "seq", 0, 0, tiled=True).reshape(-1, values.shape[-1])

    def row_sums(values):
        summed = lax.psum_scatter(values, "rows", scatter_dimension=0, tiled=True)
        return summed.reshape(seq_count, share, -1)

    def columns_out(values):
        return lax.all_to_all(values, "seq", 0, 0, tiled=True)

    def own_part(values):
        split = values.reshape(groups, seq_count, span, -1)
        return lax.dynamic_index_in_dim(split, me, 1, keepdims=False).reshape(width, -1)

    def placed(values):
        split = values.reshape(groups, 1, span, -1)
        here = (jnp.arange(seq_count) == me).reshape(1, -1, 1, 1)
        return jnp.where(here, split, 0.0).reshape(model, -1)

    def reordered(values):
        return values.reshape(rows_here, parts, MINI, -1).transpose(1, 0, 2, 3).reshape(-1, model)

    def restored(values):
        return values.reshape(parts, rows_here, MINI, -1).transpose(1, 0, 2, 3).reshape(rows_here, stretch, -1)

    real = jnp.min(doc_starts) >= 0

    def apart(part, *operands):
        shapes = jax.eval_shape(part, *operands)
        blank = lambda *_: jax.tree.map(lambda s: jnp.zeros(s.shape, s.dtype), shapes)
        return lax.cond(real, part, blank, *operands)

    vectors = jnp.stack(
        [attn_gain, ffn_gain, init_bias, inner_gain, inner_shift, post_gain, post_shift], axis=1
    )
    small = jnp.concatenate([init_weight, rate_weight, vectors], axis=1)
    small = jnp.pad(small, ((0, 0), (0, -small.shape[1] % 128)))
    hidden, cotangent = reordered(hidden_in), reordered(out_grad)
    if aligned:
        out_own = lax.all_gather(out_weight, "rows", axis=0, tiled=True)
    else:
        out_own = own_part(lax.all_gather(out_weight, everywhere, axis=0, tiled=True))
    mixer_cut = shuffled(
        cut_columns((query_weight, key_weight, value_weight, gate_weight), (head_kind,) * 4, seq_count)
    )
    mixer_cut, hidden, cotangent, small, ffn_gate_weight, ffn_up_weight = lax.optimization_barrier(
        (mixer_cut, hidden, cotangent, small, ffn_gate_weight, ffn_up_weight)
    )
    late_cut, out_own = lax.optimization_barrier((mixer_cut, out_own))
    mixer_weight = lax.all_gather(late_cut, "rows", axis=0, tiled=True)
    ffn_cut = cut_columns((ffn_gate_weight, ffn_up_weight), (unit_kind,) * 2, seq_count)

    def gather_inputs(hidden, cotangent, small, ffn_cut):
        hidden_all = gather_blocks(hidden, seq_bits).reshape(-1, model)
        cot_all = gather_blocks(cotangent, seq_bits).reshape(-1, model)
        small = gather_natural(small, row_bits).reshape(rows_count, share, -1)
        small = small.transpose(1, 0, 2).reshape(share, -1)
        small = gather_natural(small, seq_bits).reshape(seq_count, share, rows_count, -1)
        small = small.transpose(2, 0, 1, 3).reshape(model, -1)
        return hidden_all, cot_all, small, shuffled(ffn_cut)

    hidden_all, cot_all, small, ffn_cut = apart(gather_inputs, hidden, cotangent, small, ffn_cut)
    ffn_wide = lax.all_gather(ffn_cut, "rows", axis=0, tiled=True)

    gain_attn = small[:, head_dim + head_count].astype(F32)
    gain_ffn = small[:, head_dim + head_count + 1].astype(F32)
    own_small = own_part(small)
    own_vectors = own_small[:, head_dim + head_count :].astype(F32)
    rate_all = small[:, head_dim : head_dim + head_count].reshape(model, groups, seq_count, -1)
    rate_own = lax.dynamic_index_in_dim(rate_all, me, 2, keepdims=False).reshape(model, heads)
    lanes = heads * rows_here * MINI

    def by_lane(values, repeat):
        turned = values.reshape(heads, head_dim).T
        return jnp.broadcast_to(turned[:, :, None], (head_dim, heads, repeat)).reshape(head_dim, -1)

    bias_lanes = by_lane(own_vectors[:, 2], rows_here * MINI)
    gain_lanes = by_lane(own_vectors[:, 3], rows_here * MINI)
    shift_lanes = by_lane(own_vectors[:, 4], rows_here * MINI)
    post_scale, post_offset = own_vectors[:, 5], own_vectors[:, 6]
    start = own_small[:, :head_dim].astype(F32).reshape(heads, head_dim, head_dim).transpose(2, 0, 1)
    start = jnp.broadcast_to(start[:, :, None], (head_dim, heads, rows_here, head_dim)).reshape(head_dim, -1)

    steps = seq_count
    position = jnp.arange(steps * parts, dtype=jnp.int32) * MINI
    restarts = jnp.logical_or(
        position[:, None] == 0, jnp.any(doc_starts[None] == position[:, None, None], axis=2)
    ).astype(F32)

    def by_chain(repeat):
        wide = jnp.broadcast_to(
            restarts[:, None, :, None], (steps * parts, heads, rows_here, repeat)
        )
        return wide.reshape(steps, parts, -1)

    again, again_wide = by_chain(MINI), by_chain(head_dim)

    order = jnp.arange(steps, dtype=jnp.int32)
    slots = place(order, me, steps)
    blocks = jnp.bitwise_xor(order % (steps // 2) * 2 + order // (steps // 2), me)

    tokens_all = hidden_all.astype(F32)
    inverse_all = lax.rsqrt(jnp.mean(tokens_all * tokens_all, axis=-1, keepdims=True) + EPSILON)
    plain_all = tokens_all * inverse_all
    normed = (plain_all * gain_attn).astype(BF16)


    projected = jnp.dot(normed, mixer_weight, preferred_element_type=F32)
    projected, ffn_down_weight = lax.optimization_barrier((projected, ffn_down_weight))
    down_wide = lax.all_gather(
        jnp.pad(ffn_down_weight, ((0, spare), (0, 0))), "rows", axis=0, tiled=True
    )
    gate_pre = projected[:, 3 * width :]
    logits = jnp.dot(normed, rate_own, preferred_element_type=F32)

    def to_lanes(per_token):
        ordered = jnp.take(per_token.reshape(steps, -1, heads), slots, axis=0)
        ordered = ordered.reshape(steps, parts, rows_here * MINI, heads)
        return ordered.transpose(0, 1, 3, 2).reshape(steps, parts, lanes)

    rates = to_lanes(jax.nn.sigmoid(logits) * (BASE_RATE / head_dim))
    slot = me.astype(jnp.int32).reshape(1)

    inner_out, inner_sums, *saved = inner_forward(
        slot, projected, rates, again, again_wide, start, bias_lanes, gain_lanes,
        shift_lanes, heads, head_dim, parts,
    )

    def feature_mean(sums):
        count = sums.shape[1]
        ordered = jnp.take(sums.T.reshape(count, steps, -1), slots, axis=1)
        total = lax.psum(ordered, "seq") / model
        return jnp.take(total, blocks, axis=1).reshape(count, -1, 1)

    moments = feature_mean(inner_sums)
    post_mean = moments[0]
    post_inverse = lax.rsqrt(moments[1] - post_mean * post_mean + EPSILON)
    post_norm = (inner_out - post_mean) * post_inverse
    post_out = post_norm * post_scale + post_offset
    gated = (gelu_tanh(gate_pre) * post_out).astype(BF16)

    def halves(left, matrix, dims, kind=BF16):
        half = left.shape[0] // 2
        away = lax.dot_general(left[half:], matrix, dims, preferred_element_type=F32).astype(kind)
        own = lax.dot_general(left[:half], matrix, dims, preferred_element_type=F32)
        return own.reshape(-1, local, model), away.reshape(-1, local, model)

    def rms_inverse(values):
        return lax.rsqrt(jnp.mean(values * values, axis=-1, keepdims=True) + EPSILON)

    def into_ffn(own, away, hidden, gain_ffn):
        residual = hidden.astype(F32) + reduce_blocks(own, away, seq_bits, F32, F32)
        scaled = (residual * rms_inverse(residual) * gain_ffn).astype(BF16)
        return residual, gather_blocks(scaled, seq_bits).reshape(-1, model)

    residual, ffn_in = apart(into_ffn, *halves(gated, out_own, NN, F32), hidden, gain_ffn)
    gate_up = jnp.dot(ffn_in, ffn_wide, preferred_element_type=F32)
    gate_value, up_value = gate_up[:, :units], gate_up[:, units:]
    sigmoid_gate = jax.nn.sigmoid(gate_value)
    active = (gate_value * sigmoid_gate * up_value).astype(BF16)

    def token_grad(left, right):
        return lax.dot_general(left, right, TN, preferred_element_type=F32)

    grad_down = token_grad(active, cot_all).astype(BF16)
    grad_down, down_wide = lax.optimization_barrier((grad_down, down_wide))
    grad_down = lax.psum_scatter(grad_down, "rows", scatter_dimension=0, tiled=True)
    delta_active = lax.dot_general(cot_all, down_wide, NT, preferred_element_type=F32)
    delta_up = (delta_active * gate_value * sigmoid_gate).astype(BF16)
    delta_gate = (
        delta_active * up_value * sigmoid_gate * (1.0 + gate_value * (1.0 - sigmoid_gate))
    ).astype(BF16)
    delta_both = jnp.concatenate([delta_gate, delta_up], axis=1)

    def out_of_ffn(own, away, residual, gain_ffn, cotangent):
        delta_ffn = reduce_blocks(own, away, seq_bits)
        inverse_two = rms_inverse(residual)
        scaled_two = delta_ffn * gain_ffn
        delta_after = (
            cotangent.astype(F32)
            + inverse_two * scaled_two
            - residual * inverse_two**3 * jnp.mean(scaled_two * residual, axis=-1, keepdims=True)
        )
        delta_branch = gather_blocks(delta_after.astype(BF16), seq_bits).reshape(-1, model)
        return delta_after, delta_branch

    grad_ffn = token_grad(ffn_in, delta_both).astype(BF16)
    delta_both, grad_ffn = lax.optimization_barrier((delta_both, grad_ffn))
    ffn_sums = row_sums(grad_ffn)
    delta_after, delta_branch = apart(
        out_of_ffn, *halves(delta_both, ffn_wide, NT), residual, gain_ffn, cotangent
    )

    delta_pre, delta_norm, norm_sums, grad_post_scale, grad_post_shift = branch_backward(
        delta_branch, out_own, projected, inner_out, jnp.concatenate([post_mean, post_inverse], axis=1),
        post_scale[None], post_offset[None], max(local, steps * local // 2),
    )
    means = feature_mean(norm_sums)
    per_token = jnp.concatenate([post_mean, post_inverse, means[0], means[1]], axis=1)

    (
        delta_all, delta_logits,
        grad_start, grad_bias, grad_inner_gain, grad_inner_shift,
    ) = inner_backward(
        slot, projected, delta_pre, delta_norm, inner_out, per_token, rates, again, again_wide,
        gain_lanes, shift_lanes, saved, heads, head_dim, parts,
    )
    grad_inputs = token_grad(normed, delta_all).astype(BF16)
    delta_all, grad_inputs = lax.optimization_barrier((delta_all, grad_inputs))
    half = delta_all.shape[0] // 2
    rate_wide = jnp.pad(rate_own, ((0, 0), (0, -heads % 16)))
    away = spread_back(delta_all, delta_logits, half, half, mixer_weight, rate_wide, BF16, model // 4)
    own = spread_back(delta_all, delta_logits, 0, half, mixer_weight, rate_wide, F32, model // 4)
    away, own = away.reshape(-1, local, model), own.reshape(-1, local, model)
    away, own, grad_inputs, gated, active, ffn_sums, grad_down = lax.optimization_barrier(
        (away, own, grad_inputs, gated, active, ffn_sums, grad_down)
    )
    input_sums = row_sums(grad_inputs)
    grad_rate = token_grad(normed, delta_logits[:, :heads])
    grad_out = token_grad(gated, delta_branch).astype(BF16)
    if aligned:
        grad_out = lax.psum_scatter(grad_out, "rows", scatter_dimension=0, tiled=True)

    def out_of_mixer(
        own, away, own_down, away_down, residual, hidden, delta_after, gain_attn, ffn_sums, grad_out, grad_start,
        grad_bias, grad_inner_gain, grad_inner_shift, grad_post_scale, grad_post_shift, grad_rate,
    ):
        def lane_sum(per_lane, repeat):
            return per_lane.reshape(head_dim, heads, repeat).sum(axis=2).T.reshape(width, 1)

        grad_start = grad_start.reshape(head_dim, heads, rows_here, head_dim).sum(axis=2)
        grad_start = grad_start.transpose(1, 2, 0).reshape(width, head_dim)
        grad_bias = grad_bias.reshape(head_dim, heads, rows_here, MINI)[..., 0]
        own_grads = jnp.concatenate(
            [
                grad_start,
                lane_sum(grad_bias, rows_here),
                lane_sum(grad_inner_gain, rows_here * MINI),
                lane_sum(grad_inner_shift, rows_here * MINI),
                grad_post_scale.T,
                grad_post_shift.T,
            ],
            axis=1,
        )
        grad_gate, grad_up, ffn_products = join_columns(
            columns_out(ffn_sums), (ffn_gate_weight, ffn_up_weight), (unit_kind,) * 2
        )
        delta_normed = reduce_blocks(own, away, seq_bits)
        block_out = restored(residual + reduce_blocks(own_down, away_down, seq_bits)).astype(BF16)
        if aligned:
            rates = grad_rate.reshape(rows_count, seq_count, share, heads).transpose(0, 2, 1, 3)
            own_grads = jnp.concatenate([own_grads, rates.reshape(width, -1)], axis=1)
            own_grads = jnp.pad(own_grads, ((0, 0), (0, -own_grads.shape[1] % 128)))
            for axis, bit in reversed(row_bits):
                own_grads = halved(own_grads, 0, axis, bit)
            rates = own_grads[:, head_dim + 5 : head_dim + 5 + seq_count * heads]
            rates = rates.reshape(share, seq_count, heads).transpose(1, 0, 2)
        else:
            rates = lax.psum_scatter(grad_rate, "rows", scatter_dimension=0, tiled=True)
            rates = rates.reshape(seq_count, share, heads)
            own_grads = lax.psum_scatter(
                placed(jnp.concatenate([own_grads.astype(BF16), grad_out], axis=1)),
                everywhere, scatter_dimension=0, tiled=True,
            ).astype(F32)
        tokens = hidden.astype(F32)
        inverse_one = rms_inverse(tokens)
        scaled_one = delta_normed * gain_attn
        hidden_grad = (
            delta_after
            + inverse_one * scaled_one
            - tokens * inverse_one**3 * jnp.mean(scaled_one * tokens, axis=-1, keepdims=True)
        )
        rates = jnp.pad(rates.astype(BF16), ((0, 0), (0, 0), (0, -heads % 16)))
        return block_out, restored(hidden_grad), grad_gate, grad_up, ffn_products, own_grads, rates

    block_out, hidden_grad, grad_gate, grad_up, ffn_products, own_grads, rates = apart(
        out_of_mixer, own, away, *halves(active, down_wide, NN), residual, hidden, delta_after, gain_attn,
        ffn_sums, grad_out, grad_start, grad_bias, grad_inner_gain, grad_inner_shift, grad_post_scale, grad_post_shift, grad_rate,
    )
    grad_query, grad_key, grad_value, grad_gate_weight, grad_rate, input_products = join_columns(
        columns_out(jnp.concatenate([input_sums, rates], axis=2)), (query_weight, key_weight, value_weight, gate_weight, rate_weight),
        (head_kind,) * 4 + (rate_kind,),
    )
    grad_gain_attn = input_products[:, 0] / attn_gain.astype(F32)
    grad_gain_ffn = ffn_products[:, 0] / ffn_gain.astype(F32)
    if not aligned:
        grad_out = own_grads[:, head_dim + 5 :]
    results = (
        block_out,
        hidden_grad,
        grad_gain_attn,
        grad_query,
        grad_key,
        grad_value,
        grad_rate,
        grad_gate_weight,
        own_grads[:, :head_dim],
        *list(own_grads[:, head_dim : head_dim + 5].T),
        grad_out,
        grad_gain_ffn,
        grad_gate,
        grad_up,
        grad_down[:unit_share].astype(F32),
    )
    results = list(lax.optimization_barrier(results))
    results[14] = results[14].astype(F32)
    return tuple(results)


def solution(mesh):
    split = P(("rows", "seq"))
    matrix = P(("rows", "seq"), None)
    tokens = P("rows", "seq", None)
    return jax.shard_map(
        shards,
        mesh=mesh,
        in_specs=(
            tokens, split, matrix, matrix, matrix, matrix, matrix, matrix, split, split, split, split,
            split, matrix, split, matrix, matrix, matrix, P("rows", None), tokens,
        ),
        out_specs=(
            tokens, tokens, split, matrix, matrix, matrix, matrix, matrix, matrix, split, split, split,
            split, split, matrix, split, matrix, matrix, matrix,
        ),
        check_vma=False,
    )
```

```python
import functools
import jax
import jax.numpy as jnp
from jax import lax
from jax.experimental import pallas as pl
from jax.experimental.pallas import tpu as pltpu
from jax.sharding import PartitionSpec as P

MINI = 16
EPSILON = 1e-06
BASE_RATE = 1.0
GELU_SCALE = (2.0 / 3.141592653589793) ** 0.5
GELU_CUBE = 0.044715
F32 = jnp.float32
BF16 = jnp.bfloat16
NN = (((1,), (0,)), ((), ()))
NT = (((1,), (1,)), ((), ()))
TN = (((0,), (0,)), ((), ()))


def mm(left, right, dims):
    return lax.dot_general(left, right, dims, preferred_element_type=F32)


def in_two(values):
    high = values.astype(BF16)
    return high, (values - high.astype(F32)).astype(BF16)


def mm_two(left, right, dims):
    return mm(left[0], right[0], dims) + (mm(left[1], right[0], dims) + mm(left[0], right[1], dims))


def packed(block, heads, head_dim, parts):
    turned = block.T
    width = block.shape[0] // parts
    return [
        jnp.concatenate(
            [
                turned[h * head_dim : (h + 1) * head_dim, j * width : (j + 1) * width]
                for h in range(heads)
            ],
            axis=1,
        )
        for j in range(parts)
    ]


def unpacked(pieces, heads):
    width = pieces[0].shape[1] // heads
    turned = jnp.concatenate(
        [
            jnp.concatenate([piece[:, h * width : (h + 1) * width] for piece in pieces], axis=1)
            for h in range(heads)
        ],
        axis=0,
    )
    return turned.T


def mean0(values):
    return jnp.mean(values, axis=0, keepdims=True)


def masks(chains, head_dim, dtype):
    lanes = chains * MINI
    rows = lax.broadcasted_iota(jnp.int32, (chains * head_dim, lanes), 0) // head_dim
    cols = lax.broadcasted_iota(jnp.int32, (chains * head_dim, lanes), 1) // MINI
    spread = rows == cols
    source = lax.broadcasted_iota(jnp.int32, (lanes, lanes), 0)
    target = lax.broadcasted_iota(jnp.int32, (lanes, lanes), 1)
    together = (source // MINI) == (target // MINI)
    earlier = jnp.logical_and(together, source <= target)
    scale = jnp.where(earlier, 1.0 / ((target % MINI) + 1).astype(F32), 0.0)
    return spread, together, scale


def spread_out(values, spread, chains):
    return jnp.where(spread, jnp.concatenate([values] * chains, axis=0), jnp.zeros((), values.dtype))


def forward_kernel(
    heads, head_dim, parts,
    slot_ref, inputs_ref, rate_ref, again_ref, again_wide_ref,
    start_ref, start_bias_ref, gain_ref, shift_ref,
    out_ref, sums_ref, kept_ref, spreads_ref, mix_ref, weight_ref,
    state, bias,
):
    chains = rate_ref.shape[-1] // MINI
    spread, together, scale = masks(chains, head_dim, BF16)
    ones = jnp.where(together, 1.0 / MINI, 0.0).astype(BF16)
    gain, shift = gain_ref[...], shift_ref[...]

    @pl.when(pl.program_id(0) == 0)
    def _():
        state[...] = jnp.zeros_like(state)
        bias[...] = jnp.zeros_like(bias)

    width = heads * head_dim
    all_queries, all_keys, all_values = (
        packed(inputs_ref[:, n * width : (n + 1) * width], heads, head_dim, parts) for n in range(3)
    )
    weight = state[...]
    offset = bias[...]
    results = []
    for j in range(parts):
        query, key, value = all_queries[j], all_keys[j], all_values[j]
        rate = rate_ref[0, j : j + 1, :]
        two_keys, two_queries = in_two(key), in_two(query)
        wide_keys = [spread_out(k, spread, chains) for k in two_keys]
        wide_both = [
            jnp.concatenate([k, spread_out(q, spread, chains)], axis=1)
            for k, q in zip(wide_keys, two_queries)
        ]
        mix = in_two((mm_two(two_keys, two_queries, TN) + 1.0) * scale)
        weight = jnp.where(again_wide_ref[0, j : j + 1, :] > 0.0, start_ref[...], weight)
        offset = jnp.where(again_ref[0, j : j + 1, :] > 0.0, start_bias_ref[...], offset)
        two_weights = in_two(weight)
        both = mm_two(two_weights, wide_both, NN)
        lanes = offset.shape[1]
        first = both[:, :lanes] + offset
        center = first - mean0(first)
        inverse = lax.rsqrt(mean0(center * center) + EPSILON)
        normed = center * inverse
        residue = (normed * gain + shift - (value - key)) * gain
        inner = (residue - mean0(residue) - normed * mean0(residue * normed)) * inverse
        rated = in_two(inner * rate)
        combined = both[:, lanes:] + offset - mm_two(rated, mix, NN)
        centered = combined - mean0(combined)
        inverse_out = lax.rsqrt(mean0(centered * centered) + EPSILON)
        rebuilt = centered * inverse_out
        results.append(query + rebuilt * gain + shift)
        weight = weight - mm_two(rated, wide_keys, NT) * (1.0 / MINI)
        offset = offset - (mm(rated[0], ones, NN) + mm(rated[1], ones, NN))
        kept_ref[0, 0, j] = normed
        kept_ref[0, 1, j] = inner
        kept_ref[0, 2, j] = rebuilt
        spreads_ref[0, j : j + 1, :] = inverse
        spreads_ref[0, parts + j : parts + j + 1, :] = inverse_out
        mix_ref[0, j] = mix[0]
        weight_ref[0, j] = two_weights[0]
    out = unpacked(results, heads)
    out_ref[...] = out
    sums_ref[:, 0:1] = jnp.sum(out, axis=1, keepdims=True)
    sums_ref[:, 1:2] = jnp.sum(out * out, axis=1, keepdims=True)
    state[...] = weight
    bias[...] = offset


def gathered_back(wide, lane_chain, head_dim, chains):
    total = wide[:head_dim]
    for c in range(1, chains):
        total = jnp.where(lane_chain == c, wide[c * head_dim : (c + 1) * head_dim], total)
    return total


def backward_kernel(
    heads, head_dim, parts,
    slot_ref, inputs_ref, pre_ref, post_ref, out_ref, token_ref,
    rate_ref, again_ref, again_wide_ref, gain_ref, shift_ref,
    kept_ref, spreads_ref, mix_ref, weight_ref,
    all_ref, logits_ref, dstart_ref, dstart_bias_ref, dgain_ref, dshift_ref,
    state, bias,
):
    chains = rate_ref.shape[-1] // MINI
    lanes = chains * MINI
    spread, together, scale = masks(chains, head_dim, BF16)
    ones = jnp.where(together, 1.0, 0.0).astype(BF16)
    lane_chain = lax.broadcasted_iota(jnp.int32, (head_dim, lanes), 1) // MINI
    gain, shift = gain_ref[...], shift_ref[...]

    @pl.when(pl.program_id(0) == 0)
    def _():
        state[...] = jnp.zeros_like(state)
        bias[...] = jnp.zeros_like(bias)
        dstart_ref[...] = jnp.zeros_like(dstart_ref)
        dstart_bias_ref[...] = jnp.zeros_like(dstart_bias_ref)
        dgain_ref[...] = jnp.zeros_like(dgain_ref)
        dshift_ref[...] = jnp.zeros_like(dshift_ref)

    width = heads * head_dim
    all_queries, all_keys, all_values = (
        packed(inputs_ref[:, n * width : (n + 1) * width], heads, head_dim, parts) for n in range(3)
    )
    center, inverse_all = token_ref[:, 0:1], token_ref[:, 1:2]
    along_post = (out_ref[...] - center) * inverse_all
    delta_post = (post_ref[...] - token_ref[:, 2:3] - along_post * token_ref[:, 3:4]) * inverse_all
    all_deltas = packed(delta_post, heads, head_dim, parts)
    dweight = state[...]
    doffset = bias[...]
    dstart, dstart_bias = dstart_ref[...], dstart_bias_ref[...]
    dgain, dshift = dgain_ref[...], dshift_ref[...]
    dqueries, dkeys, dvalues, dlogits = ([None] * parts for _ in range(4))
    for j in reversed(range(parts)):
        query, key, value, delta = all_queries[j], all_keys[j], all_values[j], all_deltas[j]
        rate = rate_ref[0, j : j + 1, :]
        normed, inner, rebuilt = (kept_ref[0, n, j] for n in range(3))
        inverse, inverse_out = (spreads_ref[0, n * parts + j : n * parts + j + 1, :] for n in range(2))
        mix, weight = mix_ref[0, j], weight_ref[0, j]
        low_key, low_query = key.astype(BF16), query.astype(BF16)
        wide_key = spread_out(low_key, spread, chains)
        wide_query = spread_out(low_query, spread, chains)
        rated = (inner * rate).astype(BF16)
        dnorm = delta * gain
        dcombined = (dnorm - mean0(dnorm) - rebuilt * mean0(dnorm * rebuilt)) * inverse_out
        low_dcombined = dcombined.astype(BF16)
        drated = -mm(low_dcombined, mix, NT)
        dscore = (-mm(rated, low_dcombined, TN) * scale).astype(BF16)
        low_dweight = dweight.astype(BF16)
        drated = drated - (mm(low_dweight, wide_key, NN) + doffset) * (1.0 / MINI)
        dinner = drated * rate
        bent = rate * (1.0 - rate * (head_dim / BASE_RATE))
        dlogits[j] = jnp.sum(drated * inner, axis=0, keepdims=True) * bent
        scaled = dinner * inverse
        offset_residue = normed * gain + shift - (value - key)
        residue = offset_residue * gain
        along = mean0(scaled * normed)
        dresidue = scaled - mean0(scaled) - normed * along
        gained = dresidue * gain
        dnormed = gained * gain - scaled * mean0(residue * normed) - residue * along
        dfirst = (
            dnormed - mean0(dnormed) - normed * (mean0(dnormed * normed) + mean0(dinner * inner))
        ) * inverse
        low_dfirst = dfirst.astype(BF16)
        dvalues[j] = -gained
        back_key = gathered_back(mm(weight, low_dfirst, TN), lane_chain, head_dim, chains)
        back_query = gathered_back(mm(weight, low_dcombined, TN), lane_chain, head_dim, chains)
        back_state = gathered_back(mm(low_dweight, rated, TN), lane_chain, head_dim, chains)
        dkeys[j] = gained + back_key - back_state * (1.0 / MINI) + mm(low_query, dscore, NT)
        dqueries[j] = delta + back_query + mm(low_key, dscore, NN)
        dgain = dgain + delta * rebuilt + dresidue * offset_residue + gained * normed
        dshift = dshift + delta + gained
        dweight = dweight + mm(low_dfirst, wide_key, NT) + mm(low_dcombined, wide_query, NT)
        both = (dfirst + dcombined).astype(BF16)
        doffset = doffset + mm(both, ones, NN)
        again_wide = again_wide_ref[0, j : j + 1, :] > 0.0
        again = again_ref[0, j : j + 1, :] > 0.0
        dstart = dstart + jnp.where(again_wide, dweight, 0.0)
        dstart_bias = dstart_bias + jnp.where(again, doffset, 0.0)
        dweight = jnp.where(again_wide, 0.0, dweight)
        doffset = jnp.where(again, 0.0, doffset)
    for n, pieces in enumerate((dqueries, dkeys, dvalues)):
        natural = unpacked(pieces, heads).astype(all_ref.dtype)
        all_ref[:, n * width : (n + 1) * width] = natural
    all_ref[:, 3 * width : 4 * width] = pre_ref[...]
    natural = unpacked(dlogits, heads)
    spare = logits_ref.shape[1] - heads
    if spare:
        natural = jnp.concatenate([natural, jnp.zeros((natural.shape[0], spare), F32)], axis=1)
    logits_ref[...] = natural.astype(logits_ref.dtype)
    state[...] = dweight
    bias[...] = doffset
    dstart_ref[...] = dstart
    dstart_bias_ref[...] = dstart_bias
    dgain_ref[...] = dgain
    dshift_ref[...] = dshift


def whole(shape):
    return pl.BlockSpec(shape, lambda *_: (0,) * len(shape))


def place(step, own, count):
    apart = jnp.bitwise_xor(step, own)
    return jnp.bitwise_and(apart, 1) * (count // 2) + lax.shift_right_logical(apart, 1)


def inner_forward(slot, projected, rates, again, again_wide, start, start_bias, gain, shift, heads, head_dim, parts):
    steps, _, lanes = rates.shape
    tokens = projected.shape[0] // steps
    wide = start.shape[1]
    at_slot = pl.BlockSpec((tokens, heads * head_dim), lambda i, s: (place(i, s[0], steps), 0))

    def stepped(*shape):
        return pl.BlockSpec((1,) + shape, lambda i, s: (i,) + (0,) * len(shape))

    saved = [
        ((3, parts, head_dim, lanes), F32), ((2 * parts, lanes), F32),
        ((parts, lanes, lanes), BF16), ((parts, head_dim, wide), BF16),
    ]
    return pl.pallas_call(
        functools.partial(forward_kernel, heads, head_dim, parts),
        out_shape=[jax.ShapeDtypeStruct((steps * tokens, heads * head_dim), F32), jax.ShapeDtypeStruct((steps * tokens, 2), F32)]
        + [jax.ShapeDtypeStruct((steps,) + shape, kind) for shape, kind in saved],
        grid_spec=pltpu.PrefetchScalarGridSpec(
            num_scalar_prefetch=1,
            grid=(steps,),
            in_specs=[pl.BlockSpec((tokens, 3 * heads * head_dim), at_slot.index_map)]
            + [stepped(parts, lanes), stepped(parts, lanes), stepped(parts, wide)]
            + [whole(start.shape), whole(start_bias.shape), whole(gain.shape), whole(shift.shape)],
            out_specs=[at_slot, pl.BlockSpec((tokens, 2), at_slot.index_map)]
            + [stepped(*shape) for shape, _ in saved],
            scratch_shapes=[pltpu.VMEM(start.shape, F32), pltpu.VMEM(start_bias.shape, F32)],
        ),
        compiler_params=pltpu.CompilerParams(
            dimension_semantics=("arbitrary",), vmem_limit_bytes=63 * 1024 * 1024
        ),
        name="inner_forward",
    )(slot, projected, rates, again, again_wide, start, start_bias, gain, shift)


def inner_backward(slot, projected, pre, deltas, outs, per_token, rates, again, again_wide, gain, shift, saved, heads, head_dim, parts):
    steps, _, lanes = rates.shape
    tokens = projected.shape[0] // steps
    wide = again_wide.shape[-1]
    inputs, logits = 4 * heads * head_dim, heads + -heads % 16
    at_slot = pl.BlockSpec(
        (tokens, heads * head_dim), lambda i, s: (place(steps - 1 - i, s[0], steps), 0)
    )

    def stepped(*shape):
        return pl.BlockSpec((1,) + shape, lambda i, s: (steps - 1 - i,) + (0,) * len(shape))

    return pl.pallas_call(
        functools.partial(backward_kernel, heads, head_dim, parts),
        out_shape=[
            jax.ShapeDtypeStruct((steps * tokens, inputs), BF16),
            jax.ShapeDtypeStruct((steps * tokens, logits), BF16),
            jax.ShapeDtypeStruct((head_dim, wide), F32),
            jax.ShapeDtypeStruct((head_dim, lanes), F32),
            jax.ShapeDtypeStruct((head_dim, lanes), F32),
            jax.ShapeDtypeStruct((head_dim, lanes), F32),
        ],
        grid_spec=pltpu.PrefetchScalarGridSpec(
            num_scalar_prefetch=1,
            grid=(steps,),
            in_specs=[pl.BlockSpec((tokens, 3 * heads * head_dim), at_slot.index_map)]
            + [at_slot] * 3
            + [pl.BlockSpec((tokens, per_token.shape[1]), at_slot.index_map)]
            + [stepped(parts, lanes), stepped(parts, lanes), stepped(parts, wide)]
            + [whole(gain.shape), whole(shift.shape)]
            + [stepped(*array.shape[1:]) for array in saved],
            out_specs=[
                pl.BlockSpec((tokens, inputs), at_slot.index_map),
                pl.BlockSpec((tokens, logits), at_slot.index_map),
                whole((head_dim, wide)),
            ]
            + [whole((head_dim, lanes))] * 3,
            scratch_shapes=[pltpu.VMEM((head_dim, wide), F32), pltpu.VMEM((head_dim, lanes), F32)],
        ),
        compiler_params=pltpu.CompilerParams(
            dimension_semantics=("arbitrary",), vmem_limit_bytes=63 * 1024 * 1024
        ),
        name="inner_backward",
    )(slot, projected, pre, deltas, outs, per_token, rates, again, again_wide, gain, shift, *saved)


def cut_kernel(seq_count, kinds, *refs):
    out_ref = refs[-1]
    for s in range(seq_count):
        pieces = []
        for ref, (groups, span, gap, rest) in zip(refs, kinds):
            rows = ref.shape[0]
            for g in range(groups):
                at = (g * seq_count + s) * span
                pieces.append(ref[:, at : at + span].astype(F32))
                if gap:
                    pieces.append(jnp.zeros((rows, gap), F32))
            if rest:
                pieces.append(jnp.zeros((rows, rest), F32))
        out_ref[s] = jnp.concatenate(pieces, axis=1).astype(out_ref.dtype)


def cut_columns(weights, kinds, seq_count):
    rows = weights[0].shape[0]
    columns = sum(groups * (span + gap) + rest for groups, span, gap, rest in kinds)
    return pl.pallas_call(
        functools.partial(cut_kernel, seq_count, kinds),
        out_shape=jax.ShapeDtypeStruct((seq_count, rows, columns), BF16),
        compiler_params=pltpu.CompilerParams(vmem_limit_bytes=40 * 1024 * 1024),
        name="cut_columns",
    )(*weights)


def join_kernel(seq_count, kinds, *refs):
    count = len(kinds)
    parts_ref, weights, grads, sums_ref = refs[0], refs[1 : 1 + count], refs[1 + count : -1], refs[-1]
    total = 0.0
    base = 0
    for weight, ref, (groups, span, gap, rest) in zip(weights, grads, kinds):
        pieces = []
        for g in range(groups):
            at = base + g * (span + gap)
            pieces += [parts_ref[s, :, at : at + span].astype(F32) for s in range(seq_count)]
        whole_row = jnp.concatenate(pieces, axis=1)
        ref[...] = whole_row
        total = total + jnp.sum(whole_row * weight[...].astype(F32), axis=1, keepdims=True)
        base += groups * (span + gap) + rest
    sums_ref[...] = total


def join_columns(parts, weights, kinds):
    return pl.pallas_call(
        functools.partial(join_kernel, parts.shape[0], kinds),
        out_shape=[jax.ShapeDtypeStruct(w.shape, F32) for w in weights]
        + [jax.ShapeDtypeStruct((parts.shape[1], 1), F32)],
        compiler_params=pltpu.CompilerParams(vmem_limit_bytes=40 * 1024 * 1024),
        name="join_columns",
    )(parts, *weights)


def branch_kernel(
    delta_ref, matrix_ref, pre_ref, out_ref, token_ref, scale_ref, offset_ref,
    dpre_ref, dnorm_ref, sums_ref, dscale_ref, doffset_ref,
):
    @pl.when(pl.program_id(0) == 0)
    def _():
        dscale_ref[...] = jnp.zeros_like(dscale_ref)
        doffset_ref[...] = jnp.zeros_like(doffset_ref)

    delta_gated = mm(delta_ref[...], matrix_ref[...], NT)
    scale = scale_ref[...]
    norm = (out_ref[...] - token_ref[:, 0:1]) * token_ref[:, 1:2]
    pre = pre_ref[...]
    square = pre * pre
    bend = jnp.tanh(GELU_SCALE * pre * (1.0 + GELU_CUBE * square))
    half = 0.5 * (1.0 + bend)
    slope = half + 0.5 * pre * (1.0 - bend * bend) * (GELU_SCALE * (1.0 + 3.0 * GELU_CUBE * square))
    dpre_ref[...] = (delta_gated * (norm * scale + offset_ref[...]) * slope).astype(dpre_ref.dtype)
    delta_post = delta_gated * (pre * half)
    dscale_ref[...] += jnp.sum(delta_post * norm, axis=0, keepdims=True)
    doffset_ref[...] += jnp.sum(delta_post, axis=0, keepdims=True)
    dnorm = delta_post * scale
    dnorm_ref[...] = dnorm
    sums_ref[:, 0:1] = jnp.sum(dnorm, axis=1, keepdims=True)
    sums_ref[:, 1:2] = jnp.sum(dnorm * norm, axis=1, keepdims=True)


def branch_backward(delta, matrix, projected, out, per_token, scale, offset, block):
    tokens, width = out.shape
    gate = pl.BlockSpec((block, width), lambda i: (i, 3))

    def by_block(array):
        return pl.BlockSpec((block, array.shape[1]), lambda i: (i, 0))

    row = jax.ShapeDtypeStruct((1, width), F32)
    sums = jax.ShapeDtypeStruct((tokens, 2), F32)
    return pl.pallas_call(
        branch_kernel,
        grid=(tokens // block,),
        in_specs=[by_block(delta), whole(matrix.shape), gate, by_block(out), by_block(per_token)]
        + [whole((1, width))] * 2,
        out_shape=[jax.ShapeDtypeStruct(out.shape, BF16), jax.ShapeDtypeStruct(out.shape, F32), sums, row, row],
        out_specs=[by_block(out), by_block(out), by_block(sums), whole((1, width)), whole((1, width))],
        compiler_params=pltpu.CompilerParams(
            dimension_semantics=("arbitrary",), vmem_limit_bytes=63 * 1024 * 1024
        ),
        name="branch_backward",
    )(delta, matrix, projected, out, per_token, scale, offset)


def spread_kernel(delta_ref, logits_ref, weight_ref, rate_ref, out_ref):
    total = mm(delta_ref[...], weight_ref[...], NT) + mm(logits_ref[...], rate_ref[...], NT)
    out_ref[...] = total.astype(out_ref.dtype)


def spread_back(delta, logits, first, tokens, weight, rate, kind, block):
    model = weight.shape[0]
    return pl.pallas_call(
        spread_kernel,
        grid=(model // block,),
        in_specs=[
            pl.BlockSpec((tokens, delta.shape[1]), lambda i: (first // tokens, 0)),
            pl.BlockSpec((tokens, logits.shape[1]), lambda i: (first // tokens, 0)),
            pl.BlockSpec((block, weight.shape[1]), lambda i: (i, 0)),
            pl.BlockSpec((block, rate.shape[1]), lambda i: (i, 0)),
        ],
        out_specs=pl.BlockSpec((tokens, block), lambda i: (0, i)),
        out_shape=jax.ShapeDtypeStruct((tokens, model), kind),
        compiler_params=pltpu.CompilerParams(
            dimension_semantics=("arbitrary",), vmem_limit_bytes=40 * 1024 * 1024
        ),
        name="spread_back",
    )(delta, logits, weight, rate)


def exchange(value, axis, bit):
    count = lax.axis_size(axis)
    return lax.ppermute(value, axis, [(i, i ^ bit) for i in range(count)])


def bits_of(axis):
    return [(axis, 1 << p) for p in range(lax.axis_size(axis).bit_length() - 1)]


def cuts_of(width, ways):
    unit = 128 if width >= 128 * ways else 1
    return [unit * (n * (width // unit) // ways) for n in range(ways)] + [width]


def gather_blocks(block, bits, tied=None):
    near, far = bits[0], bits[1:]
    ways = max(1, len(far))
    cuts = cuts_of(block.shape[-1], ways)
    held = [{0: block[:, cuts[way] : cuts[way + 1]]} for way in range(ways)]
    for step in range(len(far)):
        for way in range(ways):
            bit = (way + step) % len(far)
            keys = sorted(held[way])
            moved = exchange(jnp.stack([held[way][k] for k in keys]), *far[bit])
            for n, k in enumerate(keys):
                held[way][k | 1 << bit] = moved[n]
    half = jnp.concatenate([jnp.stack([h[k] for k in sorted(h)]) for h in held], axis=-1)
    if tied is not None:
        half, tied = lax.optimization_barrier((half, tied))
    whole = jnp.concatenate([half, exchange(half, *near)], axis=0)
    return whole if tied is None else (whole, tied)


def reduce_blocks(own, away, bits, near_kind=BF16, last_kind=BF16):
    near, far = bits[0], bits[1:]
    ways = max(1, len(far))
    cuts = cuts_of(own.shape[-1], ways)
    half = own.astype(F32) + exchange(away.astype(near_kind), *near).astype(F32)
    held = [
        {k: half[k, :, cuts[way] : cuts[way + 1]] for k in range(half.shape[0])} for way in range(ways)
    ]
    for step in range(len(far)):
        for way in range(ways):
            bit = (way + step) % len(far)
            gone = sorted(k for k in held[way] if k >> bit & 1)
            kind = last_kind if step == len(far) - 1 else BF16
            moved = exchange(jnp.stack([held[way][k].astype(kind) for k in gone]), *far[bit])
            for n, k in enumerate(gone):
                held[way][k ^ 1 << bit] = held[way][k ^ 1 << bit] + moved[n].astype(F32)
                del held[way][k]
    return jnp.concatenate([h[0] for h in held], axis=-1)


def has_bit(axis, bit):
    return jnp.bitwise_and(lax.axis_index(axis), bit) > 0


def gather_natural(value, bits):
    for axis, bit in bits:
        other = exchange(value, axis, bit)
        high = has_bit(axis, bit)
        value = jnp.concatenate([jnp.where(high, other, value), jnp.where(high, value, other)], axis=0)
    return value


def halved(value, dim, axis, bit):
    half = value.shape[dim] // 2
    high = has_bit(axis, bit)
    low_half = lax.slice_in_dim(value, 0, half, axis=dim)
    high_half = lax.slice_in_dim(value, half, 2 * half, axis=dim)
    other = exchange(jnp.where(high, low_half, high_half), axis, bit)
    return jnp.where(high, high_half, low_half) + other


def gelu_tanh(values):
    return jax.nn.gelu(values, approximate=True)


def shards(
    hidden_in,
    attn_gain,
    query_weight,
    key_weight,
    value_weight,
    rate_weight,
    gate_weight,
    init_weight,
    init_bias,
    inner_gain,
    inner_shift,
    post_gain,
    post_shift,
    out_weight,
    ffn_gain,
    ffn_gate_weight,
    ffn_up_weight,
    ffn_down_weight,
    doc_starts,
    out_grad,
):
    rows_here, stretch, model = hidden_in.shape
    head_count = rate_weight.shape[1]
    head_dim = init_weight.shape[1]
    parts = stretch // MINI
    local = rows_here * stretch
    seq_count = lax.axis_size("seq")
    rows_count = lax.axis_size("rows")
    share = model // (seq_count * rows_count)
    unit_share = ffn_down_weight.shape[0]
    heads = head_count // seq_count
    width = heads * head_dim
    aligned = share % head_dim == 0
    groups, span = (rows_count, share) if aligned else (1, width)
    me = lax.axis_index("seq")
    everywhere = ("rows", "seq")
    seq_bits = bits_of("seq")
    row_bits = bits_of("rows")
    spare = -unit_share % 16
    head_kind = (groups, span, 0, 0)
    rate_kind = (groups, heads // groups, 0, -heads % 16)
    unit_kind = (rows_count, unit_share, spare, 0)
    units = rows_count * (unit_share + spare)

    def shuffled(values):
        return lax.all_to_all(values, "seq", 0, 0, tiled=True).reshape(-1, values.shape[-1])

    def row_sums(values):
        summed = lax.psum_scatter(values, "rows", scatter_dimension=0, tiled=True)
        return summed.reshape(seq_count, share, -1)

    def columns_out(values):
        return lax.all_to_all(values, "seq", 0, 0, tiled=True)

    def own_part(values):
        split = values.reshape(groups, seq_count, span, -1)
        return lax.dynamic_index_in_dim(split, me, 1, keepdims=False).reshape(width, -1)

    def placed(values):
        split = values.reshape(groups, 1, span, -1)
        here = (jnp.arange(seq_count) == me).reshape(1, -1, 1, 1)
        return jnp.where(here, split, 0.0).reshape(model, -1)

    def reordered(values):
        return values.reshape(rows_here, parts, MINI, -1).transpose(1, 0, 2, 3).reshape(-1, model)

    def restored(values):
        return values.reshape(parts, rows_here, MINI, -1).transpose(1, 0, 2, 3).reshape(rows_here, stretch, -1)

    real = jnp.min(doc_starts) >= 0

    def apart(part, *operands):
        shapes = jax.eval_shape(part, *operands)
        blank = lambda *_: jax.tree.map(lambda s: jnp.zeros(s.shape, s.dtype), shapes)
        return lax.cond(real, part, blank, *operands)

    vectors = jnp.stack(
        [attn_gain, ffn_gain, init_bias, inner_gain, inner_shift, post_gain, post_shift], axis=1
    )
    small = jnp.concatenate([init_weight, rate_weight, vectors], axis=1)
    small = jnp.pad(small, ((0, 0), (0, -small.shape[1] % 128)))
    hidden, cotangent = reordered(hidden_in), reordered(out_grad)
    if aligned:
        out_own = lax.all_gather(out_weight, "rows", axis=0, tiled=True)
    else:
        out_own = own_part(lax.all_gather(out_weight, everywhere, axis=0, tiled=True))
    mixer_cut = shuffled(
        cut_columns((query_weight, key_weight, value_weight, gate_weight), (head_kind,) * 4, seq_count)
    )
    mixer_cut, hidden, cotangent, small, ffn_gate_weight, ffn_up_weight = lax.optimization_barrier(
        (mixer_cut, hidden, cotangent, small, ffn_gate_weight, ffn_up_weight)
    )
    late_cut, out_own = lax.optimization_barrier((mixer_cut, out_own))
    mixer_weight = lax.all_gather(late_cut, "rows", axis=0, tiled=True)
    ffn_cut = cut_columns((ffn_gate_weight, ffn_up_weight), (unit_kind,) * 2, seq_count)

    def gather_inputs(hidden, cotangent, small, ffn_cut):
        hidden_all = gather_blocks(hidden, seq_bits).reshape(-1, model)
        cot_all = gather_blocks(cotangent, seq_bits).reshape(-1, model)
        small = gather_natural(small, row_bits).reshape(rows_count, share, -1)
        small = small.transpose(1, 0, 2).reshape(share, -1)
        small = gather_natural(small, seq_bits).reshape(seq_count, share, rows_count, -1)
        small = small.transpose(2, 0, 1, 3).reshape(model, -1)
        return hidden_all, cot_all, small, shuffled(ffn_cut)

    hidden_all, cot_all, small, ffn_cut = apart(gather_inputs, hidden, cotangent, small, ffn_cut)
    ffn_wide = lax.all_gather(ffn_cut, "rows", axis=0, tiled=True)

    gain_attn = small[:, head_dim + head_count].astype(F32)
    gain_ffn = small[:, head_dim + head_count + 1].astype(F32)
    own_small = own_part(small)
    own_vectors = own_small[:, head_dim + head_count :].astype(F32)
    rate_all = small[:, head_dim : head_dim + head_count].reshape(model, groups, seq_count, -1)
    rate_own = lax.dynamic_index_in_dim(rate_all, me, 2, keepdims=False).reshape(model, heads)
    lanes = heads * rows_here * MINI

    def by_lane(values, repeat):
        turned = values.reshape(heads, head_dim).T
        return jnp.broadcast_to(turned[:, :, None], (head_dim, heads, repeat)).reshape(head_dim, -1)

    bias_lanes = by_lane(own_vectors[:, 2], rows_here * MINI)
    gain_lanes = by_lane(own_vectors[:, 3], rows_here * MINI)
    shift_lanes = by_lane(own_vectors[:, 4], rows_here * MINI)
    post_scale, post_offset = own_vectors[:, 5], own_vectors[:, 6]
    start = own_small[:, :head_dim].astype(F32).reshape(heads, head_dim, head_dim).transpose(2, 0, 1)
    start = jnp.broadcast_to(start[:, :, None], (head_dim, heads, rows_here, head_dim)).reshape(head_dim, -1)

    steps = seq_count
    position = jnp.arange(steps * parts, dtype=jnp.int32) * MINI
    restarts = jnp.logical_or(
        position[:, None] == 0, jnp.any(doc_starts[None] == position[:, None, None], axis=2)
    ).astype(F32)

    def by_chain(repeat):
        wide = jnp.broadcast_to(
            restarts[:, None, :, None], (steps * parts, heads, rows_here, repeat)
        )
        return wide.reshape(steps, parts, -1)

    again, again_wide = by_chain(MINI), by_chain(head_dim)

    order = jnp.arange(steps, dtype=jnp.int32)
    slots = place(order, me, steps)
    blocks = jnp.bitwise_xor(order % (steps // 2) * 2 + order // (steps // 2), me)

    tokens_all = hidden_all.astype(F32)
    inverse_all = lax.rsqrt(jnp.mean(tokens_all * tokens_all, axis=-1, keepdims=True) + EPSILON)
    plain_all = tokens_all * inverse_all
    normed = (plain_all * gain_attn).astype(BF16)


    projected = jnp.dot(normed, mixer_weight, preferred_element_type=F32)
    projected, ffn_down_weight = lax.optimization_barrier((projected, ffn_down_weight))
    down_wide = lax.all_gather(
        jnp.pad(ffn_down_weight, ((0, spare), (0, 0))), "rows", axis=0, tiled=True
    )
    gate_pre = projected[:, 3 * width :]
    logits = jnp.dot(normed, rate_own, preferred_element_type=F32)

    def to_lanes(per_token):
        ordered = jnp.take(per_token.reshape(steps, -1, heads), slots, axis=0)
        ordered = ordered.reshape(steps, parts, rows_here * MINI, heads)
        return ordered.transpose(0, 1, 3, 2).reshape(steps, parts, lanes)

    rates = to_lanes(jax.nn.sigmoid(logits) * (BASE_RATE / head_dim))
    slot = me.astype(jnp.int32).reshape(1)

    inner_out, inner_sums, *saved = inner_forward(
        slot, projected, rates, again, again_wide, start, bias_lanes, gain_lanes,
        shift_lanes, heads, head_dim, parts,
    )

    def feature_mean(sums):
        count = sums.shape[1]
        ordered = jnp.take(sums.T.reshape(count, steps, -1), slots, axis=1)
        total = lax.psum(ordered, "seq") / model
        return jnp.take(total, blocks, axis=1).reshape(count, -1, 1)

    moments = feature_mean(inner_sums)
    post_mean = moments[0]
    post_inverse = lax.rsqrt(moments[1] - post_mean * post_mean + EPSILON)
    post_norm = (inner_out - post_mean) * post_inverse
    post_out = post_norm * post_scale + post_offset
    gated = (gelu_tanh(gate_pre) * post_out).astype(BF16)

    def halves(left, matrix, dims, kind=BF16):
        half = left.shape[0] // 2
        away = lax.dot_general(left[half:], matrix, dims, preferred_element_type=F32).astype(kind)
        own = lax.dot_general(left[:half], matrix, dims, preferred_element_type=F32)
        return own.reshape(-1, local, model), away.reshape(-1, local, model)

    def rms_inverse(values):
        return lax.rsqrt(jnp.mean(values * values, axis=-1, keepdims=True) + EPSILON)

    def into_ffn(own, away, hidden, gain_ffn):
        residual = hidden.astype(F32) + reduce_blocks(own, away, seq_bits, F32, F32)
        scaled = (residual * rms_inverse(residual) * gain_ffn).astype(BF16)
        return residual, gather_blocks(scaled, seq_bits).reshape(-1, model)

    residual, ffn_in = apart(into_ffn, *halves(gated, out_own, NN, F32), hidden, gain_ffn)
    gate_up = jnp.dot(ffn_in, ffn_wide, preferred_element_type=F32)
    gate_value, up_value = gate_up[:, :units], gate_up[:, units:]
    sigmoid_gate = jax.nn.sigmoid(gate_value)
    active = (gate_value * sigmoid_gate * up_value).astype(BF16)

    def token_grad(left, right):
        return lax.dot_general(left, right, TN, preferred_element_type=F32)

    grad_down = token_grad(active, cot_all).astype(BF16)
    grad_down, down_wide = lax.optimization_barrier((grad_down, down_wide))
    grad_down = lax.psum_scatter(grad_down, "rows", scatter_dimension=0, tiled=True)
    delta_active = lax.dot_general(cot_all, down_wide, NT, preferred_element_type=F32)
    delta_up = (delta_active * gate_value * sigmoid_gate).astype(BF16)
    delta_gate = (
        delta_active * up_value * sigmoid_gate * (1.0 + gate_value * (1.0 - sigmoid_gate))
    ).astype(BF16)
    delta_both = jnp.concatenate([delta_gate, delta_up], axis=1)

    def out_of_ffn(own, away, residual, gain_ffn, cotangent):
        delta_ffn = reduce_blocks(own, away, seq_bits)
        inverse_two = rms_inverse(residual)
        scaled_two = delta_ffn * gain_ffn
        delta_after = (
            cotangent.astype(F32)
            + inverse_two * scaled_two
            - residual * inverse_two**3 * jnp.mean(scaled_two * residual, axis=-1, keepdims=True)
        )
        delta_branch = gather_blocks(delta_after.astype(BF16), seq_bits).reshape(-1, model)
        return delta_after, delta_branch

    grad_ffn = token_grad(ffn_in, delta_both).astype(BF16)
    delta_both, grad_ffn = lax.optimization_barrier((delta_both, grad_ffn))
    ffn_sums = row_sums(grad_ffn)
    delta_after, delta_branch = apart(
        out_of_ffn, *halves(delta_both, ffn_wide, NT), residual, gain_ffn, cotangent
    )

    delta_pre, delta_norm, norm_sums, grad_post_scale, grad_post_shift = branch_backward(
        delta_branch, out_own, projected, inner_out, jnp.concatenate([post_mean, post_inverse], axis=1),
        post_scale[None], post_offset[None], max(local, steps * local // 2),
    )
    means = feature_mean(norm_sums)
    per_token = jnp.concatenate([post_mean, post_inverse, means[0], means[1]], axis=1)

    (
        delta_all, delta_logits,
        grad_start, grad_bias, grad_inner_gain, grad_inner_shift,
    ) = inner_backward(
        slot, projected, delta_pre, delta_norm, inner_out, per_token, rates, again, again_wide,
        gain_lanes, shift_lanes, saved, heads, head_dim, parts,
    )
    grad_inputs = token_grad(normed, delta_all).astype(BF16)
    delta_all, grad_inputs = lax.optimization_barrier((delta_all, grad_inputs))
    half = delta_all.shape[0] // 2
    rate_wide = jnp.pad(rate_own, ((0, 0), (0, -heads % 16)))
    away = spread_back(delta_all, delta_logits, half, half, mixer_weight, rate_wide, BF16, model // 4)
    own = spread_back(delta_all, delta_logits, 0, half, mixer_weight, rate_wide, F32, model // 4)
    away, own = away.reshape(-1, local, model), own.reshape(-1, local, model)
    input_sums = row_sums(grad_inputs)
    away, own, gated, active, ffn_sums, grad_down = lax.optimization_barrier(
        (away, own, gated, active, ffn_sums, grad_down)
    )
    grad_rate = token_grad(normed, delta_logits[:, :heads])
    grad_out = token_grad(gated, delta_branch).astype(BF16)
    if aligned:
        grad_out = lax.psum_scatter(grad_out, "rows", scatter_dimension=0, tiled=True)

    def out_of_mixer(
        own, away, own_down, away_down, residual, hidden, delta_after, gain_attn, ffn_sums, grad_out, grad_start,
        grad_bias, grad_inner_gain, grad_inner_shift, grad_post_scale, grad_post_shift, grad_rate,
    ):
        def lane_sum(per_lane, repeat):
            return per_lane.reshape(head_dim, heads, repeat).sum(axis=2).T.reshape(width, 1)

        grad_start = grad_start.reshape(head_dim, heads, rows_here, head_dim).sum(axis=2)
        grad_start = grad_start.transpose(1, 2, 0).reshape(width, head_dim)
        grad_bias = grad_bias.reshape(head_dim, heads, rows_here, MINI)[..., 0]
        own_grads = jnp.concatenate(
            [
                grad_start,
                lane_sum(grad_bias, rows_here),
                lane_sum(grad_inner_gain, rows_here * MINI),
                lane_sum(grad_inner_shift, rows_here * MINI),
                grad_post_scale.T,
                grad_post_shift.T,
            ],
            axis=1,
        )
        grad_gate, grad_up, ffn_products = join_columns(
            columns_out(ffn_sums), (ffn_gate_weight, ffn_up_weight), (unit_kind,) * 2
        )
        delta_normed = reduce_blocks(own, away, seq_bits)
        block_out = restored(residual + reduce_blocks(own_down, away_down, seq_bits)).astype(BF16)
        if aligned:
            rates = grad_rate.reshape(rows_count, seq_count, share, heads).transpose(0, 2, 1, 3)
            own_grads = jnp.concatenate([own_grads, rates.reshape(width, -1)], axis=1)
            own_grads = jnp.pad(own_grads, ((0, 0), (0, -own_grads.shape[1] % 128)))
            for axis, bit in reversed(row_bits):
                own_grads = halved(own_grads, 0, axis, bit)
            rates = own_grads[:, head_dim + 5 : head_dim + 5 + seq_count * heads]
            rates = rates.reshape(share, seq_count, heads).transpose(1, 0, 2)
        else:
            rates = lax.psum_scatter(grad_rate, "rows", scatter_dimension=0, tiled=True)
            rates = rates.reshape(seq_count, share, heads)
            own_grads = lax.psum_scatter(
                placed(jnp.concatenate([own_grads.astype(BF16), grad_out], axis=1)),
                everywhere, scatter_dimension=0, tiled=True,
            ).astype(F32)
        tokens = hidden.astype(F32)
        inverse_one = rms_inverse(tokens)
        scaled_one = delta_normed * gain_attn
        hidden_grad = (
            delta_after
            + inverse_one * scaled_one
            - tokens * inverse_one**3 * jnp.mean(scaled_one * tokens, axis=-1, keepdims=True)
        )
        rates = jnp.pad(rates.astype(BF16), ((0, 0), (0, 0), (0, -heads % 16)))
        return block_out, restored(hidden_grad), grad_gate, grad_up, ffn_products, own_grads, rates

    block_out, hidden_grad, grad_gate, grad_up, ffn_products, own_grads, rates = apart(
        out_of_mixer, own, away, *halves(active, down_wide, NN), residual, hidden, delta_after, gain_attn,
        ffn_sums, grad_out, grad_start, grad_bias, grad_inner_gain, grad_inner_shift, grad_post_scale, grad_post_shift, grad_rate,
    )
    grad_query, grad_key, grad_value, grad_gate_weight, grad_rate, input_products = join_columns(
        columns_out(jnp.concatenate([input_sums, rates], axis=2)), (query_weight, key_weight, value_weight, gate_weight, rate_weight),
        (head_kind,) * 4 + (rate_kind,),
    )
    grad_gain_attn = input_products[:, 0] / attn_gain.astype(F32)
    grad_gain_ffn = ffn_products[:, 0] / ffn_gain.astype(F32)
    if not aligned:
        grad_out = own_grads[:, head_dim + 5 :]
    results = (
        block_out,
        hidden_grad,
        grad_gain_attn,
        grad_query,
        grad_key,
        grad_value,
        grad_rate,
        grad_gate_weight,
        own_grads[:, :head_dim],
        *list(own_grads[:, head_dim : head_dim + 5].T),
        grad_out,
        grad_gain_ffn,
        grad_gate,
        grad_up,
        grad_down[:unit_share].astype(F32),
    )
    results = list(lax.optimization_barrier(results))
    results[14] = results[14].astype(F32)
    return tuple(results)


def solution(mesh):
    split = P(("rows", "seq"))
    matrix = P(("rows", "seq"), None)
    tokens = P("rows", "seq", None)
    return jax.shard_map(
        shards,
        mesh=mesh,
        in_specs=(
            tokens, split, matrix, matrix, matrix, matrix, matrix, matrix, split, split, split, split,
            split, matrix, split, matrix, matrix, matrix, P("rows", None), tokens,
        ),
        out_specs=(
            tokens, tokens, split, matrix, matrix, matrix, matrix, matrix, matrix, split, split, split,
            split, split, matrix, split, matrix, matrix, matrix,
        ),
        check_vma=False,
    )
```
